32 devices in a mesh: dp: 16 (over z, y, core), seq: 2 (over x).
Axes of the slice: x: 2, y: 2, z: 4, core: 2. Of those that a mesh axis runs over, the one named last changes fastest.
Arguments:
- tokens: bfloat16 [32, 640, 768], P('dp', 'seq'), may hold values from -6 to 6
- seg_count: int32 [32], P('dp'), may hold values from 5 to 128, as said below
- seg_align: int32 [32, 512], P('dp'), may hold values from 0 to 127, as said below
- cotangent: bfloat16 [32, 640, 768], P('dp', 'seq'), may hold values from -6 to 6
- qkv_weight: bfloat16 [768, 2304], replicated, may hold values from -0.21875 to 0.21875
- query_bias: float32 [768], replicated, may hold values from -3 to 3
- value_bias: float32 [768], replicated, may hold values from -3 to 3
- output_weight: bfloat16 [768, 768], replicated, may hold values from -2 to 2
- output_bias: float32 [768], replicated, may hold values from -3 to 3
- first_gain: float32 [768], replicated, may hold values from 0.1 to 1.9
- first_shift: float32 [768], replicated, may hold values from -3 to 3
- inner_weight: bfloat16 [768, 3072], replicated, may hold values from -0.21875 to 0.21875
- inner_bias: float32 [3072], replicated, may hold values from -3 to 3
- outer_weight: bfloat16 [3072, 768], replicated, may hold values from -0.109375 to 0.109375
- outer_bias: float32 [768], replicated, may hold values from -3 to 3
- second_gain: float32 [768], replicated, may hold values from 0.1 to 1.9
- second_shift: float32 [768], replicated, may hold values from -3 to 3
Outputs:
- block_output: bfloat16 [32, 640, 768], P('dp', 'seq')
- tokens_grad: bfloat16 [32, 640, 768], P('dp', 'seq')
- qkv_weight_grad: float32 [768, 2304], P('dp')
- query_bias_grad: float32 [768], P('dp')
- value_bias_grad: float32 [768], P('dp')
- output_weight_grad: float32 [768, 768], P('dp')
- output_bias_grad: float32 [768], P('dp')
- first_gain_grad: float32 [768], P('dp')
- first_shift_grad: float32 [768], P('dp')
- inner_weight_grad: float32 [768, 3072], P('dp')
- inner_bias_grad: float32 [3072], P('dp')
- outer_weight_grad: float32 [3072, 768], P('dp')
- outer_bias_grad: float32 [768], P('dp')
- second_gain_grad: float32 [768], P('dp')
- second_shift_grad: float32 [768], P('dp')
The draws below stay inside these ranges and needn't reach their ends.
Inputs may be any that keep to these rules, and one draw needn't show every extreme that they name: `seg_count`: heavy tailed; some document has exactly 128 segment tokens. `seg_align`: below the document's seg_count.
All inputs are finite; a program needn't handle non-finite values.
Results may differ from the reference program's by a relative error of at most 0.015.
Values may be sent and summed in bfloat16 or wider, within the bound.
A program may use at most 192 MiB of HBM per device.

```python
import jax
import jax.numpy as jnp
from jax import lax

D = 768
H = 12
FF = 3072
TEXT = 512
SEG_MOST = 128
SLOTS = 640
DOCS = 32


def count_draw(key):
    spread = SEG_MOST - 5
    streams = jax.random.split(jax.random.fold_in(key, 101), 4)
    factor_a = jax.random.randint(streams[0], (DOCS,), 0, spread + 1)
    factor_b = jax.random.randint(streams[1], (DOCS,), 0, spread + 1)
    factor_c = jax.random.randint(streams[2], (DOCS,), 0, spread + 1)
    counts = 5 + factor_a * factor_b * factor_c // (spread * spread)
    shuffled = jax.random.permutation(streams[3], DOCS)
    counts = counts.at[shuffled[0]].set(SEG_MOST)
    counts = counts.at[shuffled[1]].set(5)
    return (counts.astype(jnp.int32), shuffled[0])


def draw_seg_count(key, part):
    counts, top_doc = count_draw(key)
    return counts


def draw_seg_align(key, part):
    counts, top_doc = count_draw(key)
    key = jax.random.fold_in(key, 5)
    raw_bits = jax.random.randint(key, (DOCS, TEXT), 0, 1 << 20)
    aligned = raw_bits % counts[:, None]
    aligned = aligned.at[top_doc, 0].set(SEG_MOST - 1)
    return aligned.astype(jnp.int32)


def spiked(result, stream_key, source, target, shards_of, factor):
    owner, partner = [(jnp.arange(result.shape[axis_at]) // (result.shape[axis_at] // shards_of)).reshape([-1 if axis == axis_at else 1 for axis in range(result.ndim)]) for axis_at in (source, target)]
    chosen = jax.random.permutation(stream_key, shards_of)[partner]
    strong = (owner == chosen) | (owner == (partner + shards_of // 2) % shards_of)
    return jnp.where(strong, factor * result, result)


def level_of(rng, dims, cuts, low, top_value):
    factor_of, own = 1.0, jax.random.fold_in(rng, 6)
    for position, blocks in cuts:
        heights = jnp.exp(jax.random.uniform(jax.random.fold_in(own, position), (blocks,), jnp.float32, low / len(cuts), top_value / len(cuts)))
        factor_of = factor_of * jnp.repeat(heights, dims[position] // blocks).reshape([-1 if axis == position else 1 for axis in range(len(dims))])
    return factor_of


def noise(key, shape, scale, most, cuts=(), held_as=jnp.bfloat16):
    factor_of = level_of(key, shape, cuts, -0.22, 0.18) if cuts else 1.0
    values = jax.random.normal(key, shape, jnp.float32) * scale * factor_of
    return jnp.minimum(jnp.maximum(values, -most), most).astype(held_as)


def gaussian_with(stream_key, extent, scale, most, shards, heavy, kind=jnp.bfloat16):
    entries = scale * jax.random.normal(stream_key, extent, jnp.float32)
    if shards:
        entries = entries * level_of(stream_key, extent, shards, -0.22, 0.18)
    return jnp.clip(spiked(entries, jax.random.fold_in(stream_key, 3), *heavy), -most, most).astype(kind)


def setup_inputs(seed: int = 0) -> dict:
    key_list = jax.random.split(jax.random.key(seed), 18)
    tokens = gaussian_with(key_list[0], (DOCS, SLOTS, D), 1.0, 6.0, ((0, 16), (1, 2)), (0, 2, 16, 2.0))
    seg_count = draw_seg_count(jax.random.fold_in(key_list[17], 71), 0)
    seg_align = draw_seg_align(jax.random.fold_in(key_list[17], 71), 0)
    cotangent = gaussian_with(key_list[3], (DOCS, SLOTS, D), 1.0, 6.0, ((0, 16), (1, 2)), (0, 2, 16, 2.0))
    qkv_weight = noise(key_list[4], (D, 3 * D), D ** -0.5, 0.21875)
    query_bias = noise(key_list[5], (D,), 0.5, 3.0, (), jnp.float32)
    value_bias = noise(key_list[6], (D,), 0.5, 3.0, (), jnp.float32)
    output_weight = noise(key_list[7], (D, D), (D * 8 // SLOTS) ** -0.5, 2.0)
    output_bias = noise(key_list[8], (D,), 0.5, 3.0, (), jnp.float32)
    first_gain = jnp.clip(1.0 + 0.18 * jax.random.normal(key_list[9], (D,), jnp.float32), 0.1, 1.9)
    first_shift = noise(key_list[10], (D,), 0.5, 3.0, (), jnp.float32)
    inner_weight = noise(key_list[11], (D, FF), D ** -0.5, 0.21875)
    inner_bias = noise(key_list[12], (FF,), 0.5, 3.0, (), jnp.float32)
    outer_weight = noise(key_list[13], (FF, D), FF ** -0.5, 0.109375)
    outer_bias = noise(key_list[14], (D,), 0.5, 3.0, (), jnp.float32)
    second_gain = jnp.clip(1.0 + 0.18 * jax.random.normal(key_list[15], (D,), jnp.float32), 0.1, 1.9)
    second_shift = noise(key_list[16], (D,), 0.5, 3.0, (), jnp.float32)
    return {"tokens": tokens, "seg_count": seg_count, "seg_align": seg_align, "cotangent": cotangent, "qkv_weight": qkv_weight, "query_bias": query_bias, "value_bias": value_bias, "output_weight": output_weight, "output_bias": output_bias, "first_gain": first_gain, "first_shift": first_shift, "inner_weight": inner_weight, "inner_bias": inner_bias, "outer_weight": outer_weight, "outer_bias": outer_bias, "second_gain": second_gain, "second_shift": second_shift}


LAYOUT_REWARD = 2.0
BLOCKED_SCORE = -1000000000.0
NORM_EPS = 1e-05

@jax.custom_vjp
def low(v):
    return lax.optimization_barrier(v.astype(jnp.bfloat16)).astype(jnp.float32)

@jax.custom_vjp
def low_back(v):
    return v

def low_keep(v):
    return (low(v), None)

def low_pass(kept, grad):
    return (grad,)

def back_keep(v):
    return (v, None)

def back_low(kept, grad):
    return (low(grad),)
low.defvjp(low_keep, low_pass)
low_back.defvjp(back_keep, back_low)

def slot_groups(seg_count, seg_align, all_slots):
    doc_count, text_slots = seg_align.shape
    slot_index = jnp.arange(all_slots, dtype=jnp.int32)
    filler = jnp.zeros((doc_count, all_slots - text_slots), jnp.int32)
    padded = jnp.concatenate([seg_align.astype(jnp.int32), filler], axis=1)
    is_text = slot_index < text_slots
    groups = jnp.where(is_text[None, :], padded, (slot_index - text_slots)[None, :])
    present_keys = slot_index[None, :] < text_slots + seg_count.astype(jnp.int32)[:, None]
    return (groups, is_text, present_keys)

def layer_norm(hidden, gain, shift):
    centre = hidden - lax.optimization_barrier(jnp.mean(hidden, axis=-1, keepdims=True))
    spread = lax.optimization_barrier(jnp.mean(centre * centre, axis=-1, keepdims=True))
    return centre * lax.rsqrt(spread + NORM_EPS) * gain + shift

def smooth_gate(inner):
    return jax.nn.gelu(inner, approximate=False)

def matmul(left, right):
    return jnp.dot(left, right, precision=lax.Precision.HIGHEST)

def document_layer(params, doc_rows, doc_groups, is_text, document_present):
    qkv_weight, query_bias, value_bias, output_weight, output_bias, first_gain, first_shift, inner_weight, inner_bias, outer_weight, outer_bias, second_gain, second_shift = params
    slot_count, features = doc_rows.shape
    head_dim = features // H
    scaling = head_dim ** (-0.5)
    pre = matmul(doc_rows, qkv_weight)
    queries = low(low_back(pre[:, :features] + query_bias))
    all_keys = low(low_back(pre[:, features:2 * features]))
    values = low(low_back(pre[:, 2 * features:] + value_bias))
    query_heads = queries.reshape(slot_count, H, head_dim)
    key_heads = all_keys.reshape(slot_count, H, head_dim)
    value_heads = values.reshape(slot_count, H, head_dim)
    unadjusted_scores = jnp.einsum('qhd,khd->hqk', query_heads, key_heads, precision=lax.Precision.HIGHEST) * scaling
    matched_pairs = (doc_groups[:, None] == doc_groups[None, :]) & (is_text[:, None] != is_text[None, :])
    logit_scores = jnp.where(document_present[None, None, :], unadjusted_scores + LAYOUT_REWARD * matched_pairs.astype(jnp.float32)[None], BLOCKED_SCORE)
    logit_scores = low_back(logit_scores)
    attn_probs = jax.nn.softmax(logit_scores, axis=-1)
    context = jnp.einsum('hqk,khd->qhd', low(attn_probs), value_heads, precision=lax.Precision.HIGHEST)
    context = low(low_back(context.reshape(slot_count, features)))
    attended = low_back(matmul(context, output_weight) + output_bias)
    normed_one = layer_norm(doc_rows + attended, first_gain, first_shift)
    inner = low_back(matmul(low(normed_one), inner_weight) + inner_bias)
    hidden = low(smooth_gate(inner))
    mlp_out = low_back(matmul(hidden, outer_weight) + outer_bias)
    return layer_norm(normed_one + mlp_out, second_gain, second_shift)

def reference(tokens, seg_count, seg_align, cotangent, qkv_weight, query_bias, value_bias, output_weight, output_bias, first_gain, first_shift, inner_weight, inner_bias, outer_weight, outer_bias, second_gain, second_shift):
    weights = (qkv_weight.astype(jnp.float32), query_bias.astype(jnp.float32), value_bias.astype(jnp.float32), output_weight.astype(jnp.float32), output_bias.astype(jnp.float32), first_gain.astype(jnp.float32), first_shift.astype(jnp.float32), inner_weight.astype(jnp.float32), inner_bias.astype(jnp.float32), outer_weight.astype(jnp.float32), outer_bias.astype(jnp.float32), second_gain.astype(jnp.float32), second_shift.astype(jnp.float32))
    groups, is_text, present_keys = slot_groups(seg_count, seg_align, SLOTS)
    inputs = tokens.astype(jnp.float32)
    pulled = cotangent.astype(jnp.float32)

    def doc_step(summed, doc_item):
        doc_rows, doc_cotangent, doc_groups, document_present = doc_item

        def forward(params, rows_in):
            return document_layer(params, rows_in, doc_groups, is_text, document_present)
        doc_output, pull_back = jax.vjp(forward, weights, doc_rows)
        weight_grads, rows_grad = pull_back(doc_cotangent)
        summed = jax.tree.map(jnp.add, summed, weight_grads)
        return (summed, (doc_output, rows_grad))
    zero_grads = jax.tree.map(jnp.zeros_like, weights)
    summed, (outputs, rows_grads) = lax.scan(doc_step, zero_grads, (inputs, pulled, groups, present_keys))
    return (outputs.astype(jnp.bfloat16), rows_grads.astype(jnp.bfloat16), summed[0], summed[1], summed[2], summed[3], summed[4], summed[5], summed[6], summed[7], summed[8], summed[9], summed[10], summed[11], summed[12])
```

```python
import functools

import jax
import jax.numpy as jnp
from jax import lax
from jax.experimental import pallas as pl
from jax.experimental.pallas import tpu as pltpu
from jax.sharding import PartitionSpec as P

H = 12


LAYOUT_REWARD = 2.0
BLOCKED_SCORE = -1000000000.0
NORM_EPS = 1e-05


MESH = pl.DeviceIdType.MESH
BITS = {"c": 0, "y": 1, "l": 2, "h": 3}


def add_into(target, other, rows):
    lead = target.shape[:-2]
    total = 1
    for size in lead:
        total *= size
    row_step = 16
    while rows % (row_step * 2) == 0 and row_step < 64:
        row_step *= 2

    def step(index, carry):
        row = pl.multiple_of((index % (rows // row_step)) * row_step, row_step)
        rest = index // (rows // row_step)
        place = []
        for size in reversed(lead):
            place.append(rest % size)
            rest = rest // size
        place = tuple(reversed(place)) + (pl.ds(row, row_step), slice(None))
        target[place] = (
            target[place].astype(jnp.float32) + other[place].astype(jnp.float32)
        ).astype(jnp.bfloat16)
        return carry

    lax.fori_loop(0, total * (rows // row_step), step, 0)


class Job:
    def __init__(self, source, rows, columns, order, buffers, me, seq, sems):
        self.current = source
        self.rows, self.columns = rows, columns
        self.order, self.buffers = order, buffers
        self.me, self.seq = me, seq
        self.sems = sems
        self.bits = ["h", "l", "y", "c"]
        self.stage = 0
        self.copy = None

    def start(self):
        bit = self.order[self.stage]
        buffer = self.buffers[self.stage]
        lead = (slice(None),) * len(self.bits)
        if bit == "x":
            half = self.columns // 2
            given = self.current.at[lead + (slice(None), pl.ds(pl.multiple_of((1 - self.seq) * half, 128), half))]
            self.own = self.current.at[lead + (slice(None), pl.ds(pl.multiple_of(self.seq * half, 128), half))]
            device = (self.me, 1 - self.seq)
            self.columns = half
        elif bit == "g":
            given = self.current
            device = (self.me, 1 - self.seq)
        else:
            place = self.bits.index(bit)
            weight = 1 << BITS[bit]
            mine = (self.me // weight) % 2
            given = self.current.at[(slice(None),) * place + (1 - mine,)]
            self.own = self.current.at[(slice(None),) * place + (mine,)]
            device = (self.me + weight * (1 - 2 * mine), self.seq)
            self.bits.pop(place)
        self.copy = pltpu.make_async_remote_copy(
            src_ref=given, dst_ref=buffer, send_sem=self.sems[0].at[self.stage], recv_sem=self.sems[1].at[self.stage],
            device_id=device, device_id_type=MESH)
        self.copy.start()

    def finish(self):
        self.copy.wait()
        buffer = self.buffers[self.stage]
        if self.order[self.stage] != "g":
            add_into(buffer, self.own, self.rows)
            self.current = buffer
        self.stage += 1


def job_shapes(rows, columns, order):
    bits = 4
    shapes = []
    for bit in order:
        if bit == "x":
            columns //= 2
        elif bit != "g":
            bits -= 1
        shapes.append((2,) * bits + (rows, columns))
    return shapes


def job_table(shapes):
    jobs = []
    for index, (rows, columns) in enumerate(shapes):
        if rows % 48 == 0 and rows > 48:
            cut = rows // 3
            jobs.append((index, 0, cut, 0, columns, "cxlhyg"))
            jobs.append((index, cut, rows - cut, 0, columns, "cyxlhg"))
        elif columns % 768 == 0 and columns > 768:
            cut = columns // 3 // 256 * 256
            jobs.append((index, 0, rows, 0, cut, "cxlhyg"))
            jobs.append((index, 0, rows, cut, columns - cut, "cyxlhg"))
        else:
            jobs.append((index, 0, rows, 0, columns, "cyxlhg"))
    return jobs


def sum_kernel(table, n_tensors, *refs):
    tensors, small = refs[:n_tensors], refs[n_tensors]
    outs, small_out = refs[n_tensors + 1 : 2 * n_tensors + 1], refs[2 * n_tensors + 1]
    rest = list(refs[2 * n_tensors + 2 :])
    me, seq = lax.axis_index("dp"), lax.axis_index("seq")
    barrier = pltpu.get_barrier_semaphore()
    partners = [(me, 1 - seq)]
    for bit in "cylh":
        weight = 1 << BITS[bit]
        partners.append((me + weight * (1 - 2 * ((me // weight) % 2)), seq))
    for partner in partners:
        pl.semaphore_signal(barrier, inc=1, device_id=partner, device_id_type=MESH)
    pl.semaphore_wait(barrier, len(partners))
    jobs = []
    for index, row, rows, column, columns, order in table:
        buffers = [rest.pop(0) for _ in order]
        sems = (rest.pop(0), rest.pop(0))
        lead = (slice(None),) * 4
        source = tensors[index].at[lead + (pl.ds(row, rows), pl.ds(column, columns))]
        jobs.append(Job(source, rows, columns, order, buffers, me, seq, sems))
    small_buffers, small_send, small_recv = rest
    small_out[...] = small[...]

    def small_copy(stage):
        partner = partners[stage]
        return pltpu.make_async_remote_copy(
            src_ref=small_out if stage == 0 else small_out, dst_ref=small_buffers.at[stage],
            send_sem=small_send.at[stage], recv_sem=small_recv.at[stage], device_id=partner, device_id_type=MESH)

    for job in jobs:
        job.start()
    small_copy(0).start()
    stages = len(table[0][-1])
    for stage in range(stages):
        for job in jobs:
            job.finish()
            if stage + 1 < stages:
                job.start()
        if stage < len(partners):
            small_copy(stage).wait()
            small_out[...] += small_buffers[stage]
            if stage + 1 < len(partners):
                small_copy(stage + 1).start()
    for job, (index, row, rows, column, columns, order) in zip(jobs, table):
        half = columns // 2
        out = outs[index]
        kept, got = job.current, job.buffers[-1]
        for side in range(2):
            @pl.when(seq == side)
            def _():
                out[pl.ds(row, rows), pl.ds(column + side * half, half)] = kept[...].astype(jnp.float32)
                out[pl.ds(row, rows), pl.ds(column + (1 - side) * half, half)] = got[...].astype(jnp.float32)


def sum_over_mesh(grads, small):
    shapes = [(grad.shape[0] // 16, grad.shape[1]) for grad in grads]
    table = job_table(shapes)
    scratch = []
    for index, row, rows, column, columns, order in table:
        scratch += [pltpu.VMEM(shape, jnp.bfloat16) for shape in job_shapes(rows, columns, order)]
        scratch += [pltpu.SemaphoreType.DMA((len(order),))] * 2
    scratch += [pltpu.VMEM((5,) + small.shape, jnp.float32), pltpu.SemaphoreType.DMA((5,)), pltpu.SemaphoreType.DMA((5,))]
    blocks = [grad.reshape(2, 2, 2, 2, rows, columns) for grad, (rows, columns) in zip(grads, shapes)]
    vmem = pl.BlockSpec(memory_space=pltpu.VMEM)
    return pl.pallas_call(
        functools.partial(sum_kernel, table, len(grads)),
        out_shape=[jax.ShapeDtypeStruct(shape, jnp.float32) for shape in shapes] + [jax.ShapeDtypeStruct(small.shape, jnp.float32)],
        in_specs=[vmem] * (len(grads) + 1),
        out_specs=[vmem] * (len(grads) + 1),
        scratch_shapes=scratch,
        compiler_params=pltpu.CompilerParams(collective_id=0, has_side_effects=True, vmem_limit_bytes=60 * 2**20),
    )(*blocks, small)


def slot_groups(seg_count, seg_align, all_slots):
    doc_count, text_slots = seg_align.shape
    slot_index = jnp.arange(all_slots, dtype=jnp.int32)
    filler = jnp.zeros((doc_count, all_slots - text_slots), jnp.int32)
    padded = jnp.concatenate([seg_align, filler], axis=1)
    is_text = slot_index < text_slots
    groups = jnp.where(is_text[None, :], padded, (slot_index - text_slots)[None, :])
    present_keys = slot_index[None, :] < text_slots + seg_count[:, None]
    return (groups, is_text, present_keys)


def layer_norm(hidden, gain, shift):
    centre = hidden - jnp.mean(hidden, axis=-1, keepdims=True)
    spread = jnp.mean(centre * centre, axis=-1, keepdims=True)
    return centre * lax.rsqrt(spread + NORM_EPS) * gain + shift


def smooth_gate(inner):
    return jax.nn.gelu(inner, approximate=False)


def softmax_rows(logit_scores):
    return jax.nn.softmax(logit_scores, axis=-1)


def project(tokens, qkv_weight, query_bias, value_bias):
    doc_count, slot_count, features = tokens.shape
    token_rows = tokens.reshape(doc_count * slot_count, features)
    pre = jnp.dot(token_rows, qkv_weight, preferred_element_type=jnp.float32)
    queries = (pre[:, :features] + query_bias).astype(jnp.bfloat16)
    own_keys = (
        pre[:, features : 2 * features]
        .astype(jnp.bfloat16)
        .reshape(doc_count, slot_count, features)
    )
    own_values = (
        (pre[:, 2 * features :] + value_bias)
        .astype(jnp.bfloat16)
        .reshape(doc_count, slot_count, features)
    )
    return (queries, own_keys, own_values)


def local(
    tokens,
    seg_count,
    seg_align,
    cotangent,
    qkv_weight,
    query_bias,
    value_bias,
    output_weight,
    output_bias,
    first_gain,
    first_shift,
    inner_weight,
    inner_bias,
    outer_weight,
    outer_bias,
    second_gain,
    second_shift,
):
    tokens = lax.all_to_all(tokens, "seq", 0, 1, tiled=True)
    cotangent = lax.all_to_all(cotangent, "seq", 0, 1, tiled=True)
    doc_count, slot_count, features = tokens.shape
    row_count = doc_count * slot_count
    seg_count = lax.dynamic_slice_in_dim(seg_count, lax.axis_index("seq") * doc_count, doc_count, 0)
    seg_align = lax.dynamic_slice_in_dim(seg_align, lax.axis_index("seq") * doc_count, doc_count, 0)
    head_dim = features // H
    scaling = head_dim ** (-0.5)
    all_slots = slot_count
    groups, is_text, present_keys = slot_groups(seg_count, seg_align, all_slots)
    matched_pairs = (groups[:, :, None] == groups[:, None, :]) & (
        is_text[None, :, None] != is_text[None, None, :]
    )
    layout_reward = LAYOUT_REWARD * matched_pairs.astype(jnp.float32)
    queries, all_keys, values = project(tokens, qkv_weight, query_bias, value_bias)
    query_heads = queries.reshape(doc_count, slot_count, H, head_dim)
    key_heads = all_keys.reshape(doc_count, all_slots, H, head_dim)
    value_heads = values.reshape(doc_count, all_slots, H, head_dim)
    unadjusted_scores = (
        jnp.einsum("bqhd,bkhd->bhqk", query_heads, key_heads, preferred_element_type=jnp.float32)
        * scaling
    )
    logit_scores = jnp.where(
        present_keys[:, None, None, :], unadjusted_scores + layout_reward[:, None], BLOCKED_SCORE
    )
    attn_probs, soft_pull = jax.vjp(softmax_rows, logit_scores)
    probs_low = attn_probs.astype(jnp.bfloat16)
    context = jnp.einsum(
        "bhqk,bkhd->bqhd", probs_low, value_heads, preferred_element_type=jnp.float32
    )
    context = context.reshape(row_count, features).astype(jnp.bfloat16)
    token_rows = tokens.reshape(row_count, features)
    attended = jnp.dot(context, output_weight, preferred_element_type=jnp.float32) + output_bias
    normed_one, first_pull = jax.vjp(
        layer_norm, token_rows.astype(jnp.float32) + attended, first_gain, first_shift
    )
    normed_low = normed_one.astype(jnp.bfloat16)
    inner = jnp.dot(normed_low, inner_weight, preferred_element_type=jnp.float32) + inner_bias
    activated, gate_pull = jax.vjp(smooth_gate, inner)
    hidden = activated.astype(jnp.bfloat16)
    mlp_out = jnp.dot(hidden, outer_weight, preferred_element_type=jnp.float32) + outer_bias
    layer_out, second_pull = jax.vjp(layer_norm, normed_one + mlp_out, second_gain, second_shift)
    grad_out = cotangent.reshape(row_count, features).astype(jnp.float32)
    grad_second, second_gain_grad, second_shift_grad = second_pull(grad_out)
    grad_mlp = grad_second.astype(jnp.bfloat16)
    outer_weight_grad = jnp.einsum(
        "rf,rd->fd", hidden, grad_mlp, preferred_element_type=jnp.float32
    )
    outer_bias_grad = jnp.sum(grad_mlp.astype(jnp.float32), axis=0)
    grad_hidden = jnp.einsum(
        "rd,fd->rf", grad_mlp, outer_weight, preferred_element_type=jnp.float32
    )
    grad_inner = gate_pull(grad_hidden)[0].astype(jnp.bfloat16)
    inner_weight_grad = jnp.einsum(
        "rd,rf->df", normed_low, grad_inner, preferred_element_type=jnp.float32
    )
    inner_bias_grad = jnp.sum(grad_inner.astype(jnp.float32), axis=0)
    grad_normed = grad_second + jnp.einsum(
        "rf,df->rd", grad_inner, inner_weight, preferred_element_type=jnp.float32
    )
    grad_first, first_gain_grad, first_shift_grad = first_pull(grad_normed)
    grad_attended = grad_first.astype(jnp.bfloat16)
    output_weight_grad = jnp.einsum(
        "rc,rd->cd", context, grad_attended, preferred_element_type=jnp.float32
    )
    output_bias_grad = jnp.sum(grad_attended.astype(jnp.float32), axis=0)
    grad_context = jnp.einsum(
        "rd,cd->rc", grad_attended, output_weight, preferred_element_type=jnp.float32
    )
    grad_context = grad_context.astype(jnp.bfloat16).reshape(doc_count, slot_count, H, head_dim)
    grad_probs = jnp.einsum(
        "bqhd,bkhd->bhqk", grad_context, value_heads, preferred_element_type=jnp.float32
    )
    grad_scores = soft_pull(grad_probs)[0].astype(jnp.bfloat16)
    grad_queries = (
        jnp.einsum("bhqk,bkhd->bqhd", grad_scores, key_heads, preferred_element_type=jnp.float32)
        * scaling
    )
    grad_queries = grad_queries.astype(jnp.bfloat16).reshape(row_count, features)
    key_term = (
        jnp.einsum("bhqk,bqhd->bkhd", grad_scores, query_heads, preferred_element_type=jnp.float32)
        * scaling
    )
    value_term = jnp.einsum(
        "bhqk,bqhd->bkhd", probs_low, grad_context, preferred_element_type=jnp.float32
    )
    grad_keys = key_term.astype(jnp.bfloat16).reshape(row_count, features)
    grad_values = value_term.astype(jnp.bfloat16).reshape(row_count, features)
    grad_project = jnp.concatenate([grad_queries, grad_keys, grad_values], axis=1)
    qkv_weight_grad = jnp.einsum(
        "rd,re->de", token_rows, grad_project, preferred_element_type=jnp.float32
    )
    query_bias_grad = jnp.sum(grad_queries.astype(jnp.float32), axis=0)
    value_bias_grad = jnp.sum(grad_values.astype(jnp.float32), axis=0)
    tokens_grad = grad_first + jnp.einsum(
        "re,de->rd", grad_project, qkv_weight, preferred_element_type=jnp.float32
    )
    tokens_grad = tokens_grad.astype(jnp.bfloat16).reshape(doc_count, slot_count, features)
    vectors = [
        query_bias_grad,
        value_bias_grad,
        output_bias_grad,
        first_gain_grad,
        first_shift_grad,
        outer_bias_grad,
        second_gain_grad,
        second_shift_grad,
        inner_bias_grad,
    ]
    matrices = [outer_weight_grad, inner_weight_grad, output_weight_grad, qkv_weight_grad]
    dp = lax.axis_size("dp")
    if dp == 16 and lax.axis_size("seq") == 2:
        flat = jnp.concatenate(vectors + [jnp.zeros((16 * features - sum(v.size for v in vectors),), jnp.float32)])
        *matrices, sums = sum_over_mesh([m.astype(jnp.bfloat16) for m in matrices], flat.reshape(16, features))
        sums, place, parts = sums.reshape(-1), 0, []
        for vector in vectors:
            share = vector.size // dp
            parts.append(lax.dynamic_slice_in_dim(sums, place + lax.axis_index("dp") * share, share, 0))
            place += vector.size
        vectors = parts
    else:
        matrices, vectors = [
            [
                lax.psum(lax.psum_scatter(v, "dp", scatter_dimension=0, tiled=True), "seq")
                for v in group
            ]
            for group in (matrices, vectors)
        ]
    summed = (
        matrices[3],
        vectors[0],
        vectors[1],
        matrices[2],
        vectors[2],
        vectors[3],
        vectors[4],
        matrices[1],
        vectors[8],
        matrices[0],
        vectors[5],
        vectors[6],
        vectors[7],
    )
    block_output = layer_out.astype(jnp.bfloat16).reshape(doc_count, slot_count, features)
    block_output = lax.all_to_all(block_output, "seq", 1, 0, tiled=True)
    tokens_grad = lax.all_to_all(tokens_grad, "seq", 1, 0, tiled=True)
    return (
        block_output,
        tokens_grad,
        summed[0],
        summed[1],
        summed[2],
        summed[3],
        summed[4],
        summed[5],
        summed[6],
        summed[7],
        summed[8],
        summed[9],
        summed[10],
        summed[11],
        summed[12],
    )


def solution(mesh):
    return jax.shard_map(
        local,
        mesh=mesh,
        in_specs=(
            P("dp", "seq", None),
            P("dp"),
            P("dp", None),
            P("dp", "seq", None),
            P(),
            P(),
            P(),
            P(),
            P(),
            P(),
            P(),
            P(),
            P(),
            P(),
            P(),
            P(),
            P(),
        ),
        out_specs=(
            P("dp", "seq", None),
            P("dp", "seq", None),
            P("dp", None),
            P("dp"),
            P("dp"),
            P("dp", None),
            P("dp"),
            P("dp"),
            P("dp"),
            P("dp", None),
            P("dp"),
            P("dp", None),
            P("dp"),
            P("dp"),
            P("dp"),
        ),
        check_vma=False,
    )
```

```python
import functools

import jax
import jax.numpy as jnp
from jax import lax
from jax.experimental import pallas as pl
from jax.experimental.pallas import tpu as pltpu
from jax.sharding import PartitionSpec as P

MESH = pl.DeviceIdType.MESH
BITS = {"c": 0, "y": 1, "l": 2, "h": 3}


def add_into(target, other, rows):
    lead = target.shape[:-2]
    total = 1
    for size in lead:
        total *= size
    row_step = 16
    while rows % (row_step * 2) == 0 and row_step < 64:
        row_step *= 2

    def step(index, carry):
        row = pl.multiple_of((index % (rows // row_step)) * row_step, row_step)
        rest = index // (rows // row_step)
        place = []
        for size in reversed(lead):
            place.append(rest % size)
            rest = rest // size
        place = tuple(reversed(place)) + (pl.ds(row, row_step), slice(None))
        target[place] = (
            target[place].astype(jnp.float32) + other[place].astype(jnp.float32)
        ).astype(jnp.bfloat16)
        return carry

    lax.fori_loop(0, total * (rows // row_step), step, 0)


class Job:
    def __init__(self, source, rows, columns, order, buffers, me, seq, sems):
        self.current = source
        self.rows, self.columns = rows, columns
        self.order, self.buffers = order, buffers
        self.me, self.seq = me, seq
        self.sems = sems
        self.bits = ["h", "l", "y", "c"]
        self.stage = 0
        self.copy = None

    def start(self):
        bit = self.order[self.stage]
        buffer = self.buffers[self.stage]
        lead = (slice(None),) * len(self.bits)
        if bit == "x":
            half = self.columns // 2
            given = self.current.at[lead + (slice(None), pl.ds(pl.multiple_of((1 - self.seq) * half, 128), half))]
            self.own = self.current.at[lead + (slice(None), pl.ds(pl.multiple_of(self.seq * half, 128), half))]
            device = (self.me, 1 - self.seq)
            self.columns = half
        elif bit == "g":
            given = self.current
            device = (self.me, 1 - self.seq)
        else:
            place = self.bits.index(bit)
            weight = 1 << BITS[bit]
            mine = (self.me // weight) % 2
            given = self.current.at[(slice(None),) * place + (1 - mine,)]
            self.own = self.current.at[(slice(None),) * place + (mine,)]
            device = (self.me + weight * (1 - 2 * mine), self.seq)
            self.bits.pop(place)
        self.copy = pltpu.make_async_remote_copy(
            src_ref=given, dst_ref=buffer, send_sem=self.sems[0].at[self.stage], recv_sem=self.sems[1].at[self.stage],
            device_id=device, device_id_type=MESH)
        self.copy.start()

    def finish(self):
        self.copy.wait()
        buffer = self.buffers[self.stage]
        if self.order[self.stage] != "g":
            add_into(buffer, self.own, self.rows)
            self.current = buffer
        self.stage += 1


def job_shapes(rows, columns, order):
    bits = 4
    shapes = []
    for bit in order:
        if bit == "x":
            columns //= 2
        elif bit != "g":
            bits -= 1
        shapes.append((2,) * bits + (rows, columns))
    return shapes


def job_table(shapes):
    jobs = []
    for index, (rows, columns) in enumerate(shapes):
        if rows % 48 == 0 and rows > 48:
            cut = rows // 3
            jobs.append((index, 0, cut, 0, columns, "cxlhyg"))
            jobs.append((index, cut, rows - cut, 0, columns, "cyxlhg"))
        elif columns % 768 == 0 and columns > 768:
            cut = columns // 3 // 256 * 256
            jobs.append((index, 0, rows, 0, cut, "cxlhyg"))
            jobs.append((index, 0, rows, cut, columns - cut, "cyxlhg"))
        else:
            jobs.append((index, 0, rows, 0, columns, "cyxlhg"))
    return jobs


def sum_kernel(table, n_tensors, *refs):
    tensors, small = refs[:n_tensors], refs[n_tensors]
    outs, small_out = refs[n_tensors + 1 : 2 * n_tensors + 1], refs[2 * n_tensors + 1]
    rest = list(refs[2 * n_tensors + 2 :])
    me, seq = lax.axis_index("dp"), lax.axis_index("seq")
    barrier = pltpu.get_barrier_semaphore()
    partners = [(me, 1 - seq)]
    for bit in "cylh":
        weight = 1 << BITS[bit]
        partners.append((me + weight * (1 - 2 * ((me // weight) % 2)), seq))
    for partner in partners:
        pl.semaphore_signal(barrier, inc=1, device_id=partner, device_id_type=MESH)
    pl.semaphore_wait(barrier, len(partners))
    jobs = []
    for index, row, rows, column, columns, order in table:
        buffers = [rest.pop(0) for _ in order]
        sems = (rest.pop(0), rest.pop(0))
        lead = (slice(None),) * 4
        source = tensors[index].at[lead + (pl.ds(row, rows), pl.ds(column, columns))]
        jobs.append(Job(source, rows, columns, order, buffers, me, seq, sems))
    small_buffers, small_send, small_recv = rest
    small_out[...] = small[...]

    def small_copy(stage):
        partner = partners[stage]
        return pltpu.make_async_remote_copy(
            src_ref=small_out if stage == 0 else small_out, dst_ref=small_buffers.at[stage],
            send_sem=small_send.at[stage], recv_sem=small_recv.at[stage], device_id=partner, device_id_type=MESH)

    for job in jobs:
        job.start()
    small_copy(0).start()
    stages = len(table[0][-1])
    for stage in range(stages):
        for job in jobs:
            job.finish()
            if stage + 1 < stages:
                job.start()
        if stage < len(partners):
            small_copy(stage).wait()
            small_out[...] += small_buffers[stage]
            if stage + 1 < len(partners):
                small_copy(stage + 1).start()
    for job, (index, row, rows, column, columns, order) in zip(jobs, table):
        half = columns // 2
        out = outs[index]
        kept, got = job.current, job.buffers[-1]
        for side in range(2):
            @pl.when(seq == side)
            def _():
                out[pl.ds(row, rows), pl.ds(column + side * half, half)] = kept[...].astype(jnp.float32)
                out[pl.ds(row, rows), pl.ds(column + (1 - side) * half, half)] = got[...].astype(jnp.float32)


def sum_over_mesh(grads, small):
    shapes = [(grad.shape[0] // 16, grad.shape[1]) for grad in grads]
    table = job_table(shapes)
    scratch = []
    for index, row, rows, column, columns, order in table:
        scratch += [pltpu.VMEM(shape, jnp.bfloat16) for shape in job_shapes(rows, columns, order)]
        scratch += [pltpu.SemaphoreType.DMA((len(order),))] * 2
    scratch += [pltpu.VMEM((5,) + small.shape, jnp.float32), pltpu.SemaphoreType.DMA((5,)), pltpu.SemaphoreType.DMA((5,))]
    blocks = [grad.reshape(2, 2, 2, 2, rows, columns) for grad, (rows, columns) in zip(grads, shapes)]
    vmem = pl.BlockSpec(memory_space=pltpu.VMEM)
    return pl.pallas_call(
        functools.partial(sum_kernel, table, len(grads)),
        out_shape=[jax.ShapeDtypeStruct(shape, jnp.float32) for shape in shapes] + [jax.ShapeDtypeStruct(small.shape, jnp.float32)],
        in_specs=[vmem] * (len(grads) + 1),
        out_specs=[vmem] * (len(grads) + 1),
        scratch_shapes=scratch,
        compiler_params=pltpu.CompilerParams(collective_id=0, has_side_effects=True, vmem_limit_bytes=60 * 2**20),
    )(*blocks, small)


LAYOUT_REWARD = 2.0
BLOCKED_SCORE = -1000000000.0
NORM_EPS = 1e-05
LOG2E = 1.4426950408889634
HEAD = 64
PAIR = 128
WIDE = 256
BF, F32 = jnp.bfloat16, jnp.float32


def dot(left, right):
    return jnp.dot(left, right, preferred_element_type=F32)


def dot_nt(left, right):
    return lax.dot_general(left, right, (((1,), (1,)), ((), ())), preferred_element_type=F32)


def dot_tn(left, right):
    return lax.dot_general(left, right, (((0,), (0,)), ((), ())), preferred_element_type=F32)


def at(start, size):
    return pl.ds(pl.multiple_of(start, size), size)


def loop(count, body):
    def step(index, carry):
        body(index)
        return carry

    lax.fori_loop(0, count, step, 0)


def fold_rows(block):
    rows, columns = block.shape
    return jnp.sum(block.reshape(rows // 8, 8, columns), axis=0)


def project_tokens(x, w_qkv, bias_row, qkv, rows):
    columns = w_qkv.shape[1]

    def body(index):
        here = at(index * WIDE, WIDE)
        qkv[rows, here] = (dot(x[rows, :], w_qkv[:, here]) + bias_row[0:1, here]).astype(BF)

    loop(columns // WIDE, body)


def fill_reward(reward, seg_row, count):
    text = seg_row.shape[1]
    segs = reward.shape[0] - text
    key = lax.broadcasted_iota(jnp.int32, (segs, text), 0)
    match = jnp.where(key == seg_row, LAYOUT_REWARD * LOG2E, 0.0).astype(F32)
    dead = jnp.where(key >= count, BLOCKED_SCORE * LOG2E, 0.0).astype(F32)
    turned = jnp.transpose(match)
    reward[...] = jnp.zeros_like(reward)
    slots = text + segs
    for head in range(2):
        reward[text:slots, head * slots : head * slots + text] = match + dead
        reward[text:slots, head * slots + text : (head + 1) * slots] = dead[:, :segs]
        reward[0:text, head * slots + text : (head + 1) * slots] = turned


def split_heads(block, both):
    slots = block.shape[0]
    first = lax.broadcasted_iota(jnp.int32, block.shape, 1) < HEAD
    zero = jnp.zeros_like(block)
    both[0:slots, :] = jnp.where(first, block, zero)
    both[slots:, :] = jnp.where(first, zero, block)


def attend(qkv, reward, probs_of, context_t, both, turned, side):
    slots, features = qkv.shape[0], qkv.shape[1] // 3
    pairs = features // PAIR
    scaling = HEAD ** (-0.5) * LOG2E

    def pair_step(pair):
        here = at(pair * PAIR, PAIR)
        keys = qkv[:, at(features + pair * PAIR, PAIR)]
        split_heads(qkv[:, here], both)
        turned[...] = jnp.transpose(qkv[:, at(2 * features + pair * PAIR, PAIR)])
        probs = probs_of(pair)

        for chunk in range(2 * slots // WIDE):
            block = slice(chunk * WIDE, (chunk + 1) * WIDE)
            scores = dot_nt(keys, both[block, :]) * scaling + reward[:, block]
            scores = jnp.exp2(scores - jnp.max(scores, axis=0, keepdims=True))
            low = (scores * (1.0 / jnp.sum(scores, axis=0, keepdims=True))).astype(BF)
            probs[:, block] = low
            side[:, block] = dot(turned[...], low).astype(BF)
        context_t[at(pair * PAIR, HEAD), :] = side[:HEAD, :slots]
        context_t[at(pair * PAIR + HEAD, HEAD), :] = side[HEAD:, slots:]

    return pair_step, pairs


def first_norm(x, attended, bias, gain, shift, normal, root, low, rows):
    def body(index):
        here = at(index * rows, rows)
        hidden = x[here, :].astype(F32) + (attended[here, :] + bias[...])
        centre = hidden - jnp.mean(hidden, axis=1, keepdims=True)
        inverse = lax.rsqrt(jnp.mean(centre * centre, axis=1, keepdims=True) + NORM_EPS)
        unit = centre * inverse
        normal[here, :] = unit
        root[here, :] = jnp.broadcast_to(inverse, (rows, PAIR))
        low[here, :] = (unit * gain[...] + shift[...]).astype(BF)

    loop(x.shape[0] // rows, body)


def gate(inner):
    normal = 0.5 * (1.0 + lax.erf(inner * 0.7071067811865476))
    density = jnp.exp2(inner * inner * (-0.5 * LOG2E)) * 0.3989422804014327
    return inner * normal, normal + inner * density


def feed_forward(low, w_inner, b_inner, hidden, slope):
    def body(index):
        here = at(index * WIDE, WIDE)
        value, grade = gate(dot(low[...], w_inner[:, here]) + b_inner[0:1, here])
        hidden[:, here] = value.astype(BF)
        slope[:, here] = grade.astype(BF)

    loop(w_inner.shape[1] // WIDE, body)


def second_norm(normal, first_gain, first_shift, mlp, bias, gain, shift, cotangent, output, grad, grad_low, sums, rows):
    sums[0:3] = jnp.zeros((3,) + sums.shape[1:], F32)

    def body(index):
        here = at(index * rows, rows)
        one = normal[here, :] * first_gain[...] + first_shift[...]
        total = one + (mlp[here, :] + bias[...])
        centre = total - jnp.mean(total, axis=1, keepdims=True)
        inverse = lax.rsqrt(jnp.mean(centre * centre, axis=1, keepdims=True) + NORM_EPS)
        unit = centre * inverse
        output[here, :] = (unit * gain[...] + shift[...]).astype(BF)
        pull = cotangent[here, :].astype(F32)
        scaled = pull * gain[...]
        back = inverse * (
            scaled
            - jnp.mean(scaled, axis=1, keepdims=True)
            - unit * jnp.mean(scaled * unit, axis=1, keepdims=True)
        )
        rounded = back.astype(BF)
        grad[here, :] = back
        grad_low[here, :] = rounded
        sums[0] += fold_rows(pull * unit)
        sums[1] += fold_rows(pull)
        sums[2] += fold_rows(rounded.astype(F32))

    loop(normal.shape[0] // rows, body)


def first_norm_back(grad_second, back, normal, root, gain, grad_first, grad_low, sums, rows):
    sums[3:6] = jnp.zeros((3,) + sums.shape[1:], F32)

    def body(index):
        here = at(index * rows, rows)
        pull = grad_second[here, :] + back[here, :]
        unit = normal[here, :]
        scaled = pull * gain[...]
        inverse = root[here, 0:1]
        first = inverse * (
            scaled
            - jnp.mean(scaled, axis=1, keepdims=True)
            - unit * jnp.mean(scaled * unit, axis=1, keepdims=True)
        )
        rounded = first.astype(BF)
        grad_first[here, :] = first
        grad_low[here, :] = rounded
        sums[3] += fold_rows(pull * unit)
        sums[4] += fold_rows(pull)
        sums[5] += fold_rows(rounded.astype(F32))

    loop(normal.shape[0] // rows, body)


def attend_back(qkv, grad_context, probs_of, grad_qkv, both, both_grad, turned, scores, side):
    slots, features = qkv.shape[0], qkv.shape[1] // 3
    scaling = HEAD ** (-0.5)

    def pair_step(pair):
        here = at(pair * PAIR, PAIR)
        there = at(features + pair * PAIR, PAIR)
        last = at(2 * features + pair * PAIR, PAIR)
        split_heads(qkv[:, here], both)
        split_heads(grad_context[:, here], both_grad)
        turned[...] = jnp.transpose(qkv[:, there])
        values = qkv[:, last]
        probs = probs_of(pair)
        for chunk in range(2 * slots // WIDE):
            block = slice(chunk * WIDE, (chunk + 1) * WIDE)
            pull = dot_nt(values, both_grad[block, :])
            weight = probs[:, block].astype(F32)
            mean = jnp.sum(weight * pull, axis=0, keepdims=True)
            low = (weight * (pull - mean)).astype(BF)
            scores[:, block] = low
            side[:, block] = dot(turned[...], low)
        grad_qkv[:, there] = (dot(scores[...], both[...]) * scaling).astype(BF)
        grad_qkv[:, last] = dot(probs[...], both_grad[...]).astype(BF)
        mine = jnp.concatenate([side[:HEAD, :slots], side[HEAD:, slots:]], axis=0)
        grad_qkv[:, here] = jnp.transpose(mine * scaling).astype(BF)

    return pair_step, features // PAIR


def forward_kernel(x, seg_align, seg_count, w_qkv, bias_row, w_out, b_out, gain, shift,
                   qkv, probs_hbm, context_t, normal, root, low, reward, both, turned, side, attended, probs_buf, sem):
    slots = x.shape[0]
    fill_reward(reward, seg_align[...], seg_count[0])
    project_tokens(x, w_qkv, bias_row, qkv, slice(0, slots))
    step, pairs = attend(qkv, reward, lambda pair: probs_buf.at[pair % 2], context_t, both, turned, side)
    def out_copy(pair):
        return pltpu.make_async_copy(probs_buf.at[pair % 2], probs_hbm.at[pair], sem.at[pair % 2])
    def body(pair):
        @pl.when(pair >= 2)
        def _(): out_copy(pair - 2).wait()
        step(pair)
        out_copy(pair).start()
    loop(pairs, body)
    out_copy(pairs - 2).wait(); out_copy(pairs - 1).wait()
    ctx = jnp.transpose(context_t[...])
    both_ctx = low
    low[...] = ctx
    for c in range(w_out.shape[1] // WIDE):
        here = slice(c * WIDE, (c + 1) * WIDE)
        attended[:, here] = dot(low[...], w_out[:, here])
    first_norm(x, attended, b_out, gain, shift, normal, root, low, 32)

def forward(x, seg_align, seg_count, w_qkv, bias_row, w_out, b_out, gain, shift):
    slots, features = x.shape
    v = pl.BlockSpec(memory_space=pltpu.VMEM)
    return pl.pallas_call(forward_kernel, name='fwd',
        out_shape=[jax.ShapeDtypeStruct((slots, 3*features), BF), jax.ShapeDtypeStruct((features//PAIR, slots, 2*slots), BF),
                   jax.ShapeDtypeStruct((features, slots), BF), jax.ShapeDtypeStruct((slots, features), F32), jax.ShapeDtypeStruct((slots, PAIR), F32), jax.ShapeDtypeStruct((slots, features), BF)],
        in_specs=[v, v, pl.BlockSpec(memory_space=pltpu.SMEM), v, v, v, v, v, v],
        out_specs=[v, pl.BlockSpec(memory_space=pltpu.HBM), v, v, v, v],
        scratch_shapes=[pltpu.VMEM((slots, 2*slots), F32), pltpu.VMEM((2*slots, PAIR), BF), pltpu.VMEM((PAIR, slots), BF), pltpu.VMEM((PAIR, 2*slots), BF), pltpu.VMEM((slots, features), F32),
           pltpu.VMEM((2, slots, 2*slots), BF), pltpu.SemaphoreType.DMA((2,))],
        compiler_params=pltpu.CompilerParams(vmem_limit_bytes=60*2**20))(x, seg_align, seg_count, w_qkv, bias_row, w_out, b_out, gain, shift)


def back1_kernel(cot, normal, root, low,
        w_inner, b_inner, w_outer, b_outer, gain1, shift1, gain2, shift2,
        out, g_inner, g_outer, sums, grad_first, grad_att, hidden, slope, acc, grad_second, grad_mlp, flat):
    slots, features = cot.shape
    wide = w_inner.shape[1]
    sums[...] = jnp.zeros_like(sums)
    feed_forward(low, w_inner, b_inner, hidden, slope)
    for c in range(features // WIDE):
        here = slice(c * WIDE, (c + 1) * WIDE)
        acc[:, here] = dot(hidden[...], w_outer[:, here])
    second_norm(normal, gain1, shift1, acc, b_outer, gain2, shift2, cot, out, grad_second, grad_mlp, sums, 32)
    flat[...] = jnp.transpose(low[...])
    step_w = 768
    def ff(index):
        here = at(index * step_w, step_w)
        g_outer[here, :] = dot_tn(hidden[:, here], grad_mlp[...]).astype(BF)
        low_grad = (dot_nt(grad_mlp[...], w_outer[here, :]) * slope[:, here].astype(F32)).astype(BF)
        hidden[:, here] = low_grad
        g_inner[:, here] = dot(flat[...], low_grad).astype(BF)
    loop(wide // step_w, ff)
    for c in range(wide // features):
        sums[8 + c] = fold_rows(hidden[:, c * features:(c + 1) * features].astype(F32))
    for c in range(features // WIDE):
        here = slice(c * WIDE, (c + 1) * WIDE)
        acc[:, here] = dot_nt(hidden[...], w_inner[here, :])
    first_norm_back(grad_second, acc, normal, root, gain1, grad_first, grad_att, sums, 32)

def back1(*args):
    cot = args[0]; wide = args[4].shape[1]
    slots, features = cot.shape
    v = pl.BlockSpec(memory_space=pltpu.VMEM)
    S = jax.ShapeDtypeStruct; V = pltpu.VMEM
    return pl.pallas_call(back1_kernel, name="back1",
        out_shape=[S((slots, features), BF), S((features, wide), BF), S((wide, features), BF), S((16, 8, features), F32), S((slots, features), F32), S((slots, features), BF)],
        in_specs=[v]*12, out_specs=[v]*6,
        scratch_shapes=[V((slots, wide), BF), V((slots, wide), BF), V((slots, features), F32), V((slots, features), F32), V((slots, features), BF), V((features, slots), BF)],
        compiler_params=pltpu.CompilerParams(vmem_limit_bytes=60*2**20))(*args)

def back2_kernel(x, qkv, probs_hbm, context_t, grad_first, grad_att, w_qkv, w_out,
        tokens_grad, g_qkv, g_out, sums, grad_ctx, grad_qkv,
        both, both_grad, turned, scores, side, flat, probs_buf, sem):
    slots, features = x.shape
    for c in range(features // WIDE):
        here = slice(c * WIDE, (c + 1) * WIDE)
        g_out[:, here] = dot(context_t[...], grad_att[:, here]).astype(BF)
        grad_ctx[:, here] = dot_nt(grad_att[...], w_out[here, :]).astype(BF)
    def in_copy(pair):
        return pltpu.make_async_copy(probs_hbm.at[pair], probs_buf.at[pair % 2], sem.at[pair % 2])
    step, pairs = attend_back(qkv, grad_ctx, lambda pair: probs_buf.at[pair % 2], grad_qkv, both, both_grad, turned, scores, side)
    in_copy(0).start()
    def body(pair):
        @pl.when(pair + 1 < pairs)
        def _(): in_copy(pair + 1).start()
        in_copy(pair).wait()
        step(pair)
    loop(pairs, body)
    sums[0] = fold_rows(grad_qkv[:, :features].astype(F32))
    sums[1] = fold_rows(grad_qkv[:, 2*features:].astype(F32))
    flat[...] = jnp.transpose(x[...])
    def qg(index):
        here = at(index * WIDE, WIDE)
        g_qkv[:, here] = dot(flat[...], grad_qkv[:, here]).astype(BF)
    loop(3 * features // WIDE, qg)
    for c in range(features // WIDE):
        here = slice(c * WIDE, (c + 1) * WIDE)
        tokens_grad[:, here] = (grad_first[:, here] + dot_nt(grad_qkv[...], w_qkv[here, :])).astype(BF)

def back2(*args):
    x = args[0]
    slots, features = x.shape
    v = pl.BlockSpec(memory_space=pltpu.VMEM)
    S = jax.ShapeDtypeStruct; V = pltpu.VMEM
    return pl.pallas_call(back2_kernel, name="back2",
        out_shape=[S((slots, features), BF), S((features, 3*features), BF), S((features, features), BF), S((2, 8, features), F32)],
        in_specs=[v, v, pl.BlockSpec(memory_space=pltpu.HBM)] + [v] * 5,
        out_specs=[v]*4,
        scratch_shapes=[V((slots, features), BF), V((slots, 3*features), BF),
           V((2*slots, PAIR), BF), V((2*slots, PAIR), BF), V((PAIR, slots), BF), V((slots, 2*slots), BF), V((PAIR, 2*slots), F32), V((features, slots), BF), V((2, slots, 2*slots), BF), pltpu.SemaphoreType.DMA((2,))],
        compiler_params=pltpu.CompilerParams(vmem_limit_bytes=60*2**20))(*args)

def backward(x, cotangent, qkv, probs, ctxt, normal, root, low, w_qkv, w_out, w_inner, b_inner, w_outer, b_outer, g1, s1, g2, s2):
    out, gi, gu, sums, gf, ga = back1(cotangent, normal, root, low, w_inner, b_inner, w_outer, b_outer, g1, s1, g2, s2)
    tg, gq, go, sums2 = back2(x, qkv, probs, ctxt, gf, ga, w_qkv, w_out)
    return out, tg, gq, go, gi, gu, sums.at[6:8].set(sums2)


def local(
    tokens,
    seg_count,
    seg_align,
    cotangent,
    qkv_weight,
    query_bias,
    value_bias,
    output_weight,
    output_bias,
    first_gain,
    first_shift,
    inner_weight,
    inner_bias,
    outer_weight,
    outer_bias,
    second_gain,
    second_shift,
):
    tokens = lax.all_to_all(tokens, "seq", 0, 1, tiled=True)
    cotangent = lax.all_to_all(cotangent, "seq", 0, 1, tiled=True)
    features = tokens.shape[2]
    document = lax.axis_index("seq")
    seg_count = lax.dynamic_slice_in_dim(seg_count, document, 1, 0)
    seg_align = lax.dynamic_slice_in_dim(seg_align, document, 1, 0)
    row = lambda v: v.reshape(1, -1)
    bias_row = row(jnp.concatenate([query_bias, jnp.zeros_like(query_bias), value_bias]))
    first_gain, first_shift, second_gain, second_shift = map(row, (first_gain, first_shift, second_gain, second_shift))
    tokens, cotangent = tokens[0], cotangent[0]
    qkv, probs, context_t, normal, root, low = forward(
        tokens, seg_align, seg_count, qkv_weight, bias_row, output_weight, row(output_bias), first_gain, first_shift
    )
    block_output, tokens_grad, qkv_weight_grad, output_weight_grad, inner_weight_grad, outer_weight_grad, sums = backward(
        tokens, cotangent, qkv, probs, context_t, normal, root, low, qkv_weight, output_weight,
        inner_weight, row(inner_bias), outer_weight, row(outer_bias), first_gain, first_shift, second_gain, second_shift,
    )
    sums = jnp.sum(sums, axis=1)
    second_gain_grad, second_shift_grad, outer_bias_grad, first_gain_grad = sums[0], sums[1], sums[2], sums[3]
    first_shift_grad, output_bias_grad, query_bias_grad, value_bias_grad = sums[4], sums[5], sums[6], sums[7]
    inner_bias_grad = sums[8:12].reshape(-1)
    vectors = [
        query_bias_grad,
        value_bias_grad,
        output_bias_grad,
        first_gain_grad,
        first_shift_grad,
        outer_bias_grad,
        second_gain_grad,
        second_shift_grad,
        inner_bias_grad,
    ]
    matrices = [outer_weight_grad, inner_weight_grad, output_weight_grad, qkv_weight_grad]
    dp = lax.axis_size("dp")
    if dp == 16 and lax.axis_size("seq") == 2:
        flat = jnp.concatenate(vectors + [jnp.zeros((16 * features - sum(v.size for v in vectors),), jnp.float32)])
        *matrices, sums = sum_over_mesh([m.astype(jnp.bfloat16) for m in matrices], flat.reshape(16, features))
        sums, place, parts = sums.reshape(-1), 0, []
        for vector in vectors:
            share = vector.size // dp
            parts.append(lax.dynamic_slice_in_dim(sums, place + lax.axis_index("dp") * share, share, 0))
            place += vector.size
        vectors = parts
    else:
        matrices, vectors = [
            [
                lax.psum(lax.psum_scatter(v.astype(jnp.float32), "dp", scatter_dimension=0, tiled=True), "seq")
                for v in group
            ]
            for group in (matrices, vectors)
        ]
    summed = (
        matrices[3],
        vectors[0],
        vectors[1],
        matrices[2],
        vectors[2],
        vectors[3],
        vectors[4],
        matrices[1],
        vectors[8],
        matrices[0],
        vectors[5],
        vectors[6],
        vectors[7],
    )
    block_output = lax.all_to_all(block_output[None], "seq", 1, 0, tiled=True)
    tokens_grad = lax.all_to_all(tokens_grad[None], "seq", 1, 0, tiled=True)
    return (
        block_output,
        tokens_grad,
        summed[0],
        summed[1],
        summed[2],
        summed[3],
        summed[4],
        summed[5],
        summed[6],
        summed[7],
        summed[8],
        summed[9],
        summed[10],
        summed[11],
        summed[12],
    )


def solution(mesh):
    return jax.shard_map(
        local,
        mesh=mesh,
        in_specs=(
            P("dp", "seq", None),
            P("dp"),
            P("dp", None),
            P("dp", "seq", None),
            P(),
            P(),
            P(),
            P(),
            P(),
            P(),
            P(),
            P(),
            P(),
            P(),
            P(),
            P(),
            P(),
        ),
        out_specs=(
            P("dp", "seq", None),
            P("dp", "seq", None),
            P("dp", None),
            P("dp"),
            P("dp"),
            P("dp", None),
            P("dp"),
            P("dp"),
            P("dp"),
            P("dp", None),
            P("dp"),
            P("dp", None),
            P("dp"),
            P("dp"),
            P("dp"),
        ),
        check_vma=False,
    )
```

```python
import functools

import jax
import jax.numpy as jnp
from jax import lax
from jax.experimental import pallas as pl
from jax.experimental.pallas import tpu as pltpu
from jax.sharding import PartitionSpec as P

H = 12


LAYOUT_REWARD = 2.0
BLOCKED_SCORE = -1000000000.0
NORM_EPS = 1e-05
LOG2E = 1.4426950408889634
HEAD = 64
PAIR = 128
WIDE = 256
BF, F32 = jnp.bfloat16, jnp.float32


def dot(left, right):
    return jnp.dot(left, right, preferred_element_type=F32)


def dot_nt(left, right):
    return lax.dot_general(left, right, (((1,), (1,)), ((), ())), preferred_element_type=F32)


def dot_tn(left, right):
    return lax.dot_general(left, right, (((0,), (0,)), ((), ())), preferred_element_type=F32)


def at(start, size):
    return pl.ds(pl.multiple_of(start, size), size)


def loop(count, body):
    def step(index, carry):
        body(index)
        return carry

    lax.fori_loop(0, count, step, 0)


def fold_rows(block):
    rows, columns = block.shape
    return jnp.sum(block.reshape(rows // 8, 8, columns), axis=0)


def project_tokens(x, w_qkv, bias_row, qkv, rows):
    columns = w_qkv.shape[1]

    def body(index):
        here = at(index * WIDE, WIDE)
        qkv[rows, here] = (dot(x[rows, :], w_qkv[:, here]) + bias_row[0:1, here]).astype(BF)

    loop(columns // WIDE, body)


def fill_reward(reward, seg_row, count):
    text = seg_row.shape[1]
    segs = reward.shape[0] - text
    key = lax.broadcasted_iota(jnp.int32, (segs, text), 0)
    match = jnp.where(key == seg_row, LAYOUT_REWARD * LOG2E, 0.0).astype(F32)
    dead = jnp.where(key >= count, BLOCKED_SCORE * LOG2E, 0.0).astype(F32)
    turned = jnp.transpose(match)
    reward[...] = jnp.zeros_like(reward)
    slots = text + segs
    for head in range(2):
        reward[text:slots, head * slots : head * slots + text] = match + dead
        reward[text:slots, head * slots + text : (head + 1) * slots] = dead[:, :segs]
        reward[0:text, head * slots + text : (head + 1) * slots] = turned


def split_heads(block, both):
    slots = block.shape[0]
    first = lax.broadcasted_iota(jnp.int32, block.shape, 1) < HEAD
    zero = jnp.zeros_like(block)
    both[0:slots, :] = jnp.where(first, block, zero)
    both[slots:, :] = jnp.where(first, zero, block)


def attend(qkv, reward, probs_of, context_t, both, turned, side):
    slots, features = qkv.shape[0], qkv.shape[1] // 3
    pairs = features // PAIR
    scaling = HEAD ** (-0.5) * LOG2E

    def pair_step(pair):
        here = at(pair * PAIR, PAIR)
        keys = qkv[:, at(features + pair * PAIR, PAIR)]
        split_heads(qkv[:, here], both)
        turned[...] = jnp.transpose(qkv[:, at(2 * features + pair * PAIR, PAIR)])
        probs = probs_of(pair)

        for chunk in range(2 * slots // WIDE):
            block = slice(chunk * WIDE, (chunk + 1) * WIDE)
            scores = dot_nt(keys, both[block, :]) * scaling + reward[:, block]
            scores = jnp.exp2(scores - jnp.max(scores, axis=0, keepdims=True))
            low = (scores * (1.0 / jnp.sum(scores, axis=0, keepdims=True))).astype(BF)
            probs[:, block] = low
            side[:, block] = dot(turned[...], low).astype(BF)
        context_t[at(pair * PAIR, HEAD), :] = side[:HEAD, :slots]
        context_t[at(pair * PAIR + HEAD, HEAD), :] = side[HEAD:, slots:]

    return pair_step, pairs


def first_norm(x, attended, bias, gain, shift, normal, root, low, rows):
    def body(index):
        here = at(index * rows, rows)
        hidden = x[here, :].astype(F32) + (attended[here, :] + bias[...])
        centre = hidden - jnp.mean(hidden, axis=1, keepdims=True)
        inverse = lax.rsqrt(jnp.mean(centre * centre, axis=1, keepdims=True) + NORM_EPS)
        unit = centre * inverse
        normal[here, :] = unit
        root[here, :] = jnp.broadcast_to(inverse, (rows, PAIR))
        low[here, :] = (unit * gain[...] + shift[...]).astype(BF)

    loop(x.shape[0] // rows, body)


def gate(inner):
    normal = 0.5 * (1.0 + lax.erf(inner * 0.7071067811865476))
    density = jnp.exp2(inner * inner * (-0.5 * LOG2E)) * 0.3989422804014327
    return inner * normal, normal + inner * density


def feed_forward(low, w_inner, b_inner, hidden, slope):
    def body(index):
        here = at(index * WIDE, WIDE)
        value, grade = gate(dot(low[...], w_inner[:, here]) + b_inner[0:1, here])
        hidden[:, here] = value.astype(BF)
        slope[:, here] = grade.astype(BF)

    loop(w_inner.shape[1] // WIDE, body)


def second_norm(normal, first_gain, first_shift, mlp, bias, gain, shift, cotangent, output, grad, grad_low, sums, rows):
    sums[0:3] = jnp.zeros((3,) + sums.shape[1:], F32)

    def body(index):
        here = at(index * rows, rows)
        one = normal[here, :] * first_gain[...] + first_shift[...]
        total = one + (mlp[here, :] + bias[...])
        centre = total - jnp.mean(total, axis=1, keepdims=True)
        inverse = lax.rsqrt(jnp.mean(centre * centre, axis=1, keepdims=True) + NORM_EPS)
        unit = centre * inverse
        pull = cotangent[here, :].astype(F32)
        output[here, :] = (unit * gain[...] + shift[...]).astype(BF)
        scaled = pull * gain[...]
        back = inverse * (
            scaled
            - jnp.mean(scaled, axis=1, keepdims=True)
            - unit * jnp.mean(scaled * unit, axis=1, keepdims=True)
        )
        rounded = back.astype(BF)
        grad[here, :] = back
        grad_low[here, :] = rounded
        sums[0] += fold_rows(pull * unit)
        sums[1] += fold_rows(pull)
        sums[2] += fold_rows(rounded.astype(F32))

    loop(normal.shape[0] // rows, body)


def first_norm_back(grad_second, back, normal, root, gain, grad_first, grad_low, sums, rows):
    sums[3:6] = jnp.zeros((3,) + sums.shape[1:], F32)

    def body(index):
        here = at(index * rows, rows)
        pull = grad_second[here, :] + back[here, :]
        unit = normal[here, :]
        scaled = pull * gain[...]
        inverse = root[here, 0:1]
        first = inverse * (
            scaled
            - jnp.mean(scaled, axis=1, keepdims=True)
            - unit * jnp.mean(scaled * unit, axis=1, keepdims=True)
        )
        rounded = first.astype(BF)
        grad_first[here, :] = first
        grad_low[here, :] = rounded
        sums[3] += fold_rows(pull * unit)
        sums[4] += fold_rows(pull)
        sums[5] += fold_rows(rounded.astype(F32))

    loop(normal.shape[0] // rows, body)


def attend_back(qkv, grad_context, probs_of, grad_qkv, both, both_grad, turned, scores, side, points):
    slots, features = qkv.shape[0], qkv.shape[1] // 3
    scaling = HEAD ** (-0.5)

    def pair_step(pair):
        here = at(pair * PAIR, PAIR)
        there = at(features + pair * PAIR, PAIR)
        last = at(2 * features + pair * PAIR, PAIR)
        split_heads(qkv[:, here], both)
        split_heads(grad_context[:, here], both_grad)
        turned[...] = jnp.transpose(qkv[:, there])
        values = qkv[:, last]
        probs = probs_of(pair)
        for chunk in range(2 * slots // WIDE):
            block = slice(chunk * WIDE, (chunk + 1) * WIDE)
            pull = dot_nt(values, both_grad[block, :])
            weight = probs[:, block].astype(F32)
            mean = jnp.sum(weight * pull, axis=0, keepdims=True)
            low = (weight * (pull - mean)).astype(BF)
            scores[:, block] = low
            side[:, block] = dot(turned[...], low)
            if chunk == 2:
                points("u", pair)
        points("v", pair)
        grad_qkv[:, there] = (dot(scores[...], both[...]) * scaling).astype(BF)
        grad_qkv[:, last] = dot(probs[...], both_grad[...]).astype(BF)
        mine = jnp.concatenate([side[:HEAD, :slots], side[HEAD:, slots:]], axis=0)
        grad_qkv[:, here] = jnp.transpose(mine * scaling).astype(BF)

    return pair_step, features // PAIR


PARTS = 16
MESH = pl.DeviceIdType.MESH
UNIT_ROWS = 48
UNITS = 12
WEIGHT = {"c": 1, "y": 2, "l": 4, "h": 8}
ORDERS = ("cyxlhg", "clyhxg")
SMALL_ORDER = "cylhx"
SWAP = 0


def partner_of(bit, me, seq):
    if bit in "xg":
        return (me, 1 - seq)
    weight = WEIGHT[bit]
    return (me + weight * (1 - 2 * ((me // weight) % 2)), seq)


def stage_shapes(order, rows, columns):
    bits, shapes = 4, []
    for bit in order:
        if bit == "x":
            columns //= 2
        elif bit != "g":
            bits -= 1
        shapes.append((2,) * bits + (rows, columns))
    return shapes


def add_into(target, other):
    lead = target.shape[:-2]
    total = 1
    for size in lead:
        total *= size

    def step(index, carry):
        place, rest = [], index
        for size in reversed(lead):
            place.append(rest % size)
            rest = rest // size
        place = tuple(reversed(place)) + (slice(None), slice(None))
        target[place] = (target[place].astype(F32) + other[place].astype(F32)).astype(BF)
        return carry

    if total == 1:
        step(0, 0)
    else:
        lax.fori_loop(0, total, step, 0)


class Unit:
    def __init__(self, number, source, order, buffers, sends, recvs, me, seq):
        self.number, self.source, self.order, self.buffers = number, source, order, buffers
        self.sends, self.recvs, self.me, self.seq = sends, recvs, me, seq

    def at_stage(self, stage):
        bits = ["h", "l", "y", "c"]
        for bit in self.order[:stage]:
            if bit in bits:
                bits.remove(bit)
        current = self.buffers[stage - 1] if stage else self.source
        bit = self.order[stage]
        if bit == "g":
            return current, None
        if bit == "x":
            size = current.shape[-1] // 2
            lead = (slice(None),) * (len(bits) + 1)
            own = current.at[lead + (pl.ds(pl.multiple_of(self.seq * size, PAIR), size),)]
            return current.at[lead + (pl.ds(pl.multiple_of((1 - self.seq) * size, PAIR), size),)], own
        mine = (self.me // WEIGHT[bit]) % 2
        lead = (slice(None),) * bits.index(bit)
        return current.at[lead + (1 - mine,)], current.at[lead + (mine,)]

    def copy(self, stage):
        return pltpu.make_async_remote_copy(
            src_ref=self.at_stage(stage)[0],
            dst_ref=self.buffers[stage],
            send_sem=self.sends.at[self.number, stage],
            recv_sem=self.recvs.at[self.number, stage],
            device_id=partner_of(self.order[stage], self.me, self.seq),
            device_id_type=MESH,
        )

    def advance(self, stage):
        self.copy(stage).wait()
        self.add(stage)

    def add(self, stage):
        kept = self.at_stage(stage)[1]
        if kept is not None:
            add_into(self.buffers[stage], kept)
        if stage + 1 < len(self.order):
            self.copy(stage + 1).start()


def with_stages(schedule):
    reached = [0] * (UNITS + 1)
    plan = {}
    for point, numbers in schedule:
        steps = plan.setdefault(point, [])
        for number in numbers:
            steps.append((number, reached[number]))
            reached[number] += 1
    return plan


def layer_kernel(
    tokens, cotangent, seg_align, seg_count, vectors, w_qkv, w_out, w_inner, w_outer,
    block_output, tokens_grad, g_qkv, g_out, g_inner, g_outer, sums_out, probs_hbm,
    x, qkv, context_t, w_out_v, normal, root, cot, acc, grad_att, sums, own, small, small_got, *rest,
):
    rest = list(rest)
    buffers = [[rest.pop(0) for _ in ORDERS[0]] for _ in range(UNITS)]
    unit_send, unit_recv, outer_send, outer_recv, local_sem, pair_sem, swap_send, swap_recv, small_send, small_recv = rest
    slots, features = x.shape
    half = slots // 2
    wide = w_inner.shape[1]
    me, seq = lax.axis_index("dp"), lax.axis_index("seq")
    core = me % 2
    mine, other = at(seq * half, half), at((1 - seq) * half, half)
    b_out, gain1, shift1, b_outer, gain2, shift2 = (vectors.at[i : i + 1] for i in range(3, 9))
    columns = [slice(c * WIDE, (c + 1) * WIDE) for c in range(features // WIDE)]

    barrier = pltpu.get_barrier_semaphore()
    for bit in "xcylh":
        pl.semaphore_signal(barrier, inc=1, device_id=partner_of(bit, me, seq), device_id_type=MESH)

    def local(source, target, index):
        return pltpu.make_async_copy(source, target, local_sem.at[index])

    def swap(source, target, index):
        return pltpu.make_async_remote_copy(
            src_ref=source, dst_ref=target, send_sem=swap_send.at[index], recv_sem=swap_recv.at[index],
            device_id=(me, 1 - seq), device_id_type=MESH)

    keep_tokens = local(tokens.at[seq], x.at[mine], 0)
    keep_cot = local(cotangent.at[seq], cot.at[mine], 1)
    load_out = local(w_out, w_out_v, 2)
    swap_tokens = swap(tokens.at[1 - seq], x.at[mine], 0)
    swap_cot = swap(cotangent.at[1 - seq], cot.at[mine], 1)
    keep_output = local(cot.at[mine], block_output.at[seq], 3)
    swap_output = swap(cot.at[other], block_output.at[seq], 2)
    keep_grad = local(x.at[mine], tokens_grad.at[seq], 4)
    swap_grad = swap(x.at[other], tokens_grad.at[seq], 3)
    keep_tokens.start()

    units = [
        Unit(n, own.at[n if n < 8 else n - 8], ORDERS[n % 2], buffers[n], unit_send, unit_recv, me, seq)
        for n in range(UNITS)
    ]

    def outer_copy(j, sub):
        hi, lo = j // 2, j % 2
        return pltpu.make_async_remote_copy(
            src_ref=own.at[sub, hi, lo, :, 1 - core],
            dst_ref=buffers[sub][0].at[hi, lo],
            send_sem=outer_send.at[j, sub], recv_sem=outer_recv.at[j, sub],
            device_id=partner_of("c", me, seq), device_id_type=MESH)

    def small_copy(stage):
        return pltpu.make_async_remote_copy(
            src_ref=small, dst_ref=small_got.at[stage], send_sem=small_send.at[stage], recv_sem=small_recv.at[stage],
            device_id=partner_of(SMALL_ORDER[stage], me, seq), device_id_type=MESH)

    def advance(number, stage):
        if number == UNITS:
            small_copy(stage).wait()
            small[...] += small_got[stage]
            if stage + 1 < len(SMALL_ORDER):
                small_copy(stage + 1).start()
        elif number < 4 and stage == 0:
            for j in range(4):
                outer_copy(j, number).wait()
            units[number].add(0)
        else:
            units[number].advance(stage)

    plan = with_stages(SCHEDULE)

    def point(name):
        for number, stage in plan.get(name, ()):
            advance(number, stage)

    def points(name, index, count):
        for i in range(count):
            if (name, i) in plan:
                pl.when(index == i)(functools.partial(point, (name, i)))

    def forward(w_inner_v, w_outer_v):
        load_inner, load_outer = local(w_inner, w_inner_v, 5), local(w_outer, w_outer_v, 6)

        def attention(w_qkv_v, reward, both, turned, side, probs_buf):
            load_qkv = local(w_qkv, w_qkv_v, 7)
            load_qkv.start()
            pl.semaphore_wait(barrier, 5)
            swap_tokens.start()
            load_out.start()
            fill_reward(reward, seg_align[pl.ds(seq, 1), :], seg_count[seq])
            keep_tokens.wait()
            load_qkv.wait()

            def project(rows):
                def body(index):
                    here = at(index * WIDE, WIDE)
                    bias = vectors[pl.ds(index // 3, 1), at(index % 3 * WIDE, WIDE)]
                    qkv[rows, here] = (dot(x[rows, :], w_qkv_v[:, here]) + bias).astype(BF)

                loop(3 * features // WIDE, body)

            project(mine)
            load_inner.start()
            load_outer.start()
            keep_cot.start()
            swap_tokens.wait()
            swap_cot.start()
            project(other)
            step, pairs = attend(qkv, reward, lambda pair: probs_buf.at[pair % 2], context_t, both, turned, side)

            def out_copy(pair):
                return pltpu.make_async_copy(probs_buf.at[pair % 2], probs_hbm.at[pair], pair_sem.at[pair % 2])

            def body(pair):
                @pl.when(pair >= 2)
                def _():
                    out_copy(pair - 2).wait()

                step(pair)
                out_copy(pair).start()

            loop(pairs, body)
            out_copy(pairs - 2).wait()
            out_copy(pairs - 1).wait()

        pl.run_scoped(
            attention,
            pltpu.VMEM((features, 3 * features), BF),
            pltpu.VMEM((slots, 2 * slots), F32),
            pltpu.VMEM((2 * slots, PAIR), BF),
            pltpu.VMEM((PAIR, slots), BF),
            pltpu.VMEM((PAIR, 2 * slots), BF),
            pltpu.VMEM((2, slots, 2 * slots), BF),
        )

        def mlp(low, turned_low, hidden, slope, grad_second):
            low[...] = jnp.transpose(context_t[...])
            load_out.wait()
            for here in columns:
                acc[:, here] = dot(low[...], w_out_v[:, here])
            first_norm(x, acc, b_out, gain1, shift1, normal, root, low, 32)
            load_inner.wait()

            def inner_body(index):
                here = at(index * WIDE, WIDE)
                bias = vectors[pl.ds(9 + index // 3, 1), at(index % 3 * WIDE, WIDE)]
                value, grade = gate(dot(low[...], w_inner_v[:, here]) + bias)
                hidden[:, here] = value.astype(BF)
                slope[:, here] = grade.astype(BF)

            loop(wide // WIDE, inner_body)
            load_outer.wait()
            for here in columns:
                acc[:, here] = dot(hidden[...], w_outer_v[:, here])
            keep_cot.wait()
            swap_cot.wait()
            second_norm(normal, gain1, shift1, acc, b_outer, gain2, shift2, cot, cot, grad_second, grad_att, sums, 32)
            keep_output.start()
            swap_output.start()
            turned_low[...] = jnp.transpose(low[...])

            def outer_step(j):
                block = dot_tn(hidden[:, at(j * features, features)], grad_att[...]).astype(BF)
                block = block.reshape(2, 2, 4, UNIT_ROWS, features)
                for sub in range(4):
                    own[sub, j // 2, j % 2] = block[:, :, sub]
                for sub in range(4):
                    outer_copy(j, sub).start()

            loop(4, outer_step)

            def inner_step(j):
                here = at(j * features, features)
                low_grad = (
                    dot_nt(grad_att[...], w_outer_v[here, :]) * slope[:, here].astype(F32)
                ).astype(BF)
                hidden[:, here] = low_grad
                sums[8 + j] = fold_rows(low_grad.astype(F32))
                points("g", j, 4)
                block = dot(turned_low[...], hidden[:, here]).astype(BF)
                own[4 + j] = block.reshape(2, 2, 2, 2, UNIT_ROWS, features)
                for i in range(4):
                    pl.when(j == i)(lambda i=i: units[4 + i].copy(0).start())
                points("i", j, 4)

            loop(4, inner_step)
            for c, here in enumerate(columns):
                acc[:, here] = dot_nt(hidden[...], w_inner_v[here, :])
                point(("a", c))
            first_norm_back(grad_second, acc, normal, root, gain1, acc, grad_att, sums, 32)

        pl.run_scoped(
            mlp,
            pltpu.VMEM((slots, features), BF),
            pltpu.VMEM((features, slots), BF),
            pltpu.VMEM((slots, wide), BF),
            pltpu.VMEM((slots, wide), BF),
            pltpu.VMEM((slots, features), F32),
        )

    pl.run_scoped(forward, pltpu.VMEM(w_inner.shape, BF), pltpu.VMEM(w_outer.shape, BF))

    def back(w_qkv_v, both, both_grad, turned, scores, side, probs_buf, grad_ctx, grad_qkv, turned_x):
        load_qkv = local(w_qkv, w_qkv_v, 8)
        load_qkv.start()

        def in_copy(pair):
            return pltpu.make_async_copy(probs_hbm.at[pair], probs_buf.at[pair % 2], pair_sem.at[pair % 2])

        in_copy(0).start()
        point(("n", 0))
        for c, here in enumerate(columns):
            block = dot(context_t[...], grad_att[:, here]).astype(BF)
            own[0, :, :, :, :, :, here] = block.reshape(2, 2, 2, 2, UNIT_ROWS, WIDE)
        units[8].copy(0).start()
        point(("o", 0))
        for c, here in enumerate(columns):
            grad_ctx[:, here] = dot_nt(grad_att[...], w_out_v[here, :]).astype(BF)
        turned_x[...] = jnp.transpose(x[...])
        point(("o", 1))
        step, pairs = attend_back(
            qkv, grad_ctx, lambda pair: probs_buf.at[pair % 2], grad_qkv, both, both_grad, turned, scores, side,
            lambda name, pair: points(name, pair, pairs))

        def body(pair):
            @pl.when(pair + 1 < pairs)
            def _():
                in_copy(pair + 1).start()

            in_copy(pair).wait()
            step(pair)
            points("r", pair, pairs)

            @pl.when(pair % 2 == 1)
            def _():
                group = pair // 2
                for part in range(3):
                    there = at(part * features + group * WIDE, WIDE)
                    block = dot(turned_x[...], grad_qkv[:, there]).astype(BF)
                    own[1 + group, :, :, :, :, :, part * WIDE : (part + 1) * WIDE] = block.reshape(
                        2, 2, 2, 2, UNIT_ROWS, WIDE)
                for i in range(3):
                    pl.when(group == i)(lambda i=i: units[9 + i].copy(0).start())

            points("s", pair, pairs)

        loop(pairs, body)
        sums[6] = fold_rows(grad_qkv[:, :features].astype(F32))
        sums[7] = fold_rows(grad_qkv[:, 2 * features :].astype(F32))
        small[...] = jnp.sum(sums[...], axis=1)
        small_copy(0).start()
        load_qkv.wait()
        for side_index, rows in enumerate((other, mine)):
            for c, here in enumerate(columns):
                x[rows, here] = (acc[rows, here] + dot_nt(grad_qkv[rows, :], w_qkv_v[here, :])).astype(BF)
                point(("t", side_index * 3 + c))
            (swap_grad if side_index == 0 else keep_grad).start()

    pl.run_scoped(
        back,
        pltpu.VMEM((features, 3 * features), BF),
        pltpu.VMEM((2 * slots, PAIR), BF),
        pltpu.VMEM((2 * slots, PAIR), BF),
        pltpu.VMEM((PAIR, slots), BF),
        pltpu.VMEM((slots, 2 * slots), BF),
        pltpu.VMEM((PAIR, 2 * slots), F32),
        pltpu.VMEM((2, slots, 2 * slots), BF),
        pltpu.VMEM((slots, features), BF),
        pltpu.VMEM((slots, 3 * features), BF),
        pltpu.VMEM((features, slots), BF),
    )
    point(("end", 0))
    keep_output.wait()
    swap_output.wait()
    keep_grad.wait()
    swap_grad.wait()
    sums_out[...] = small[...]
    size = features // 2
    for number in range(UNITS):
        kept, got = (buffers[number][stage] for stage in (4, 5))
        for side in range(2):

            @pl.when(seq == side)
            def _():
                for block, place in ((kept, side), (got, 1 - side)):
                    value = block[...].astype(F32)
                    start = place * size
                    if number < 4:
                        g_outer[number * UNIT_ROWS : (number + 1) * UNIT_ROWS, start : start + size] = value
                    elif number < 8:
                        start += (number - 4) * features
                        g_inner[:, start : start + size] = value
                    elif number == 8:
                        g_out[:, start : start + size] = value
                    else:
                        for piece in range(size // PAIR):
                            column = start + piece * PAIR
                            target = column // WIDE * features + (number - 9) * WIDE + column % WIDE
                            g_qkv[:, target : target + PAIR] = value[:, piece * PAIR : (piece + 1) * PAIR]


def layer(tokens, cotangent, seg_align, seg_count, vectors, w_qkv, w_out, w_inner, w_outer):
    documents, half, features = tokens.shape
    slots, wide = 2 * half, w_inner.shape[1]
    pairs = features // PAIR
    S, V, D = jax.ShapeDtypeStruct, pltpu.VMEM, pltpu.SemaphoreType.DMA
    scratch = [
        V((slots, features), BF), V((slots, 3 * features), BF), V((features, slots), BF), V(w_out.shape, BF),
        V((slots, features), F32), V((slots, PAIR), F32), V((slots, features), BF), V((slots, features), F32),
        V((slots, features), BF), V((16, 8, features), F32), V((8, 2, 2, 2, 2, UNIT_ROWS, features), BF),
        V((16, features), F32), V((len(SMALL_ORDER), 16, features), F32),
    ]
    for number in range(UNITS):
        scratch += [V(shape, BF) for shape in stage_shapes(ORDERS[number % 2], UNIT_ROWS, features)]
    scratch += [D((UNITS, 6)), D((UNITS, 6)), D((4, 4)), D((4, 4)), D((9,)), D((2,)), D((4,)), D((4,)), D((5,)), D((5,))]
    hbm, vmem = pl.BlockSpec(memory_space=pltpu.HBM), pl.BlockSpec(memory_space=pltpu.VMEM)
    return pl.pallas_call(
        layer_kernel,
        name="layer",
        out_shape=[
            S(tokens.shape, BF), S(tokens.shape, BF), S((UNIT_ROWS, 3 * features), F32), S((UNIT_ROWS, features), F32),
            S((UNIT_ROWS, wide), F32), S((4 * UNIT_ROWS, features), F32), S((16, features), F32),
            S((pairs, slots, 2 * slots), BF),
        ],
        in_specs=[hbm, hbm, vmem, pl.BlockSpec(memory_space=pltpu.SMEM), vmem, hbm, hbm, hbm, hbm],
        out_specs=[hbm, hbm, vmem, vmem, vmem, vmem, vmem, hbm],
        scratch_shapes=scratch,
        compiler_params=pltpu.CompilerParams(collective_id=0, has_side_effects=True, vmem_limit_bytes=60 * 2**20),
    )(tokens, cotangent, seg_align, seg_count, vectors, w_qkv, w_out, w_inner, w_outer)


SCHEDULE = (
    (("i", 1), (0,)),
    (("g", 2), (1,)),
    (("i", 2), (2,)),
    (("g", 3), (3,)),
    (("i", 3), (4,)),
    (("a", 0), (5,)),
    (("a", 1), (0, 6)),
    (("a", 2), (1, 7)),
    (("n", 0), (2,)),
    (("o", 0), (0,)),
    (("o", 1), (3,)),
    (("v", 0), (8, 4, 2)),
    (("r", 0), (5,)),
    (("s", 1), (6, 4)),
    (("u", 2), (7,)),
    (("v", 2), (1, 0)),
    (("r", 2), (2,)),
    (("u", 3), (9, 3, 4, 6)),
    (("s", 3), (1,)),
    (("u", 4), (0, 8)),
    (("v", 4), (2,)),
    (("r", 4), (1,)),
    (("u", 5), (10, 5, 0)),
    (("r", 5), (9, 7, 8)),
    (("s", 5), (2, 1)),
    (("t", 0), (3,)),
    (("t", 2), (4,)),
    (("t", 4), (6,)),
    (("end", 0), (11, 12, 3, 10, 4, 5, 9, 12, 7, 8, 6, 11, 3, 12, 9, 10, 8, 5, 11, 7, 12, 6, 9, 10, 8, 5, 7, 12, 11, 9, 10, 11, 10, 11)),
)


def slot_groups(seg_count, seg_align, all_slots):
    doc_count, text_slots = seg_align.shape
    slot_index = jnp.arange(all_slots, dtype=jnp.int32)
    filler = jnp.zeros((doc_count, all_slots - text_slots), jnp.int32)
    padded = jnp.concatenate([seg_align, filler], axis=1)
    is_text = slot_index < text_slots
    groups = jnp.where(is_text[None, :], padded, (slot_index - text_slots)[None, :])
    present_keys = slot_index[None, :] < text_slots + seg_count[:, None]
    return (groups, is_text, present_keys)


def layer_norm(hidden, gain, shift):
    centre = hidden - jnp.mean(hidden, axis=-1, keepdims=True)
    spread = jnp.mean(centre * centre, axis=-1, keepdims=True)
    return centre * lax.rsqrt(spread + NORM_EPS) * gain + shift


def smooth_gate(inner):
    return jax.nn.gelu(inner, approximate=False)


def softmax_rows(logit_scores):
    return jax.nn.softmax(logit_scores, axis=-1)


def project(tokens, qkv_weight, query_bias, value_bias):
    doc_count, slot_count, features = tokens.shape
    token_rows = tokens.reshape(doc_count * slot_count, features)
    pre = jnp.dot(token_rows, qkv_weight, preferred_element_type=jnp.float32)
    queries = (pre[:, :features] + query_bias).astype(jnp.bfloat16)
    own_keys = (
        pre[:, features : 2 * features]
        .astype(jnp.bfloat16)
        .reshape(doc_count, slot_count, features)
    )
    own_values = (
        (pre[:, 2 * features :] + value_bias)
        .astype(jnp.bfloat16)
        .reshape(doc_count, slot_count, features)
    )
    all_keys, values = (
        lax.all_gather(own_keys, "seq", axis=1, tiled=True),
        lax.all_gather(own_values, "seq", axis=1, tiled=True),
    )
    return (queries, all_keys, values)


def plain(
    tokens,
    seg_count,
    seg_align,
    cotangent,
    qkv_weight,
    query_bias,
    value_bias,
    output_weight,
    output_bias,
    first_gain,
    first_shift,
    inner_weight,
    inner_bias,
    outer_weight,
    outer_bias,
    second_gain,
    second_shift,
):
    doc_count, slot_count, features = tokens.shape
    row_count = doc_count * slot_count
    head_dim = features // H
    scaling = head_dim ** (-0.5)
    all_slots = slot_count * lax.axis_size("seq")
    row_start = lax.axis_index("seq") * slot_count
    groups, is_text, present_keys = slot_groups(seg_count, seg_align, all_slots)
    group_rows = lax.dynamic_slice_in_dim(groups, row_start, slot_count, 1)
    text_rows = lax.dynamic_slice_in_dim(is_text, row_start, slot_count, 0)
    matched_pairs = (group_rows[:, :, None] == groups[:, None, :]) & (
        text_rows[None, :, None] != is_text[None, None, :]
    )
    layout_reward = LAYOUT_REWARD * matched_pairs.astype(jnp.float32)
    queries, all_keys, values = project(tokens, qkv_weight, query_bias, value_bias)
    query_heads = queries.reshape(doc_count, slot_count, H, head_dim)
    key_heads = all_keys.reshape(doc_count, all_slots, H, head_dim)
    value_heads = values.reshape(doc_count, all_slots, H, head_dim)
    unadjusted_scores = (
        jnp.einsum("bqhd,bkhd->bhqk", query_heads, key_heads, preferred_element_type=jnp.float32)
        * scaling
    )
    logit_scores = jnp.where(
        present_keys[:, None, None, :], unadjusted_scores + layout_reward[:, None], BLOCKED_SCORE
    )
    attn_probs, soft_pull = jax.vjp(softmax_rows, logit_scores)
    probs_low = attn_probs.astype(jnp.bfloat16)
    context = jnp.einsum(
        "bhqk,bkhd->bqhd", probs_low, value_heads, preferred_element_type=jnp.float32
    )
    context = context.reshape(row_count, features).astype(jnp.bfloat16)
    token_rows = tokens.reshape(row_count, features)
    attended = jnp.dot(context, output_weight, preferred_element_type=jnp.float32) + output_bias
    normed_one, first_pull = jax.vjp(
        layer_norm, token_rows.astype(jnp.float32) + attended, first_gain, first_shift
    )
    normed_low = normed_one.astype(jnp.bfloat16)
    inner = jnp.dot(normed_low, inner_weight, preferred_element_type=jnp.float32) + inner_bias
    activated, gate_pull = jax.vjp(smooth_gate, inner)
    hidden = activated.astype(jnp.bfloat16)
    mlp_out = jnp.dot(hidden, outer_weight, preferred_element_type=jnp.float32) + outer_bias
    layer_out, second_pull = jax.vjp(layer_norm, normed_one + mlp_out, second_gain, second_shift)
    grad_out = cotangent.reshape(row_count, features).astype(jnp.float32)
    grad_second, second_gain_grad, second_shift_grad = second_pull(grad_out)
    grad_mlp = grad_second.astype(jnp.bfloat16)
    outer_weight_grad = jnp.einsum(
        "rf,rd->fd", hidden, grad_mlp, preferred_element_type=jnp.float32
    )
    outer_bias_grad = jnp.sum(grad_mlp.astype(jnp.float32), axis=0)
    grad_hidden = jnp.einsum(
        "rd,fd->rf", grad_mlp, outer_weight, preferred_element_type=jnp.float32
    )
    grad_inner = gate_pull(grad_hidden)[0].astype(jnp.bfloat16)
    inner_weight_grad = jnp.einsum(
        "rd,rf->df", normed_low, grad_inner, preferred_element_type=jnp.float32
    )
    inner_bias_grad = jnp.sum(grad_inner.astype(jnp.float32), axis=0)
    grad_normed = grad_second + jnp.einsum(
        "rf,df->rd", grad_inner, inner_weight, preferred_element_type=jnp.float32
    )
    grad_first, first_gain_grad, first_shift_grad = first_pull(grad_normed)
    grad_attended = grad_first.astype(jnp.bfloat16)
    output_weight_grad = jnp.einsum(
        "rc,rd->cd", context, grad_attended, preferred_element_type=jnp.float32
    )
    output_bias_grad = jnp.sum(grad_attended.astype(jnp.float32), axis=0)
    grad_context = jnp.einsum(
        "rd,cd->rc", grad_attended, output_weight, preferred_element_type=jnp.float32
    )
    grad_context = grad_context.astype(jnp.bfloat16).reshape(doc_count, slot_count, H, head_dim)
    grad_probs = jnp.einsum(
        "bqhd,bkhd->bhqk", grad_context, value_heads, preferred_element_type=jnp.float32
    )
    grad_scores = soft_pull(grad_probs)[0].astype(jnp.bfloat16)
    grad_queries = (
        jnp.einsum("bhqk,bkhd->bqhd", grad_scores, key_heads, preferred_element_type=jnp.float32)
        * scaling
    )
    grad_queries = grad_queries.astype(jnp.bfloat16).reshape(row_count, features)
    key_term = (
        jnp.einsum("bhqk,bqhd->bkhd", grad_scores, query_heads, preferred_element_type=jnp.float32)
        * scaling
    )
    value_term = jnp.einsum(
        "bhqk,bqhd->bkhd", probs_low, grad_context, preferred_element_type=jnp.float32
    )
    key_sum, value_sum = (
        lax.psum_scatter(
            key_term.reshape(doc_count, all_slots, features).astype(jnp.bfloat16),
            "seq",
            scatter_dimension=1,
            tiled=True,
        ).astype(jnp.float32),
        lax.psum_scatter(
            value_term.reshape(doc_count, all_slots, features).astype(jnp.bfloat16),
            "seq",
            scatter_dimension=1,
            tiled=True,
        ).astype(jnp.float32),
    )
    grad_keys = key_sum.astype(jnp.bfloat16).reshape(row_count, features)
    grad_values = value_sum.astype(jnp.bfloat16).reshape(row_count, features)
    grad_project = jnp.concatenate([grad_queries, grad_keys, grad_values], axis=1)
    qkv_weight_grad = jnp.einsum(
        "rd,re->de", token_rows, grad_project, preferred_element_type=jnp.float32
    )
    query_bias_grad = jnp.sum(grad_queries.astype(jnp.float32), axis=0)
    value_bias_grad = jnp.sum(grad_values.astype(jnp.float32), axis=0)
    tokens_grad = grad_first + jnp.einsum(
        "re,de->rd", grad_project, qkv_weight, preferred_element_type=jnp.float32
    )
    tokens_grad = tokens_grad.astype(jnp.bfloat16).reshape(doc_count, slot_count, features)
    shares = (
        lax.psum_scatter(qkv_weight_grad, "dp", scatter_dimension=0, tiled=True),
        lax.psum_scatter(query_bias_grad, "dp", scatter_dimension=0, tiled=True),
        lax.psum_scatter(value_bias_grad, "dp", scatter_dimension=0, tiled=True),
        lax.psum_scatter(output_weight_grad, "dp", scatter_dimension=0, tiled=True),
        lax.psum_scatter(output_bias_grad, "dp", scatter_dimension=0, tiled=True),
        lax.psum_scatter(first_gain_grad, "dp", scatter_dimension=0, tiled=True),
        lax.psum_scatter(first_shift_grad, "dp", scatter_dimension=0, tiled=True),
        lax.psum_scatter(inner_weight_grad, "dp", scatter_dimension=0, tiled=True),
        lax.psum_scatter(inner_bias_grad, "dp", scatter_dimension=0, tiled=True),
        lax.psum_scatter(outer_weight_grad, "dp", scatter_dimension=0, tiled=True),
        lax.psum_scatter(outer_bias_grad, "dp", scatter_dimension=0, tiled=True),
        lax.psum_scatter(second_gain_grad, "dp", scatter_dimension=0, tiled=True),
        lax.psum_scatter(second_shift_grad, "dp", scatter_dimension=0, tiled=True),
    )
    summed = (
        lax.psum(shares[0].astype(jnp.bfloat16), "seq").astype(jnp.float32),
        lax.psum(shares[1].astype(jnp.bfloat16), "seq").astype(jnp.float32),
        lax.psum(shares[2].astype(jnp.bfloat16), "seq").astype(jnp.float32),
        lax.psum(shares[3].astype(jnp.bfloat16), "seq").astype(jnp.float32),
        lax.psum(shares[4].astype(jnp.bfloat16), "seq").astype(jnp.float32),
        lax.psum(shares[5].astype(jnp.bfloat16), "seq").astype(jnp.float32),
        lax.psum(shares[6].astype(jnp.bfloat16), "seq").astype(jnp.float32),
        lax.psum(shares[7].astype(jnp.bfloat16), "seq").astype(jnp.float32),
        lax.psum(shares[8].astype(jnp.bfloat16), "seq").astype(jnp.float32),
        lax.psum(shares[9].astype(jnp.bfloat16), "seq").astype(jnp.float32),
        lax.psum(shares[10].astype(jnp.bfloat16), "seq").astype(jnp.float32),
        lax.psum(shares[11].astype(jnp.bfloat16), "seq").astype(jnp.float32),
        lax.psum(shares[12].astype(jnp.bfloat16), "seq").astype(jnp.float32),
    )
    block_output = layer_out.astype(jnp.bfloat16).reshape(doc_count, slot_count, features)
    return (
        block_output,
        tokens_grad,
        summed[0],
        summed[1],
        summed[2],
        summed[3],
        summed[4],
        summed[5],
        summed[6],
        summed[7],
        summed[8],
        summed[9],
        summed[10],
        summed[11],
        summed[12],
    )


def local(
    tokens,
    seg_count,
    seg_align,
    cotangent,
    qkv_weight,
    query_bias,
    value_bias,
    output_weight,
    output_bias,
    first_gain,
    first_shift,
    inner_weight,
    inner_bias,
    outer_weight,
    outer_bias,
    second_gain,
    second_shift,
):
    dp, seq = lax.axis_size("dp"), lax.axis_size("seq")
    documents, _, features = tokens.shape
    if dp != PARTS or seq != 2 or documents != 2 or features != PARTS * UNIT_ROWS:
        return plain(
            tokens, seg_count, seg_align, cotangent, qkv_weight, query_bias, value_bias, output_weight, output_bias, first_gain, first_shift, inner_weight, inner_bias, outer_weight, outer_bias, second_gain, second_shift
        )
    vectors = jnp.concatenate(
        [
            query_bias,
            jnp.zeros_like(query_bias),
            value_bias,
            output_bias,
            first_gain,
            first_shift,
            outer_bias,
            second_gain,
            second_shift,
            inner_bias,
            jnp.zeros((3 * features,), F32),
        ]
    ).reshape(16, features)
    block_output, tokens_grad, g_qkv, g_out, g_inner, g_outer, sums, _ = layer(
        tokens, cotangent, seg_align, seg_count, vectors, qkv_weight, output_weight, inner_weight, outer_weight
    )
    place = lax.axis_index("dp")
    rows = lax.dynamic_slice(sums, (0, place * UNIT_ROWS), (8, UNIT_ROWS))
    inner_bias_grad = lax.dynamic_slice(sums[8:12].reshape(-1), (place * 4 * UNIT_ROWS,), (4 * UNIT_ROWS,))
    return (
        block_output,
        tokens_grad,
        g_qkv,
        rows[6],
        rows[7],
        g_out,
        rows[5],
        rows[3],
        rows[4],
        g_inner,
        inner_bias_grad,
        g_outer,
        rows[2],
        rows[0],
        rows[1],
    )


def solution(mesh):
    return jax.shard_map(
        local,
        mesh=mesh,
        in_specs=(
            P("dp", "seq", None),
            P("dp"),
            P("dp", None),
            P("dp", "seq", None),
            P(),
            P(),
            P(),
            P(),
            P(),
            P(),
            P(),
            P(),
            P(),
            P(),
            P(),
            P(),
            P(),
        ),
        out_specs=(
            P("dp", "seq", None),
            P("dp", "seq", None),
            P("dp", None),
            P("dp"),
            P("dp"),
            P("dp", None),
            P("dp"),
            P("dp"),
            P("dp"),
            P("dp", None),
            P("dp"),
            P("dp", None),
            P("dp"),
            P("dp"),
            P("dp"),
        ),
        check_vma=False,
    )
```

```python
import functools

import jax
import jax.numpy as jnp
from jax import lax
from jax.experimental import pallas as pl
from jax.experimental.pallas import tpu as pltpu
from jax.sharding import PartitionSpec as P

H = 12


LAYOUT_REWARD = 2.0
BLOCKED_SCORE = -1000000000.0
NORM_EPS = 1e-05
LOG2E = 1.4426950408889634
HEAD = 64
PAIR = 128
WIDE = 256
BF, F32 = jnp.bfloat16, jnp.float32


def dot(left, right):
    return jnp.dot(left, right, preferred_element_type=F32)


def dot_nt(left, right):
    return lax.dot_general(left, right, (((1,), (1,)), ((), ())), preferred_element_type=F32)


def dot_tn(left, right):
    return lax.dot_general(left, right, (((0,), (0,)), ((), ())), preferred_element_type=F32)


def at(start, size):
    return pl.ds(pl.multiple_of(start, size), size)


def loop(count, body):
    def step(index, carry):
        body(index)
        return carry

    lax.fori_loop(0, count, step, 0)


def fold_rows(block):
    rows, columns = block.shape
    return jnp.sum(block.reshape(rows // 8, 8, columns), axis=0)


def project_tokens(x, w_qkv, bias_row, qkv, rows):
    columns = w_qkv.shape[1]

    def body(index):
        here = at(index * WIDE, WIDE)
        qkv[rows, here] = (dot(x[rows, :], w_qkv[:, here]) + bias_row[0:1, here]).astype(BF)

    loop(columns // WIDE, body)


def fill_reward(reward, seg_row, count):
    text = seg_row.shape[1]
    segs = reward.shape[0] - text
    key = lax.broadcasted_iota(jnp.int32, (segs, text), 0)
    match = jnp.where(key == seg_row, LAYOUT_REWARD * LOG2E, 0.0).astype(F32)
    dead = jnp.where(key >= count, BLOCKED_SCORE * LOG2E, 0.0).astype(F32)
    turned = jnp.transpose(match)
    reward[...] = jnp.zeros_like(reward)
    slots = text + segs
    for head in range(2):
        reward[text:slots, head * slots : head * slots + text] = match + dead
        reward[text:slots, head * slots + text : (head + 1) * slots] = dead[:, :segs]
        reward[0:text, head * slots + text : (head + 1) * slots] = turned


def split_heads(block, both):
    slots = block.shape[0]
    first = lax.broadcasted_iota(jnp.int32, block.shape, 1) < HEAD
    zero = jnp.zeros_like(block)
    both[0:slots, :] = jnp.where(first, block, zero)
    both[slots:, :] = jnp.where(first, zero, block)


def attend(qkv, reward, probs_of, context_t, both, turned, side):
    slots, features = qkv.shape[0], qkv.shape[1] // 3
    pairs = features // PAIR
    scaling = HEAD ** (-0.5) * LOG2E

    def pair_step(pair):
        here = at(pair * PAIR, PAIR)
        keys = qkv[:, at(features + pair * PAIR, PAIR)]
        split_heads(qkv[:, here], both)
        turned[...] = jnp.transpose(qkv[:, at(2 * features + pair * PAIR, PAIR)])
        probs = probs_of(pair)

        for chunk in range(2 * slots // WIDE):
            block = slice(chunk * WIDE, (chunk + 1) * WIDE)
            scores = dot_nt(keys, both[block, :]) * scaling + reward[:, block]
            scores = jnp.exp2(scores - jnp.max(scores, axis=0, keepdims=True))
            low = (scores * (1.0 / jnp.sum(scores, axis=0, keepdims=True))).astype(BF)
            probs[:, block] = low
            side[:, block] = dot(turned[...], low).astype(BF)
        context_t[at(pair * PAIR, HEAD), :] = side[:HEAD, :slots]
        context_t[at(pair * PAIR + HEAD, HEAD), :] = side[HEAD:, slots:]

    return pair_step, pairs


def first_norm(x, attended, bias, gain, shift, normal, root, low, rows):
    def body(index):
        here = at(index * rows, rows)
        hidden = x[here, :].astype(F32) + (attended[here, :] + bias[...])
        centre = hidden - jnp.mean(hidden, axis=1, keepdims=True)
        inverse = lax.rsqrt(jnp.mean(centre * centre, axis=1, keepdims=True) + NORM_EPS)
        unit = centre * inverse
        normal[here, :] = unit
        root[here, :] = jnp.broadcast_to(inverse, (rows, PAIR))
        low[here, :] = (unit * gain[...] + shift[...]).astype(BF)

    loop(x.shape[0] // rows, body)


def gate(inner):
    normal = 0.5 * (1.0 + lax.erf(inner * 0.7071067811865476))
    density = jnp.exp2(inner * inner * (-0.5 * LOG2E)) * 0.3989422804014327
    return inner * normal, normal + inner * density


def feed_forward(low, w_inner, b_inner, hidden, slope):
    def body(index):
        here = at(index * WIDE, WIDE)
        value, grade = gate(dot(low[...], w_inner[:, here]) + b_inner[0:1, here])
        hidden[:, here] = value.astype(BF)
        slope[:, here] = grade.astype(BF)

    loop(w_inner.shape[1] // WIDE, body)


def second_norm(normal, first_gain, first_shift, mlp, bias, gain, shift, cotangent, output, grad, grad_low, sums, rows):
    sums[0:3] = jnp.zeros((3,) + sums.shape[1:], F32)

    def body(index):
        here = at(index * rows, rows)
        one = normal[here, :] * first_gain[...] + first_shift[...]
        total = one + (mlp[here, :] + bias[...])
        centre = total - jnp.mean(total, axis=1, keepdims=True)
        inverse = lax.rsqrt(jnp.mean(centre * centre, axis=1, keepdims=True) + NORM_EPS)
        unit = centre * inverse
        pull = cotangent[here, :].astype(F32)
        output[here, :] = (unit * gain[...] + shift[...]).astype(BF)
        scaled = pull * gain[...]
        back = inverse * (
            scaled
            - jnp.mean(scaled, axis=1, keepdims=True)
            - unit * jnp.mean(scaled * unit, axis=1, keepdims=True)
        )
        rounded = back.astype(BF)
        grad[here, :] = back
        grad_low[here, :] = rounded
        sums[0] += fold_rows(pull * unit)
        sums[1] += fold_rows(pull)
        sums[2] += fold_rows(rounded.astype(F32))

    loop(normal.shape[0] // rows, body)


def first_norm_back(grad_second, back, normal, root, gain, grad_first, grad_low, sums, rows):
    sums[3:6] = jnp.zeros((3,) + sums.shape[1:], F32)

    def body(index):
        here = at(index * rows, rows)
        pull = grad_second[here, :] + back[here, :]
        unit = normal[here, :]
        scaled = pull * gain[...]
        inverse = root[here, 0:1]
        first = inverse * (
            scaled
            - jnp.mean(scaled, axis=1, keepdims=True)
            - unit * jnp.mean(scaled * unit, axis=1, keepdims=True)
        )
        rounded = first.astype(BF)
        grad_first[here, :] = first
        grad_low[here, :] = rounded
        sums[3] += fold_rows(pull * unit)
        sums[4] += fold_rows(pull)
        sums[5] += fold_rows(rounded.astype(F32))

    loop(normal.shape[0] // rows, body)


def attend_back(qkv, grad_context, probs_of, grad_qkv, both, both_grad, turned, scores, side, points):
    slots, features = qkv.shape[0], qkv.shape[1] // 3
    scaling = HEAD ** (-0.5)

    def pair_step(pair):
        here = at(pair * PAIR, PAIR)
        there = at(features + pair * PAIR, PAIR)
        last = at(2 * features + pair * PAIR, PAIR)
        split_heads(qkv[:, here], both)
        split_heads(grad_context[:, here], both_grad)
        turned[...] = jnp.transpose(qkv[:, there])
        values = qkv[:, last]
        probs = probs_of(pair)
        for chunk in range(2 * slots // WIDE):
            block = slice(chunk * WIDE, (chunk + 1) * WIDE)
            pull = dot_nt(values, both_grad[block, :])
            weight = probs[:, block].astype(F32)
            mean = jnp.sum(weight * pull, axis=0, keepdims=True)
            low = (weight * (pull - mean)).astype(BF)
            scores[:, block] = low
            side[:, block] = dot(turned[...], low)
            if chunk == 2:
                points("u", pair)
        points("v", pair)
        grad_qkv[:, there] = (dot(scores[...], both[...]) * scaling).astype(BF)
        grad_qkv[:, last] = dot(probs[...], both_grad[...]).astype(BF)
        mine = jnp.concatenate([side[:HEAD, :slots], side[HEAD:, slots:]], axis=0)
        grad_qkv[:, here] = jnp.transpose(mine * scaling).astype(BF)

    return pair_step, features // PAIR


PARTS = 16
MESH = pl.DeviceIdType.MESH
UNIT_ROWS = 48
UNITS = 12
WEIGHT = {"c": 1, "y": 2, "l": 4, "h": 8}
ORDERS = (
    "clhxyg",
    "cyxlhg",
    "cylxhg",
    "clyxhg",
    "cxlyhg",
    "cxylhg",
    "cxylhg",
    "cylhxg",
    "cxlyhg",
    "cylhxg",
    "cxylhg",
    "cylxhg",
)
SMALL_ORDER = "cylhx"
SWAP = 0


def partner_of(bit, me, seq):
    if bit in "xg":
        return (me, 1 - seq)
    weight = WEIGHT[bit]
    return (me + weight * (1 - 2 * ((me // weight) % 2)), seq)


def stage_shapes(order, rows, columns):
    bits, shapes = 4, []
    for bit in order:
        if bit == "x":
            columns //= 2
        elif bit != "g":
            bits -= 1
        shapes.append((2,) * bits + (rows, columns))
    return shapes


def add_into(target, other):
    lead = target.shape[:-2]
    total = 1
    for size in lead:
        total *= size

    def step(index, carry):
        place, rest = [], index
        for size in reversed(lead):
            place.append(rest % size)
            rest = rest // size
        place = tuple(reversed(place)) + (slice(None), slice(None))
        target[place] = target[place] + other[place]
        return carry

    if total == 1:
        step(0, 0)
    else:
        lax.fori_loop(0, total, step, 0)


class Unit:
    def __init__(self, number, source, order, buffers, sends, recvs, me, seq):
        self.number, self.source, self.order, self.buffers = number, source, order, buffers
        self.sends, self.recvs, self.me, self.seq = sends, recvs, me, seq

    def at_stage(self, stage):
        bits = ["h", "l", "y", "c"]
        for bit in self.order[:stage]:
            if bit in bits:
                bits.remove(bit)
        current = self.buffers[stage - 1] if stage else self.source
        bit = self.order[stage]
        if bit == "g":
            return current, None
        if bit == "x":
            size = current.shape[-1] // 2
            lead = (slice(None),) * (len(bits) + 1)
            own = current.at[lead + (pl.ds(pl.multiple_of(self.seq * size, PAIR), size),)]
            return current.at[lead + (pl.ds(pl.multiple_of((1 - self.seq) * size, PAIR), size),)], own
        mine = (self.me // WEIGHT[bit]) % 2
        lead = (slice(None),) * bits.index(bit)
        return current.at[lead + (1 - mine,)], current.at[lead + (mine,)]

    def copy(self, stage):
        return pltpu.make_async_remote_copy(
            src_ref=self.at_stage(stage)[0],
            dst_ref=self.buffers[stage],
            send_sem=self.sends.at[self.number, stage],
            recv_sem=self.recvs.at[self.number, stage],
            device_id=partner_of(self.order[stage], self.me, self.seq),
            device_id_type=MESH,
        )

    def advance(self, stage):
        self.copy(stage).wait()
        self.add(stage)

    def add(self, stage):
        kept = self.at_stage(stage)[1]
        if kept is not None:
            add_into(self.buffers[stage], kept)
        if stage + 1 < len(self.order):
            self.copy(stage + 1).start()


def with_stages(schedule):
    reached = [0] * (UNITS + 1)
    plan = {}
    for point, numbers in schedule:
        steps = plan.setdefault(point, [])
        for number in numbers:
            steps.append((number, reached[number]))
            reached[number] += 1
    return plan


def layer_kernel(
    tokens, cotangent, seg_align, seg_count,
    query_bias, value_bias, output_bias, first_gain, first_shift, outer_bias, second_gain, second_shift, inner_bias,
    w_qkv, w_out, w_inner, w_outer,
    block_output, tokens_grad, shards, sums_out, probs_hbm,
    vectors, x, qkv, context_t, w_out_v, normal, root, cot, acc, grad_att, sums, own, small, small_got, *rest,
):
    rest = list(rest)
    buffers = [[rest.pop(0) for _ in ORDERS[0][:-1]] for _ in range(UNITS)]
    unit_send, unit_recv, outer_send, outer_recv, local_sem, pair_sem, swap_send, swap_recv, small_send, small_recv, vector_sem, shard_sem = rest
    slots, features = x.shape
    half = slots // 2
    wide = w_inner.shape[1]
    me, seq = lax.axis_index("dp"), lax.axis_index("seq")
    core = me % 2
    mine, other = at(seq * half, half), at((1 - seq) * half, half)
    b_out, gain1, shift1, b_outer, gain2, shift2 = (vectors.at[i : i + 1] for i in range(3, 9))
    columns = [slice(c * WIDE, (c + 1) * WIDE) for c in range(features // WIDE)]

    barrier = pltpu.get_barrier_semaphore()
    for bit in "xcylh":
        pl.semaphore_signal(barrier, inc=1, device_id=partner_of(bit, me, seq), device_id_type=MESH)

    def local(source, target, index):
        return pltpu.make_async_copy(source, target, local_sem.at[index])

    def swap(source, target, index):
        return pltpu.make_async_remote_copy(
            src_ref=source, dst_ref=target, send_sem=swap_send.at[index], recv_sem=swap_recv.at[index],
            device_id=(me, 1 - seq), device_id_type=MESH)

    keep_tokens = local(tokens.at[seq], x.at[mine], 0)
    keep_cot = local(cotangent.at[seq], cot.at[mine], 1)
    load_out = local(w_out, w_out_v, 2)
    swap_tokens = swap(tokens.at[1 - seq], x.at[mine], 0)
    swap_cot = swap(cotangent.at[1 - seq], cot.at[mine], 1)
    keep_output = local(cot.at[mine], block_output.at[seq], 3)
    swap_output = swap(cot.at[other], block_output.at[seq], 2)
    keep_grad = local(x.at[mine], tokens_grad.at[seq], 4)
    swap_grad = swap(x.at[other], tokens_grad.at[seq], 3)
    keep_tokens.start()
    rows_of = {0: query_bias, 2: value_bias, 3: output_bias, 4: first_gain, 5: first_shift, 6: outer_bias, 7: second_gain, 8: second_shift}
    load_vectors = [pltpu.make_async_copy(ref, vectors.at[i], vector_sem.at[i]) for i, ref in rows_of.items()]
    load_vectors += [
        pltpu.make_async_copy(inner_bias.at[pl.ds(i * features, features)], vectors.at[9 + i], vector_sem.at[9 + i])
        for i in range(wide // features)
    ]
    for copy in load_vectors:
        copy.start()
    vectors[1:2] = jnp.zeros((1, features), F32)

    units = [
        Unit(n, own.at[n if n < 8 else n - 8], ORDERS[n], buffers[n] + [shards.at[n, seq]], unit_send, unit_recv, me, seq)
        for n in range(UNITS)
    ]

    def keep_shard(number):
        return pltpu.make_async_copy(buffers[number][-1], shards.at[number, seq], shard_sem.at[number])

    def outer_copy(j, sub):
        hi, lo = j // 2, j % 2
        return pltpu.make_async_remote_copy(
            src_ref=own.at[sub, hi, lo, :, 1 - core],
            dst_ref=buffers[sub][0].at[hi, lo],
            send_sem=outer_send.at[j, sub], recv_sem=outer_recv.at[j, sub],
            device_id=partner_of("c", me, seq), device_id_type=MESH)

    def small_copy(stage):
        return pltpu.make_async_remote_copy(
            src_ref=small, dst_ref=small_got.at[stage], send_sem=small_send.at[stage], recv_sem=small_recv.at[stage],
            device_id=partner_of(SMALL_ORDER[stage], me, seq), device_id_type=MESH)

    def advance(number, stage):
        if number == UNITS:
            small_copy(stage).wait()
            small[...] += small_got[stage]
            if stage + 1 < len(SMALL_ORDER):
                small_copy(stage + 1).start()
        elif number < 4 and stage == 0:
            for j in range(4):
                outer_copy(j, number).wait()
            units[number].add(0)
        else:
            units[number].advance(stage)
        if number < UNITS and stage == 4:
            keep_shard(number).start()

    plan = with_stages(SCHEDULE)

    def point(name):
        for number, stage in plan.get(name, ()):
            advance(number, stage)

    def points(name, index, count):
        for i in range(count):
            if (name, i) in plan:
                pl.when(index == i)(functools.partial(point, (name, i)))

    def forward(w_inner_v, w_outer_v):
        load_inner, load_outer = local(w_inner, w_inner_v, 5), local(w_outer, w_outer_v, 6)

        def attention(w_qkv_v, reward, both, turned, side, probs_buf):
            load_qkv = local(w_qkv, w_qkv_v, 7)
            load_qkv.start()
            pl.semaphore_wait(barrier, 5)
            swap_tokens.start()
            load_out.start()
            fill_reward(reward, seg_align[pl.ds(seq, 1), :], seg_count[seq])
            keep_tokens.wait()
            for copy in load_vectors:
                copy.wait()
            load_qkv.wait()

            def project(rows):
                def body(index):
                    here = at(index * WIDE, WIDE)
                    bias = vectors[pl.ds(index // 3, 1), at(index % 3 * WIDE, WIDE)]
                    qkv[rows, here] = (dot(x[rows, :], w_qkv_v[:, here]) + bias).astype(BF)

                loop(3 * features // WIDE, body)

            project(mine)
            load_inner.start()
            load_outer.start()
            keep_cot.start()
            swap_tokens.wait()
            swap_cot.start()
            project(other)
            step, pairs = attend(qkv, reward, lambda pair: probs_buf.at[pair % 2], context_t, both, turned, side)

            def out_copy(pair):
                return pltpu.make_async_copy(probs_buf.at[pair % 2], probs_hbm.at[pair], pair_sem.at[pair % 2])

            def body(pair):
                @pl.when(pair >= 2)
                def _():
                    out_copy(pair - 2).wait()

                step(pair)
                out_copy(pair).start()

            loop(pairs, body)
            out_copy(pairs - 2).wait()
            out_copy(pairs - 1).wait()

        pl.run_scoped(
            attention,
            pltpu.VMEM((features, 3 * features), BF),
            pltpu.VMEM((slots, 2 * slots), F32),
            pltpu.VMEM((2 * slots, PAIR), BF),
            pltpu.VMEM((PAIR, slots), BF),
            pltpu.VMEM((PAIR, 2 * slots), BF),
            pltpu.VMEM((2, slots, 2 * slots), BF),
        )

        def mlp(low, turned_low, hidden, slope, grad_second):
            low[...] = jnp.transpose(context_t[...])
            load_out.wait()
            for here in columns:
                acc[:, here] = dot(low[...], w_out_v[:, here])
            first_norm(x, acc, b_out, gain1, shift1, normal, root, low, 160)
            load_inner.wait()

            def inner_body(index):
                here = at(index * WIDE, WIDE)
                bias = vectors[pl.ds(9 + index // 3, 1), at(index % 3 * WIDE, WIDE)]
                value, grade = gate(dot(low[...], w_inner_v[:, here]) + bias)
                hidden[:, here] = value.astype(BF)
                slope[:, here] = grade.astype(BF)

            loop(wide // WIDE, inner_body)
            load_outer.wait()
            for here in columns:
                acc[:, here] = dot(hidden[...], w_outer_v[:, here])
            keep_cot.wait()
            swap_cot.wait()
            second_norm(normal, gain1, shift1, acc, b_outer, gain2, shift2, cot, cot, grad_second, grad_att, sums, 160)
            keep_output.start()
            swap_output.start()
            turned_low[...] = jnp.transpose(low[...])

            def outer_step(j):
                block = dot_tn(hidden[:, at(j * features, features)], grad_att[...]).astype(BF)
                block = block.reshape(2, 2, 4, UNIT_ROWS, features)
                for sub in range(4):
                    own[sub, j // 2, j % 2] = block[:, :, sub]
                for sub in range(4):
                    outer_copy(j, sub).start()

            loop(4, outer_step)

            def inner_step(j):
                here = at(j * features, features)
                low_grad = (
                    dot_nt(grad_att[...], w_outer_v[here, :]) * slope[:, here].astype(F32)
                ).astype(BF)
                hidden[:, here] = low_grad
                sums[8 + j] = fold_rows(low_grad.astype(F32))
                points("g", j, 4)
                block = dot(turned_low[...], hidden[:, here]).astype(BF)
                own[4 + j] = block.reshape(2, 2, 2, 2, UNIT_ROWS, features)
                for i in range(4):
                    pl.when(j == i)(lambda i=i: units[4 + i].copy(0).start())
                points("i", j, 4)

            loop(4, inner_step)
            for c, here in enumerate(columns):
                acc[:, here] = dot_nt(hidden[...], w_inner_v[here, :])
                point(("a", c))
            first_norm_back(grad_second, acc, normal, root, gain1, acc, grad_att, sums, 160)

        pl.run_scoped(
            mlp,
            pltpu.VMEM((slots, features), BF),
            pltpu.VMEM((features, slots), BF),
            pltpu.VMEM((slots, wide), BF),
            pltpu.VMEM((slots, wide), BF),
            pltpu.VMEM((slots, features), F32),
        )

    pl.run_scoped(forward, pltpu.VMEM(w_inner.shape, BF), pltpu.VMEM(w_outer.shape, BF))

    def back(w_qkv_v, both, both_grad, turned, scores, side, probs_buf, grad_ctx, grad_qkv, turned_x):
        load_qkv = local(w_qkv, w_qkv_v, 8)
        load_qkv.start()

        def in_copy(pair):
            return pltpu.make_async_copy(probs_hbm.at[pair], probs_buf.at[pair % 2], pair_sem.at[pair % 2])

        in_copy(0).start()
        point(("n", 0))
        for c, here in enumerate(columns):
            block = dot(context_t[...], grad_att[:, here]).astype(BF)
            own[0, :, :, :, :, :, here] = block.reshape(2, 2, 2, 2, UNIT_ROWS, WIDE)
        units[8].copy(0).start()
        point(("o", 0))
        for c, here in enumerate(columns):
            grad_ctx[:, here] = dot_nt(grad_att[...], w_out_v[here, :]).astype(BF)
        turned_x[...] = jnp.transpose(x[...])
        point(("o", 1))
        step, pairs = attend_back(
            qkv, grad_ctx, lambda pair: probs_buf.at[pair % 2], grad_qkv, both, both_grad, turned, scores, side,
            lambda name, pair: points(name, pair, pairs))

        def body(pair):
            @pl.when(pair + 1 < pairs)
            def _():
                in_copy(pair + 1).start()

            in_copy(pair).wait()
            step(pair)
            points("r", pair, pairs)

            @pl.when(pair % 2 == 1)
            def _():
                group = pair // 2
                for part in range(3):
                    there = at(part * features + group * WIDE, WIDE)
                    block = dot(turned_x[...], grad_qkv[:, there]).astype(BF)
                    own[1 + group, :, :, :, :, :, part * WIDE : (part + 1) * WIDE] = block.reshape(
                        2, 2, 2, 2, UNIT_ROWS, WIDE)
                for i in range(3):
                    pl.when(group == i)(lambda i=i: units[9 + i].copy(0).start())

            points("s", pair, pairs)

        loop(pairs, body)
        sums[6] = fold_rows(grad_qkv[:, :features].astype(F32))
        sums[7] = fold_rows(grad_qkv[:, 2 * features :].astype(F32))
        small[...] = jnp.sum(sums[...], axis=1)
        small_copy(0).start()
        load_qkv.wait()
        for side_index, rows in enumerate((other, mine)):
            for c, here in enumerate(columns):
                x[rows, here] = (acc[rows, here] + dot_nt(grad_qkv[rows, :], w_qkv_v[here, :])).astype(BF)
                point(("t", side_index * 3 + c))
            (swap_grad if side_index == 0 else keep_grad).start()

    pl.run_scoped(
        back,
        pltpu.VMEM((features, 3 * features), BF),
        pltpu.VMEM((2 * slots, PAIR), BF),
        pltpu.VMEM((2 * slots, PAIR), BF),
        pltpu.VMEM((PAIR, slots), BF),
        pltpu.VMEM((slots, 2 * slots), BF),
        pltpu.VMEM((PAIR, 2 * slots), F32),
        pltpu.VMEM((2, slots, 2 * slots), BF),
        pltpu.VMEM((slots, features), BF),
        pltpu.VMEM((slots, 3 * features), BF),
        pltpu.VMEM((features, slots), BF),
    )
    point(("end", 0))
    keep_output.wait()
    swap_output.wait()
    keep_grad.wait()
    swap_grad.wait()
    for number in range(UNITS):
        keep_shard(number).wait()
    sums_out[...] = small[...]


def finish_kernel(
    block_in, grad_in, shards, sums,
    block_output, tokens_grad, g_qkv, g_query, g_value, g_out, g_out_bias, g_gain1, g_shift1, g_inner, g_inner_bias,
    g_outer, g_outer_bias, g_gain2, g_shift2, sem,
):
    copies = [
        pltpu.make_async_copy(block_in, block_output, sem.at[0]),
        pltpu.make_async_copy(grad_in, tokens_grad, sem.at[1]),
    ]
    for copy in copies:
        copy.start()
    me = lax.axis_index("dp")
    features = sums.shape[1]
    size = features // 2
    for number in range(UNITS):
        for place in range(2):
            value = shards[number, place].astype(F32)
            start = place * size
            if number < 4:
                g_outer[number * UNIT_ROWS : (number + 1) * UNIT_ROWS, start : start + size] = value
            elif number < 8:
                start += (number - 4) * features
                g_inner[:, start : start + size] = value
            elif number == 8:
                g_out[:, start : start + size] = value
            else:
                for piece in range(size // PAIR):
                    column = start + piece * PAIR
                    target = column // WIDE * features + (number - 9) * WIDE + column % WIDE
                    g_qkv[:, target : target + PAIR] = value[:, piece * PAIR : (piece + 1) * PAIR]
    rows = pltpu.roll(sums[0:8], (features - me * UNIT_ROWS) % features, 1)
    for index, out in enumerate((g_gain2, g_shift2, g_outer_bias, g_gain1, g_shift1, g_out_bias, g_query, g_value)):
        out[...] = rows[index, :UNIT_ROWS]
    share = 4 * UNIT_ROWS
    place = me * share
    line = pltpu.roll(sums[pl.ds(8 + place // features, 1)], (features - place % features) % features, 1)
    g_inner_bias[...] = line[0, :share]
    for copy in copies:
        copy.wait()


def finish(block, grad, shards, sums, wide):
    features = block.shape[-1]
    S = jax.ShapeDtypeStruct
    vector = S((UNIT_ROWS,), F32)
    hbm, vmem = pl.BlockSpec(memory_space=pltpu.HBM), pl.BlockSpec(memory_space=pltpu.VMEM)
    return pl.pallas_call(
        finish_kernel,
        name="finish",
        out_shape=[
            S(block.shape, BF), S(grad.shape, BF), S((UNIT_ROWS, 3 * features), F32), vector, vector,
            S((UNIT_ROWS, features), F32), vector, vector, vector, S((UNIT_ROWS, wide), F32), S((4 * UNIT_ROWS,), F32),
            S((4 * UNIT_ROWS, features), F32), vector, vector, vector,
        ],
        in_specs=[hbm, hbm, vmem, vmem],
        out_specs=[hbm, hbm] + [vmem] * 13,
        scratch_shapes=[pltpu.SemaphoreType.DMA((2,))],
        compiler_params=pltpu.CompilerParams(vmem_limit_bytes=32 * 2**20),
    )(block, grad, shards, sums)


def layer(tokens, cotangent, seg_align, seg_count, vectors, w_qkv, w_out, w_inner, w_outer):
    documents, half, features = tokens.shape
    slots, wide = 2 * half, w_inner.shape[1]
    pairs = features // PAIR
    S, V, D = jax.ShapeDtypeStruct, pltpu.VMEM, pltpu.SemaphoreType.DMA
    scratch = [
        V((16, features), F32), V((slots, features), BF), V((slots, 3 * features), BF), V((features, slots), BF), V(w_out.shape, BF),
        V((slots, features), F32), V((slots, PAIR), F32), V((slots, features), BF), V((slots, features), F32),
        V((slots, features), BF), V((16, 8, features), F32), V((8, 2, 2, 2, 2, UNIT_ROWS, features), BF),
        V((16, features), F32), V((len(SMALL_ORDER), 16, features), F32),
    ]
    for number in range(UNITS):
        scratch += [V(shape, BF) for shape in stage_shapes(ORDERS[number], UNIT_ROWS, features)[:-1]]
    scratch += [D((UNITS, 6)), D((UNITS, 6)), D((4, 4)), D((4, 4)), D((9,)), D((2,)), D((4,)), D((4,)), D((5,)), D((5,)), D((16,)), D((UNITS,))]
    hbm, vmem = pl.BlockSpec(memory_space=pltpu.HBM), pl.BlockSpec(memory_space=pltpu.VMEM)
    return pl.pallas_call(
        layer_kernel,
        name="layer",
        out_shape=[
            S(tokens.shape, BF), S(tokens.shape, BF), S((UNITS, 2, UNIT_ROWS, features // 2), BF), S((16, features), F32),
            S((pairs, slots, 2 * slots), BF),
        ],
        in_specs=[hbm, hbm, vmem, pl.BlockSpec(memory_space=pltpu.SMEM)] + [hbm] * 13,
        out_specs=[hbm, hbm, hbm, vmem, hbm],
        scratch_shapes=scratch,
        compiler_params=pltpu.CompilerParams(collective_id=0, has_side_effects=True, vmem_limit_bytes=60 * 2**20),
    )(tokens, cotangent, seg_align, seg_count, *vectors, w_qkv, w_out, w_inner, w_outer)


SCHEDULE = (
    (("i", 2), (0, 1, 2, 3, 4)),
    (("i", 3), (5,)),
    (("a", 0), (6,)),
    (("a", 1), (7,)),
    (("n", 0), (0, 1)),
    (("o", 0), (4,)),
    (("u", 0), (8,)),
    (("v", 0), (3, 2)),
    (("u", 1), (5,)),
    (("v", 2), (0, 4, 7)),
    (("r", 2), (6,)),
    (("u", 3), (9, 2)),
    (("v", 3), (3, 1)),
    (("u", 4), (7, 5)),
    (("v", 4), (4, 1)),
    (("u", 5), (10,)),
    (("v", 5), (8, 6)),
    (("s", 5), (0, 5, 7)),
    (("t", 0), (2, 4)),
    (("t", 2), (3,)),
    (("t", 3), (1,)),
    (("t", 4), (11, 12)),
    (("end", 0), (9, 8, 0, 6, 5, 10, 7, 2, 4, 3, 11, 12, 9, 8, 6, 11, 10, 12, 1, 9, 0, 5, 8, 7, 10, 2, 3, 6, 12, 11, 10, 9, 8, 12, 11, 10, 9, 11)),
)


def slot_groups(seg_count, seg_align, all_slots):
    doc_count, text_slots = seg_align.shape
    slot_index = jnp.arange(all_slots, dtype=jnp.int32)
    filler = jnp.zeros((doc_count, all_slots - text_slots), jnp.int32)
    padded = jnp.concatenate([seg_align, filler], axis=1)
    is_text = slot_index < text_slots
    groups = jnp.where(is_text[None, :], padded, (slot_index - text_slots)[None, :])
    present_keys = slot_index[None, :] < text_slots + seg_count[:, None]
    return (groups, is_text, present_keys)


def layer_norm(hidden, gain, shift):
    centre = hidden - jnp.mean(hidden, axis=-1, keepdims=True)
    spread = jnp.mean(centre * centre, axis=-1, keepdims=True)
    return centre * lax.rsqrt(spread + NORM_EPS) * gain + shift


def smooth_gate(inner):
    return jax.nn.gelu(inner, approximate=False)


def softmax_rows(logit_scores):
    return jax.nn.softmax(logit_scores, axis=-1)


def project(tokens, qkv_weight, query_bias, value_bias):
    doc_count, slot_count, features = tokens.shape
    token_rows = tokens.reshape(doc_count * slot_count, features)
    pre = jnp.dot(token_rows, qkv_weight, preferred_element_type=jnp.float32)
    queries = (pre[:, :features] + query_bias).astype(jnp.bfloat16)
    own_keys = (
        pre[:, features : 2 * features]
        .astype(jnp.bfloat16)
        .reshape(doc_count, slot_count, features)
    )
    own_values = (
        (pre[:, 2 * features :] + value_bias)
        .astype(jnp.bfloat16)
        .reshape(doc_count, slot_count, features)
    )
    all_keys, values = (
        lax.all_gather(own_keys, "seq", axis=1, tiled=True),
        lax.all_gather(own_values, "seq", axis=1, tiled=True),
    )
    return (queries, all_keys, values)


def plain(
    tokens,
    seg_count,
    seg_align,
    cotangent,
    qkv_weight,
    query_bias,
    value_bias,
    output_weight,
    output_bias,
    first_gain,
    first_shift,
    inner_weight,
    inner_bias,
    outer_weight,
    outer_bias,
    second_gain,
    second_shift,
):
    doc_count, slot_count, features = tokens.shape
    row_count = doc_count * slot_count
    head_dim = features // H
    scaling = head_dim ** (-0.5)
    all_slots = slot_count * lax.axis_size("seq")
    row_start = lax.axis_index("seq") * slot_count
    groups, is_text, present_keys = slot_groups(seg_count, seg_align, all_slots)
    group_rows = lax.dynamic_slice_in_dim(groups, row_start, slot_count, 1)
    text_rows = lax.dynamic_slice_in_dim(is_text, row_start, slot_count, 0)
    matched_pairs = (group_rows[:, :, None] == groups[:, None, :]) & (
        text_rows[None, :, None] != is_text[None, None, :]
    )
    layout_reward = LAYOUT_REWARD * matched_pairs.astype(jnp.float32)
    queries, all_keys, values = project(tokens, qkv_weight, query_bias, value_bias)
    query_heads = queries.reshape(doc_count, slot_count, H, head_dim)
    key_heads = all_keys.reshape(doc_count, all_slots, H, head_dim)
    value_heads = values.reshape(doc_count, all_slots, H, head_dim)
    unadjusted_scores = (
        jnp.einsum("bqhd,bkhd->bhqk", query_heads, key_heads, preferred_element_type=jnp.float32)
        * scaling
    )
    logit_scores = jnp.where(
        present_keys[:, None, None, :], unadjusted_scores + layout_reward[:, None], BLOCKED_SCORE
    )
    attn_probs, soft_pull = jax.vjp(softmax_rows, logit_scores)
    probs_low = attn_probs.astype(jnp.bfloat16)
    context = jnp.einsum(
        "bhqk,bkhd->bqhd", probs_low, value_heads, preferred_element_type=jnp.float32
    )
    context = context.reshape(row_count, features).astype(jnp.bfloat16)
    token_rows = tokens.reshape(row_count, features)
    attended = jnp.dot(context, output_weight, preferred_element_type=jnp.float32) + output_bias
    normed_one, first_pull = jax.vjp(
        layer_norm, token_rows.astype(jnp.float32) + attended, first_gain, first_shift
    )
    normed_low = normed_one.astype(jnp.bfloat16)
    inner = jnp.dot(normed_low, inner_weight, preferred_element_type=jnp.float32) + inner_bias
    activated, gate_pull = jax.vjp(smooth_gate, inner)
    hidden = activated.astype(jnp.bfloat16)
    mlp_out = jnp.dot(hidden, outer_weight, preferred_element_type=jnp.float32) + outer_bias
    layer_out, second_pull = jax.vjp(layer_norm, normed_one + mlp_out, second_gain, second_shift)
    grad_out = cotangent.reshape(row_count, features).astype(jnp.float32)
    grad_second, second_gain_grad, second_shift_grad = second_pull(grad_out)
    grad_mlp = grad_second.astype(jnp.bfloat16)
    outer_weight_grad = jnp.einsum(
        "rf,rd->fd", hidden, grad_mlp, preferred_element_type=jnp.float32
    )
    outer_bias_grad = jnp.sum(grad_mlp.astype(jnp.float32), axis=0)
    grad_hidden = jnp.einsum(
        "rd,fd->rf", grad_mlp, outer_weight, preferred_element_type=jnp.float32
    )
    grad_inner = gate_pull(grad_hidden)[0].astype(jnp.bfloat16)
    inner_weight_grad = jnp.einsum(
        "rd,rf->df", normed_low, grad_inner, preferred_element_type=jnp.float32
    )
    inner_bias_grad = jnp.sum(grad_inner.astype(jnp.float32), axis=0)
    grad_normed = grad_second + jnp.einsum(
        "rf,df->rd", grad_inner, inner_weight, preferred_element_type=jnp.float32
    )
    grad_first, first_gain_grad, first_shift_grad = first_pull(grad_normed)
    grad_attended = grad_first.astype(jnp.bfloat16)
    output_weight_grad = jnp.einsum(
        "rc,rd->cd", context, grad_attended, preferred_element_type=jnp.float32
    )
    output_bias_grad = jnp.sum(grad_attended.astype(jnp.float32), axis=0)
    grad_context = jnp.einsum(
        "rd,cd->rc", grad_attended, output_weight, preferred_element_type=jnp.float32
    )
    grad_context = grad_context.astype(jnp.bfloat16).reshape(doc_count, slot_count, H, head_dim)
    grad_probs = jnp.einsum(
        "bqhd,bkhd->bhqk", grad_context, value_heads, preferred_element_type=jnp.float32
    )
    grad_scores = soft_pull(grad_probs)[0].astype(jnp.bfloat16)
    grad_queries = (
        jnp.einsum("bhqk,bkhd->bqhd", grad_scores, key_heads, preferred_element_type=jnp.float32)
        * scaling
    )
    grad_queries = grad_queries.astype(jnp.bfloat16).reshape(row_count, features)
    key_term = (
        jnp.einsum("bhqk,bqhd->bkhd", grad_scores, query_heads, preferred_element_type=jnp.float32)
        * scaling
    )
    value_term = jnp.einsum(
        "bhqk,bqhd->bkhd", probs_low, grad_context, preferred_element_type=jnp.float32
    )
    key_sum, value_sum = (
        lax.psum_scatter(
            key_term.reshape(doc_count, all_slots, features).astype(jnp.bfloat16),
            "seq",
            scatter_dimension=1,
            tiled=True,
        ).astype(jnp.float32),
        lax.psum_scatter(
            value_term.reshape(doc_count, all_slots, features).astype(jnp.bfloat16),
            "seq",
            scatter_dimension=1,
            tiled=True,
        ).astype(jnp.float32),
    )
    grad_keys = key_sum.astype(jnp.bfloat16).reshape(row_count, features)
    grad_values = value_sum.astype(jnp.bfloat16).reshape(row_count, features)
    grad_project = jnp.concatenate([grad_queries, grad_keys, grad_values], axis=1)
    qkv_weight_grad = jnp.einsum(
        "rd,re->de", token_rows, grad_project, preferred_element_type=jnp.float32
    )
    query_bias_grad = jnp.sum(grad_queries.astype(jnp.float32), axis=0)
    value_bias_grad = jnp.sum(grad_values.astype(jnp.float32), axis=0)
    tokens_grad = grad_first + jnp.einsum(
        "re,de->rd", grad_project, qkv_weight, preferred_element_type=jnp.float32
    )
    tokens_grad = tokens_grad.astype(jnp.bfloat16).reshape(doc_count, slot_count, features)
    shares = (
        lax.psum_scatter(qkv_weight_grad, "dp", scatter_dimension=0, tiled=True),
        lax.psum_scatter(query_bias_grad, "dp", scatter_dimension=0, tiled=True),
        lax.psum_scatter(value_bias_grad, "dp", scatter_dimension=0, tiled=True),
        lax.psum_scatter(output_weight_grad, "dp", scatter_dimension=0, tiled=True),
        lax.psum_scatter(output_bias_grad, "dp", scatter_dimension=0, tiled=True),
        lax.psum_scatter(first_gain_grad, "dp", scatter_dimension=0, tiled=True),
        lax.psum_scatter(first_shift_grad, "dp", scatter_dimension=0, tiled=True),
        lax.psum_scatter(inner_weight_grad, "dp", scatter_dimension=0, tiled=True),
        lax.psum_scatter(inner_bias_grad, "dp", scatter_dimension=0, tiled=True),
        lax.psum_scatter(outer_weight_grad, "dp", scatter_dimension=0, tiled=True),
        lax.psum_scatter(outer_bias_grad, "dp", scatter_dimension=0, tiled=True),
        lax.psum_scatter(second_gain_grad, "dp", scatter_dimension=0, tiled=True),
        lax.psum_scatter(second_shift_grad, "dp", scatter_dimension=0, tiled=True),
    )
    summed = (
        lax.psum(shares[0].astype(jnp.bfloat16), "seq").astype(jnp.float32),
        lax.psum(shares[1].astype(jnp.bfloat16), "seq").astype(jnp.float32),
        lax.psum(shares[2].astype(jnp.bfloat16), "seq").astype(jnp.float32),
        lax.psum(shares[3].astype(jnp.bfloat16), "seq").astype(jnp.float32),
        lax.psum(shares[4].astype(jnp.bfloat16), "seq").astype(jnp.float32),
        lax.psum(shares[5].astype(jnp.bfloat16), "seq").astype(jnp.float32),
        lax.psum(shares[6].astype(jnp.bfloat16), "seq").astype(jnp.float32),
        lax.psum(shares[7].astype(jnp.bfloat16), "seq").astype(jnp.float32),
        lax.psum(shares[8].astype(jnp.bfloat16), "seq").astype(jnp.float32),
        lax.psum(shares[9].astype(jnp.bfloat16), "seq").astype(jnp.float32),
        lax.psum(shares[10].astype(jnp.bfloat16), "seq").astype(jnp.float32),
        lax.psum(shares[11].astype(jnp.bfloat16), "seq").astype(jnp.float32),
        lax.psum(shares[12].astype(jnp.bfloat16), "seq").astype(jnp.float32),
    )
    block_output = layer_out.astype(jnp.bfloat16).reshape(doc_count, slot_count, features)
    return (
        block_output,
        tokens_grad,
        summed[0],
        summed[1],
        summed[2],
        summed[3],
        summed[4],
        summed[5],
        summed[6],
        summed[7],
        summed[8],
        summed[9],
        summed[10],
        summed[11],
        summed[12],
    )


def local(
    tokens,
    seg_count,
    seg_align,
    cotangent,
    qkv_weight,
    query_bias,
    value_bias,
    output_weight,
    output_bias,
    first_gain,
    first_shift,
    inner_weight,
    inner_bias,
    outer_weight,
    outer_bias,
    second_gain,
    second_shift,
):
    dp, seq = lax.axis_size("dp"), lax.axis_size("seq")
    documents, _, features = tokens.shape
    if dp != PARTS or seq != 2 or documents != 2 or features != PARTS * UNIT_ROWS:
        return plain(
            tokens, seg_count, seg_align, cotangent, qkv_weight, query_bias, value_bias, output_weight, output_bias, first_gain, first_shift, inner_weight, inner_bias, outer_weight, outer_bias, second_gain, second_shift
        )
    vectors = (
        query_bias, value_bias, output_bias, first_gain, first_shift, outer_bias, second_gain, second_shift, inner_bias
    )
    block, grad, shards, sums, _ = layer(
        tokens, cotangent, seg_align, seg_count, vectors, qkv_weight, output_weight, inner_weight, outer_weight
    )
    return tuple(finish(block, grad, shards, sums, inner_weight.shape[1]))


def solution(mesh):
    return jax.shard_map(
        local,
        mesh=mesh,
        in_specs=(
            P("dp", "seq", None),
            P("dp"),
            P("dp", None),
            P("dp", "seq", None),
            P(),
            P(),
            P(),
            P(),
            P(),
            P(),
            P(),
            P(),
            P(),
            P(),
            P(),
            P(),
            P(),
        ),
        out_specs=(
            P("dp", "seq", None),
            P("dp", "seq", None),
            P("dp", None),
            P("dp"),
            P("dp"),
            P("dp", None),
            P("dp"),
            P("dp"),
            P("dp"),
            P("dp", None),
            P("dp"),
            P("dp", None),
            P("dp"),
            P("dp"),
            P("dp"),
        ),
        check_vma=False,
    )
```

```python
import functools

import jax
import jax.numpy as jnp
from jax import lax
from jax.experimental import pallas as pl
from jax.experimental.pallas import tpu as pltpu
from jax.sharding import PartitionSpec as P

H = 12


LAYOUT_REWARD = 2.0
BLOCKED_SCORE = -1000000000.0
NORM_EPS = 1e-05
LOG2E = 1.4426950408889634
HEAD = 64
PAIR = 128
WIDE = 256
BF, F32 = jnp.bfloat16, jnp.float32


def dot(left, right):
    return jnp.dot(left, right, preferred_element_type=F32)


def dot_nt(left, right):
    return lax.dot_general(left, right, (((1,), (1,)), ((), ())), preferred_element_type=F32)


def dot_tn(left, right):
    return lax.dot_general(left, right, (((0,), (0,)), ((), ())), preferred_element_type=F32)


def at(start, size):
    return pl.ds(pl.multiple_of(start, size), size)


def loop(count, body):
    def step(index, carry):
        body(index)
        return carry

    lax.fori_loop(0, count, step, 0)


def fold_rows(block):
    rows, columns = block.shape
    return jnp.sum(block.reshape(rows // 8, 8, columns), axis=0)


def project_tokens(x, w_qkv, bias_row, qkv, rows):
    columns = w_qkv.shape[1]

    def body(index):
        here = at(index * WIDE, WIDE)
        qkv[rows, here] = (dot(x[rows, :], w_qkv[:, here]) + bias_row[0:1, here]).astype(BF)

    loop(columns // WIDE, body)


def fill_reward(reward, seg_row, count):
    text = seg_row.shape[1]
    segs = reward.shape[0] - text
    key = lax.broadcasted_iota(jnp.int32, (segs, text), 0)
    match = jnp.where(key == seg_row, LAYOUT_REWARD * LOG2E, 0.0).astype(F32)
    dead = jnp.where(key >= count, BLOCKED_SCORE * LOG2E, 0.0).astype(F32)
    turned = jnp.transpose(match)
    reward[...] = jnp.zeros_like(reward)
    slots = text + segs
    for head in range(2):
        reward[text:slots, head * slots : head * slots + text] = match + dead
        reward[text:slots, head * slots + text : (head + 1) * slots] = dead[:, :segs]
        reward[0:text, head * slots + text : (head + 1) * slots] = turned


def split_heads(block, both):
    slots = block.shape[0]
    first = lax.broadcasted_iota(jnp.int32, block.shape, 1) < HEAD
    zero = jnp.zeros_like(block)
    both[0:slots, :] = jnp.where(first, block, zero)
    both[slots:, :] = jnp.where(first, zero, block)


def attend(qkv, reward, probs_of, context_t, both, turned, side):
    slots, features = qkv.shape[0], qkv.shape[1] // 3
    pairs = features // PAIR
    scaling = HEAD ** (-0.5) * LOG2E

    def pair_step(pair):
        here = at(pair * PAIR, PAIR)
        keys = qkv[:, at(features + pair * PAIR, PAIR)]
        split_heads(qkv[:, here], both)
        turned[...] = jnp.transpose(qkv[:, at(2 * features + pair * PAIR, PAIR)])
        probs = probs_of(pair)

        for chunk in range(2 * slots // WIDE):
            block = slice(chunk * WIDE, (chunk + 1) * WIDE)
            scores = dot_nt(keys, both[block, :]) * scaling + reward[:, block]
            scores = jnp.exp2(scores - jnp.max(scores, axis=0, keepdims=True))
            probs[:, block] = (scores * (1.0 / jnp.sum(scores, axis=0, keepdims=True))).astype(BF)
        side[...] = dot(turned[...], probs[...]).astype(BF)
        context_t[at(pair * PAIR, HEAD), :] = side[:HEAD, :slots]
        context_t[at(pair * PAIR + HEAD, HEAD), :] = side[HEAD:, slots:]

    return pair_step, pairs


def first_norm(x, attended, bias, gain, shift, normal, root, low, rows):
    def body(index):
        here = at(index * rows, rows)
        hidden = x[here, :].astype(F32) + (attended[here, :] + bias[...])
        centre = hidden - jnp.mean(hidden, axis=1, keepdims=True)
        inverse = lax.rsqrt(jnp.mean(centre * centre, axis=1, keepdims=True) + NORM_EPS)
        unit = centre * inverse
        normal[here, :] = unit
        root[here, :] = jnp.broadcast_to(inverse, (rows, PAIR))
        low[here, :] = (unit * gain[...] + shift[...]).astype(BF)

    loop(x.shape[0] // rows, body)


def gate(inner):
    normal = 0.5 * (1.0 + lax.erf(inner * 0.7071067811865476))
    density = jnp.exp2(inner * inner * (-0.5 * LOG2E)) * 0.3989422804014327
    return inner * normal, normal + inner * density


def feed_forward(low, w_inner, b_inner, hidden, slope):
    def body(index):
        here = at(index * WIDE, WIDE)
        value, grade = gate(dot(low[...], w_inner[:, here]) + b_inner[0:1, here])
        hidden[:, here] = value.astype(BF)
        slope[:, here] = grade.astype(BF)

    loop(w_inner.shape[1] // WIDE, body)


def second_norm(normal, first_gain, first_shift, mlp, bias, gain, shift, cotangent, output, grad, grad_low, sums, rows):
    sums[0:3] = jnp.zeros((3,) + sums.shape[1:], F32)

    def body(index):
        here = at(index * rows, rows)
        one = normal[here, :] * first_gain[...] + first_shift[...]
        total = one + (mlp[here, :] + bias[...])
        centre = total - jnp.mean(total, axis=1, keepdims=True)
        inverse = lax.rsqrt(jnp.mean(centre * centre, axis=1, keepdims=True) + NORM_EPS)
        unit = centre * inverse
        pull = cotangent[here, :].astype(F32)
        output[here, :] = (unit * gain[...] + shift[...]).astype(BF)
        scaled = pull * gain[...]
        back = inverse * (
            scaled
            - jnp.mean(scaled, axis=1, keepdims=True)
            - unit * jnp.mean(scaled * unit, axis=1, keepdims=True)
        )
        rounded = back.astype(BF)
        grad[here, :] = back
        grad_low[here, :] = rounded
        sums[0] += fold_rows(pull * unit)
        sums[1] += fold_rows(pull)
        sums[2] += fold_rows(rounded.astype(F32))

    loop(normal.shape[0] // rows, body)


def first_norm_back(grad_second, back, normal, root, gain, grad_first, grad_low, sums, rows):
    sums[3:6] = jnp.zeros((3,) + sums.shape[1:], F32)

    def body(index):
        here = at(index * rows, rows)
        pull = grad_second[here, :] + back[here, :]
        unit = normal[here, :]
        scaled = pull * gain[...]
        inverse = root[here, 0:1]
        first = inverse * (
            scaled
            - jnp.mean(scaled, axis=1, keepdims=True)
            - unit * jnp.mean(scaled * unit, axis=1, keepdims=True)
        )
        rounded = first.astype(BF)
        grad_first[here, :] = first
        grad_low[here, :] = rounded
        sums[3] += fold_rows(pull * unit)
        sums[4] += fold_rows(pull)
        sums[5] += fold_rows(rounded.astype(F32))

    loop(normal.shape[0] // rows, body)


def attend_back(qkv, grad_context, probs_of, grad_qkv, both, both_grad, turned, scores, side, points):
    slots, features = qkv.shape[0], qkv.shape[1] // 3
    scaling = HEAD ** (-0.5)

    def pair_step(pair):
        here = at(pair * PAIR, PAIR)
        there = at(features + pair * PAIR, PAIR)
        last = at(2 * features + pair * PAIR, PAIR)
        split_heads(qkv[:, here], both)
        split_heads(grad_context[:, here], both_grad)
        turned[...] = jnp.transpose(qkv[:, there])
        values = qkv[:, last]
        probs = probs_of(pair)
        for chunk in range(2 * slots // WIDE):
            block = slice(chunk * WIDE, (chunk + 1) * WIDE)
            pull = dot_nt(values, both_grad[block, :])
            weight = probs[:, block].astype(F32)
            mean = jnp.sum(weight * pull, axis=0, keepdims=True)
            low = (weight * (pull - mean)).astype(BF)
            scores[:, block] = low
            if chunk == 2:
                points("u", pair)
        points("v", pair)
        side[...] = dot(turned[...], scores[...])
        grad_qkv[:, there] = (dot(scores[...], both[...]) * scaling).astype(BF)
        grad_qkv[:, last] = dot(probs[...], both_grad[...]).astype(BF)
        mine = jnp.concatenate([side[:HEAD, :slots], side[HEAD:, slots:]], axis=0)
        grad_qkv[:, here] = jnp.transpose(mine * scaling).astype(BF)

    return pair_step, features // PAIR


PARTS = 16
MESH = pl.DeviceIdType.MESH
UNIT_ROWS = 48
UNITS = 12
WEIGHT = {"c": 1, "y": 2, "l": 4, "h": 8}
ORDERS = (
    "clhxyg",
    "cyxlhg",
    "cylxhg",
    "clyxhg",
    "cxlyhg",
    "cxylhg",
    "cxylhg",
    "cylhxg",
    "cxlyhg",
    "cylhxg",
    "cxylhg",
    "cylxhg",
)
SMALL_ORDER = "cylhx"
SWAP = 0


def partner_of(bit, me, seq):
    if bit in "xg":
        return (me, 1 - seq)
    weight = WEIGHT[bit]
    return (me + weight * (1 - 2 * ((me // weight) % 2)), seq)


def stage_shapes(order, rows, columns):
    bits, shapes = 4, []
    for bit in order:
        if bit == "x":
            columns //= 2
        elif bit != "g":
            bits -= 1
        shapes.append((2,) * bits + (rows, columns))
    return shapes


def add_into(target, other):
    lead = target.shape[:-2]
    total = 1
    for size in lead:
        total *= size

    def step(index, carry):
        place, rest = [], index
        for size in reversed(lead):
            place.append(rest % size)
            rest = rest // size
        place = tuple(reversed(place)) + (slice(None), slice(None))
        target[place] = target[place] + other[place]
        return carry

    if total == 1:
        step(0, 0)
    else:
        lax.fori_loop(0, total, step, 0)


class Unit:
    def __init__(self, number, source, order, buffers, sends, recvs, me, seq):
        self.number, self.source, self.order, self.buffers = number, source, order, buffers
        self.sends, self.recvs, self.me, self.seq = sends, recvs, me, seq

    def at_stage(self, stage):
        bits = ["h", "l", "y", "c"]
        for bit in self.order[:stage]:
            if bit in bits:
                bits.remove(bit)
        current = self.buffers[stage - 1] if stage else self.source
        bit = self.order[stage]
        if bit == "g":
            return current, None
        if bit == "x":
            size = current.shape[-1] // 2
            lead = (slice(None),) * (len(bits) + 1)
            own = current.at[lead + (pl.ds(pl.multiple_of(self.seq * size, PAIR), size),)]
            return current.at[lead + (pl.ds(pl.multiple_of((1 - self.seq) * size, PAIR), size),)], own
        mine = (self.me // WEIGHT[bit]) % 2
        lead = (slice(None),) * bits.index(bit)
        return current.at[lead + (1 - mine,)], current.at[lead + (mine,)]

    def copy(self, stage):
        return pltpu.make_async_remote_copy(
            src_ref=self.at_stage(stage)[0],
            dst_ref=self.buffers[stage],
            send_sem=self.sends.at[self.number, stage],
            recv_sem=self.recvs.at[self.number, stage],
            device_id=partner_of(self.order[stage], self.me, self.seq),
            device_id_type=MESH,
        )

    def advance(self, stage):
        self.copy(stage).wait()
        self.add(stage)

    def add(self, stage):
        kept = self.at_stage(stage)[1]
        if kept is not None:
            add_into(self.buffers[stage], kept)
        if stage + 1 < len(self.order):
            self.copy(stage + 1).start()


def with_stages(schedule):
    reached = [0] * (UNITS + 1)
    plan = {}
    for point, numbers in schedule:
        steps = plan.setdefault(point, [])
        for number in numbers:
            steps.append((number, reached[number]))
            reached[number] += 1
    return plan


def layer_kernel(
    tokens, cotangent, seg_align, seg_count,
    query_bias, value_bias, output_bias, first_gain, first_shift, outer_bias, second_gain, second_shift, inner_bias,
    w_qkv, w_out, w_inner, w_outer,
    block_output, tokens_grad, shards, sums_out, probs_hbm,
    vectors, x, qkv, context_t, w_out_v, normal, root, cot, acc, grad_att, sums, own, small, small_got, *rest,
):
    rest = list(rest)
    buffers = [[rest.pop(0) for _ in ORDERS[0][:-1]] for _ in range(UNITS)]
    unit_send, unit_recv, outer_send, outer_recv, local_sem, pair_sem, swap_send, swap_recv, small_send, small_recv, vector_sem, shard_sem = rest
    slots, features = x.shape
    half = slots // 2
    wide = w_inner.shape[1]
    me, seq = lax.axis_index("dp"), lax.axis_index("seq")
    core = me % 2
    mine, other = at(seq * half, half), at((1 - seq) * half, half)
    b_out, gain1, shift1, b_outer, gain2, shift2 = (vectors.at[i : i + 1] for i in range(3, 9))
    columns = [slice(c * WIDE, (c + 1) * WIDE) for c in range(features // WIDE)]

    barrier = pltpu.get_barrier_semaphore()
    for bit in "xcylh":
        pl.semaphore_signal(barrier, inc=1, device_id=partner_of(bit, me, seq), device_id_type=MESH)

    def local(source, target, index):
        return pltpu.make_async_copy(source, target, local_sem.at[index])

    def swap(source, target, index):
        return pltpu.make_async_remote_copy(
            src_ref=source, dst_ref=target, send_sem=swap_send.at[index], recv_sem=swap_recv.at[index],
            device_id=(me, 1 - seq), device_id_type=MESH)

    keep_tokens = local(tokens.at[seq], x.at[mine], 0)
    keep_cot = local(cotangent.at[seq], cot.at[mine], 1)
    load_out = local(w_out, w_out_v, 2)
    swap_tokens = swap(tokens.at[1 - seq], x.at[mine], 0)
    swap_cot = swap(cotangent.at[1 - seq], cot.at[mine], 1)
    keep_output = local(cot.at[mine], block_output.at[seq], 3)
    swap_output = swap(cot.at[other], block_output.at[seq], 2)
    keep_grad = local(x.at[mine], tokens_grad.at[seq], 4)
    swap_grad = swap(x.at[other], tokens_grad.at[seq], 3)
    keep_tokens.start()
    rows_of = {0: query_bias, 2: value_bias, 3: output_bias, 4: first_gain, 5: first_shift, 6: outer_bias, 7: second_gain, 8: second_shift}
    load_vectors = [pltpu.make_async_copy(ref, vectors.at[i], vector_sem.at[i]) for i, ref in rows_of.items()]
    load_vectors += [
        pltpu.make_async_copy(inner_bias.at[pl.ds(i * features, features)], vectors.at[9 + i], vector_sem.at[9 + i])
        for i in range(wide // features)
    ]
    for copy in load_vectors:
        copy.start()
    vectors[1:2] = jnp.zeros((1, features), F32)

    units = [
        Unit(n, own.at[n if n < 8 else n - 8], ORDERS[n], buffers[n] + [shards.at[n, seq]], unit_send, unit_recv, me, seq)
        for n in range(UNITS)
    ]

    def keep_shard(number):
        return pltpu.make_async_copy(buffers[number][-1], shards.at[number, seq], shard_sem.at[number])

    def outer_copy(j, sub):
        hi, lo = j // 2, j % 2
        return pltpu.make_async_remote_copy(
            src_ref=own.at[sub, hi, lo, :, 1 - core],
            dst_ref=buffers[sub][0].at[hi, lo],
            send_sem=outer_send.at[j, sub], recv_sem=outer_recv.at[j, sub],
            device_id=partner_of("c", me, seq), device_id_type=MESH)

    def small_copy(stage):
        return pltpu.make_async_remote_copy(
            src_ref=small, dst_ref=small_got.at[stage], send_sem=small_send.at[stage], recv_sem=small_recv.at[stage],
            device_id=partner_of(SMALL_ORDER[stage], me, seq), device_id_type=MESH)

    def advance(number, stage):
        if number == UNITS:
            small_copy(stage).wait()
            small[...] += small_got[stage]
            if stage + 1 < len(SMALL_ORDER):
                small_copy(stage + 1).start()
        elif number < 4 and stage == 0:
            for j in range(4):
                outer_copy(j, number).wait()
            units[number].add(0)
        else:
            units[number].advance(stage)
        if number < UNITS and stage == 4:
            keep_shard(number).start()

    plan = with_stages(SCHEDULE)

    def point(name):
        for number, stage in plan.get(name, ()):
            advance(number, stage)

    def points(name, index, count):
        for i in range(count):
            if (name, i) in plan:
                pl.when(index == i)(functools.partial(point, (name, i)))

    def forward(w_inner_v, w_outer_v):
        load_inner, load_outer = local(w_inner, w_inner_v, 5), local(w_outer, w_outer_v, 6)

        def attention(w_qkv_v, reward, both, turned, side, probs_buf):
            load_qkv = local(w_qkv, w_qkv_v, 7)
            load_qkv.start()
            pl.semaphore_wait(barrier, 5)
            swap_tokens.start()
            load_out.start()
            fill_reward(reward, seg_align[pl.ds(seq, 1), :], seg_count[seq])
            keep_tokens.wait()
            for copy in load_vectors:
                copy.wait()
            load_qkv.wait()

            def project(rows):
                def body(index):
                    here = at(index * WIDE, WIDE)
                    bias = vectors[pl.ds(index // 3, 1), at(index % 3 * WIDE, WIDE)]
                    qkv[rows, here] = (dot(x[rows, :], w_qkv_v[:, here]) + bias).astype(BF)

                loop(3 * features // WIDE, body)

            project(mine)
            load_inner.start()
            load_outer.start()
            keep_cot.start()
            swap_tokens.wait()
            swap_cot.start()
            project(other)
            step, pairs = attend(qkv, reward, lambda pair: probs_buf.at[pair % 2], context_t, both, turned, side)

            def out_copy(pair):
                return pltpu.make_async_copy(probs_buf.at[pair % 2], probs_hbm.at[pair], pair_sem.at[pair % 2])

            def body(pair):
                @pl.when(pair >= 2)
                def _():
                    out_copy(pair - 2).wait()

                step(pair)
                out_copy(pair).start()

            loop(pairs, body)
            out_copy(pairs - 2).wait()
            out_copy(pairs - 1).wait()

        pl.run_scoped(
            attention,
            pltpu.VMEM((features, 3 * features), BF),
            pltpu.VMEM((slots, 2 * slots), F32),
            pltpu.VMEM((2 * slots, PAIR), BF),
            pltpu.VMEM((PAIR, slots), BF),
            pltpu.VMEM((PAIR, 2 * slots), BF),
            pltpu.VMEM((2, slots, 2 * slots), BF),
        )

        def mlp(low, turned_low, hidden, slope, grad_second):
            low[...] = jnp.transpose(context_t[...])
            load_out.wait()
            for here in columns:
                acc[:, here] = dot(low[...], w_out_v[:, here])
            first_norm(x, acc, b_out, gain1, shift1, normal, root, low, 160)
            load_inner.wait()

            def inner_body(index):
                here = at(index * WIDE, WIDE)
                bias = vectors[pl.ds(9 + index // 3, 1), at(index % 3 * WIDE, WIDE)]
                value, grade = gate(dot(low[...], w_inner_v[:, here]) + bias)
                hidden[:, here] = value.astype(BF)
                slope[:, here] = grade.astype(BF)

            loop(wide // WIDE, inner_body)
            load_outer.wait()
            for here in columns:
                acc[:, here] = dot(hidden[...], w_outer_v[:, here])
            keep_cot.wait()
            swap_cot.wait()
            second_norm(normal, gain1, shift1, acc, b_outer, gain2, shift2, cot, cot, grad_second, grad_att, sums, 160)
            keep_output.start()
            swap_output.start()

            turned_low[...] = jnp.transpose(low[...])

            def outer_step(j):
                block = dot_tn(hidden[:, at(j * features, features)], grad_att[...]).astype(BF)
                block = block.reshape(2, 2, 4, UNIT_ROWS, features)
                for sub in range(4):
                    own[sub, j // 2, j % 2] = block[:, :, sub]
                for sub in range(4):
                    outer_copy(j, sub).start()

            loop(4, outer_step)

            def inner_step(j):
                here = at(j * features, features)
                low_grad = (
                    dot_nt(grad_att[...], w_outer_v[here, :]) * slope[:, here].astype(F32)
                ).astype(BF)
                hidden[:, here] = low_grad
                sums[8 + j] = fold_rows(low_grad.astype(F32))
                points("g", j, 4)
                block = dot(turned_low[...], hidden[:, here]).astype(BF)
                own[4 + j] = block.reshape(2, 2, 2, 2, UNIT_ROWS, features)
                for i in range(4):
                    pl.when(j == i)(lambda i=i: units[4 + i].copy(0).start())
                points("i", j, 4)

            loop(4, inner_step)
            for c, here in enumerate(columns):
                acc[:, here] = dot_nt(hidden[...], w_inner_v[here, :])
                point(("a", c))
            first_norm_back(grad_second, acc, normal, root, gain1, acc, grad_att, sums, 160)

        pl.run_scoped(
            mlp,
            pltpu.VMEM((slots, features), BF),
            pltpu.VMEM((features, slots), BF),
            pltpu.VMEM((slots, wide), BF),
            pltpu.VMEM((slots, wide), BF),
            pltpu.VMEM((slots, features), F32),
        )

    pl.run_scoped(forward, pltpu.VMEM(w_inner.shape, BF), pltpu.VMEM(w_outer.shape, BF))

    def back(w_qkv_v, both, both_grad, turned, scores, side, probs_buf, grad_ctx, grad_qkv, turned_x):
        load_qkv = local(w_qkv, w_qkv_v, 8)
        load_qkv.start()

        def in_copy(pair):
            return pltpu.make_async_copy(probs_hbm.at[pair], probs_buf.at[pair % 2], pair_sem.at[pair % 2])

        in_copy(0).start()
        point(("n", 0))
        for c, here in enumerate(columns):
            block = dot(context_t[...], grad_att[:, here]).astype(BF)
            own[0, :, :, :, :, :, here] = block.reshape(2, 2, 2, 2, UNIT_ROWS, WIDE)
        units[8].copy(0).start()
        point(("o", 0))
        for c, here in enumerate(columns):
            grad_ctx[:, here] = dot_nt(grad_att[...], w_out_v[here, :]).astype(BF)
        turned_x[...] = jnp.transpose(x[...])
        point(("o", 1))
        step, pairs = attend_back(
            qkv, grad_ctx, lambda pair: probs_buf.at[pair % 2], grad_qkv, both, both_grad, turned, scores, side,
            lambda name, pair: points(name, pair, pairs))

        def body(pair):
            @pl.when(pair + 1 < pairs)
            def _():
                in_copy(pair + 1).start()

            in_copy(pair).wait()
            step(pair)
            points("r", pair, pairs)

            @pl.when(pair % 2 == 1)
            def _():
                group = pair // 2
                for part in range(3):
                    there = at(part * features + group * WIDE, WIDE)
                    block = dot(turned_x[...], grad_qkv[:, there]).astype(BF)
                    own[1 + group, :, :, :, :, :, part * WIDE : (part + 1) * WIDE] = block.reshape(
                        2, 2, 2, 2, UNIT_ROWS, WIDE)
                for i in range(3):
                    pl.when(group == i)(lambda i=i: units[9 + i].copy(0).start())

            points("s", pair, pairs)

        loop(pairs, body)
        sums[6] = fold_rows(grad_qkv[:, :features].astype(F32))
        sums[7] = fold_rows(grad_qkv[:, 2 * features :].astype(F32))
        small[...] = jnp.sum(sums[...], axis=1)
        small_copy(0).start()
        load_qkv.wait()
        for side_index, rows in enumerate((other, mine)):
            for c, here in enumerate(columns):
                x[rows, here] = (acc[rows, here] + dot_nt(grad_qkv[rows, :], w_qkv_v[here, :])).astype(BF)
                point(("t", side_index * 3 + c))
            (swap_grad if side_index == 0 else keep_grad).start()

    pl.run_scoped(
        back,
        pltpu.VMEM((features, 3 * features), BF),
        pltpu.VMEM((2 * slots, PAIR), BF),
        pltpu.VMEM((2 * slots, PAIR), BF),
        pltpu.VMEM((PAIR, slots), BF),
        pltpu.VMEM((slots, 2 * slots), BF),
        pltpu.VMEM((PAIR, 2 * slots), F32),
        pltpu.VMEM((2, slots, 2 * slots), BF),
        pltpu.VMEM((slots, features), BF),
        pltpu.VMEM((slots, 3 * features), BF),
        pltpu.VMEM((features, slots), BF),
    )
    point(("end", 0))
    keep_output.wait()
    swap_output.wait()
    keep_grad.wait()
    swap_grad.wait()
    for number in range(UNITS):
        keep_shard(number).wait()
    sums_out[...] = small[...]


def finish_kernel(
    block_in, grad_in, shards, sums,
    block_output, tokens_grad, g_qkv, g_query, g_value, g_out, g_out_bias, g_gain1, g_shift1, g_inner, g_inner_bias,
    g_outer, g_outer_bias, g_gain2, g_shift2, passed, sem,
):
    ins, outs = [], []
    for index, (source, target) in enumerate(((block_in, block_output), (grad_in, tokens_grad))):
        for part in range(2):
            buffer, number = passed.at[index, part], 2 * index + part
            ins.append(pltpu.make_async_copy(source.at[part], buffer, sem.at[0, number]))
            outs.append(pltpu.make_async_copy(buffer, target.at[part], sem.at[1, number]))
    for copy in ins:
        copy.start()
    for copy, onward in zip(ins, outs):
        copy.wait()
        onward.start()
    me = lax.axis_index("dp")
    features = sums.shape[1]
    size = features // 2
    for number in range(UNITS):
        for place in range(2):
            value = shards[number, place].astype(F32)
            start = place * size
            if number < 4:
                g_outer[number * UNIT_ROWS : (number + 1) * UNIT_ROWS, start : start + size] = value
            elif number < 8:
                start += (number - 4) * features
                g_inner[:, start : start + size] = value
            elif number == 8:
                g_out[:, start : start + size] = value
            else:
                for piece in range(size // PAIR):
                    column = start + piece * PAIR
                    target = column // WIDE * features + (number - 9) * WIDE + column % WIDE
                    g_qkv[:, target : target + PAIR] = value[:, piece * PAIR : (piece + 1) * PAIR]
    rows = pltpu.roll(sums[0:8], (features - me * UNIT_ROWS) % features, 1)
    for index, out in enumerate((g_gain2, g_shift2, g_outer_bias, g_gain1, g_shift1, g_out_bias, g_query, g_value)):
        out[...] = rows[index, :UNIT_ROWS]
    share = 4 * UNIT_ROWS
    place = me * share
    line = pltpu.roll(sums[pl.ds(8 + place // features, 1)], (features - place % features) % features, 1)
    g_inner_bias[...] = line[0, :share]
    for copy in outs:
        copy.wait()


def finish(block, grad, shards, sums, wide):
    features = block.shape[-1]
    S = jax.ShapeDtypeStruct
    vector = S((UNIT_ROWS,), F32)
    hbm, vmem = pl.BlockSpec(memory_space=pltpu.HBM), pl.BlockSpec(memory_space=pltpu.VMEM)
    return pl.pallas_call(
        finish_kernel,
        name="finish",
        out_shape=[
            S(block.shape, BF), S(grad.shape, BF), S((UNIT_ROWS, 3 * features), F32), vector, vector,
            S((UNIT_ROWS, features), F32), vector, vector, vector, S((UNIT_ROWS, wide), F32), S((4 * UNIT_ROWS,), F32),
            S((4 * UNIT_ROWS, features), F32), vector, vector, vector,
        ],
        in_specs=[hbm, hbm, vmem, vmem],
        out_specs=[hbm, hbm] + [vmem] * 13,
        scratch_shapes=[pltpu.VMEM((2,) + block.shape, BF), pltpu.SemaphoreType.DMA((2, 4))],
        compiler_params=pltpu.CompilerParams(vmem_limit_bytes=60 * 2**20),
    )(block, grad, shards, sums)


def layer(tokens, cotangent, seg_align, seg_count, vectors, w_qkv, w_out, w_inner, w_outer):
    documents, half, features = tokens.shape
    slots, wide = 2 * half, w_inner.shape[1]
    pairs = features // PAIR
    S, V, D = jax.ShapeDtypeStruct, pltpu.VMEM, pltpu.SemaphoreType.DMA
    scratch = [
        V((16, features), F32), V((slots, features), BF), V((slots, 3 * features), BF), V((features, slots), BF), V(w_out.shape, BF),
        V((slots, features), F32), V((slots, PAIR), F32), V((slots, features), BF), V((slots, features), F32),
        V((slots, features), BF), V((16, 8, features), F32), V((8, 2, 2, 2, 2, UNIT_ROWS, features), BF),
        V((16, features), F32), V((len(SMALL_ORDER), 16, features), F32),
    ]
    for number in range(UNITS):
        scratch += [V(shape, BF) for shape in stage_shapes(ORDERS[number], UNIT_ROWS, features)[:-1]]
    scratch += [D((UNITS, 6)), D((UNITS, 6)), D((4, 4)), D((4, 4)), D((9,)), D((2,)), D((4,)), D((4,)), D((5,)), D((5,)), D((16,)), D((UNITS,))]
    hbm, vmem = pl.BlockSpec(memory_space=pltpu.HBM), pl.BlockSpec(memory_space=pltpu.VMEM)
    return pl.pallas_call(
        layer_kernel,
        name="layer",
        out_shape=[
            S(tokens.shape, BF), S(tokens.shape, BF), S((UNITS, 2, UNIT_ROWS, features // 2), BF), S((16, features), F32),
            S((pairs, slots, 2 * slots), BF),
        ],
        in_specs=[hbm, hbm, vmem, pl.BlockSpec(memory_space=pltpu.SMEM)] + [hbm] * 13,
        out_specs=[hbm, hbm, hbm, vmem, hbm],
        scratch_shapes=scratch,
        compiler_params=pltpu.CompilerParams(collective_id=0, has_side_effects=True, vmem_limit_bytes=60 * 2**20),
    )(tokens, cotangent, seg_align, seg_count, *vectors, w_qkv, w_out, w_inner, w_outer)


SCHEDULE = (
    (("i", 2), (0, 1, 2, 3, 4)),
    (("i", 3), (5,)),
    (("a", 0), (6,)),
    (("a", 1), (7,)),
    (("n", 0), (0, 1)),
    (("o", 0), (4,)),
    (("u", 0), (8,)),
    (("v", 0), (3, 2)),
    (("u", 1), (5,)),
    (("v", 2), (0, 4, 7)),
    (("r", 2), (6,)),
    (("u", 3), (9, 2)),
    (("v", 3), (3, 1)),
    (("u", 4), (7, 5)),
    (("v", 4), (4, 1)),
    (("u", 5), (10,)),
    (("v", 5), (8, 6)),
    (("s", 5), (0, 5, 7)),
    (("t", 0), (2, 4)),
    (("t", 2), (3,)),
    (("t", 3), (1,)),
    (("t", 4), (11, 12)),
    (("end", 0), (9, 8, 0, 6, 5, 10, 7, 2, 4, 3, 11, 12, 9, 8, 6, 11, 10, 12, 1, 9, 0, 5, 8, 7, 10, 2, 3, 6, 12, 11, 10, 9, 8, 12, 11, 10, 9, 11)),
)


def slot_groups(seg_count, seg_align, all_slots):
    doc_count, text_slots = seg_align.shape
    slot_index = jnp.arange(all_slots, dtype=jnp.int32)
    filler = jnp.zeros((doc_count, all_slots - text_slots), jnp.int32)
    padded = jnp.concatenate([seg_align, filler], axis=1)
    is_text = slot_index < text_slots
    groups = jnp.where(is_text[None, :], padded, (slot_index - text_slots)[None, :])
    present_keys = slot_index[None, :] < text_slots + seg_count[:, None]
    return (groups, is_text, present_keys)


def layer_norm(hidden, gain, shift):
    centre = hidden - jnp.mean(hidden, axis=-1, keepdims=True)
    spread = jnp.mean(centre * centre, axis=-1, keepdims=True)
    return centre * lax.rsqrt(spread + NORM_EPS) * gain + shift


def smooth_gate(inner):
    return jax.nn.gelu(inner, approximate=False)


def softmax_rows(logit_scores):
    return jax.nn.softmax(logit_scores, axis=-1)


def project(tokens, qkv_weight, query_bias, value_bias):
    doc_count, slot_count, features = tokens.shape
    token_rows = tokens.reshape(doc_count * slot_count, features)
    pre = jnp.dot(token_rows, qkv_weight, preferred_element_type=jnp.float32)
    queries = (pre[:, :features] + query_bias).astype(jnp.bfloat16)
    own_keys = (
        pre[:, features : 2 * features]
        .astype(jnp.bfloat16)
        .reshape(doc_count, slot_count, features)
    )
    own_values = (
        (pre[:, 2 * features :] + value_bias)
        .astype(jnp.bfloat16)
        .reshape(doc_count, slot_count, features)
    )
    all_keys, values = (
        lax.all_gather(own_keys, "seq", axis=1, tiled=True),
        lax.all_gather(own_values, "seq", axis=1, tiled=True),
    )
    return (queries, all_keys, values)


def plain(
    tokens,
    seg_count,
    seg_align,
    cotangent,
    qkv_weight,
    query_bias,
    value_bias,
    output_weight,
    output_bias,
    first_gain,
    first_shift,
    inner_weight,
    inner_bias,
    outer_weight,
    outer_bias,
    second_gain,
    second_shift,
):
    doc_count, slot_count, features = tokens.shape
    row_count = doc_count * slot_count
    head_dim = features // H
    scaling = head_dim ** (-0.5)
    all_slots = slot_count * lax.axis_size("seq")
    row_start = lax.axis_index("seq") * slot_count
    groups, is_text, present_keys = slot_groups(seg_count, seg_align, all_slots)
    group_rows = lax.dynamic_slice_in_dim(groups, row_start, slot_count, 1)
    text_rows = lax.dynamic_slice_in_dim(is_text, row_start, slot_count, 0)
    matched_pairs = (group_rows[:, :, None] == groups[:, None, :]) & (
        text_rows[None, :, None] != is_text[None, None, :]
    )
    layout_reward = LAYOUT_REWARD * matched_pairs.astype(jnp.float32)
    queries, all_keys, values = project(tokens, qkv_weight, query_bias, value_bias)
    query_heads = queries.reshape(doc_count, slot_count, H, head_dim)
    key_heads = all_keys.reshape(doc_count, all_slots, H, head_dim)
    value_heads = values.reshape(doc_count, all_slots, H, head_dim)
    unadjusted_scores = (
        jnp.einsum("bqhd,bkhd->bhqk", query_heads, key_heads, preferred_element_type=jnp.float32)
        * scaling
    )
    logit_scores = jnp.where(
        present_keys[:, None, None, :], unadjusted_scores + layout_reward[:, None], BLOCKED_SCORE
    )
    attn_probs, soft_pull = jax.vjp(softmax_rows, logit_scores)
    probs_low = attn_probs.astype(jnp.bfloat16)
    context = jnp.einsum(
        "bhqk,bkhd->bqhd", probs_low, value_heads, preferred_element_type=jnp.float32
    )
    context = context.reshape(row_count, features).astype(jnp.bfloat16)
    token_rows = tokens.reshape(row_count, features)
    attended = jnp.dot(context, output_weight, preferred_element_type=jnp.float32) + output_bias
    normed_one, first_pull = jax.vjp(
        layer_norm, token_rows.astype(jnp.float32) + attended, first_gain, first_shift
    )
    normed_low = normed_one.astype(jnp.bfloat16)
    inner = jnp.dot(normed_low, inner_weight, preferred_element_type=jnp.float32) + inner_bias
    activated, gate_pull = jax.vjp(smooth_gate, inner)
    hidden = activated.astype(jnp.bfloat16)
    mlp_out = jnp.dot(hidden, outer_weight, preferred_element_type=jnp.float32) + outer_bias
    layer_out, second_pull = jax.vjp(layer_norm, normed_one + mlp_out, second_gain, second_shift)
    grad_out = cotangent.reshape(row_count, features).astype(jnp.float32)
    grad_second, second_gain_grad, second_shift_grad = second_pull(grad_out)
    grad_mlp = grad_second.astype(jnp.bfloat16)
    outer_weight_grad = jnp.einsum(
        "rf,rd->fd", hidden, grad_mlp, preferred_element_type=jnp.float32
    )
    outer_bias_grad = jnp.sum(grad_mlp.astype(jnp.float32), axis=0)
    grad_hidden = jnp.einsum(
        "rd,fd->rf", grad_mlp, outer_weight, preferred_element_type=jnp.float32
    )
    grad_inner = gate_pull(grad_hidden)[0].astype(jnp.bfloat16)
    inner_weight_grad = jnp.einsum(
        "rd,rf->df", normed_low, grad_inner, preferred_element_type=jnp.float32
    )
    inner_bias_grad = jnp.sum(grad_inner.astype(jnp.float32), axis=0)
    grad_normed = grad_second + jnp.einsum(
        "rf,df->rd", grad_inner, inner_weight, preferred_element_type=jnp.float32
    )
    grad_first, first_gain_grad, first_shift_grad = first_pull(grad_normed)
    grad_attended = grad_first.astype(jnp.bfloat16)
    output_weight_grad = jnp.einsum(
        "rc,rd->cd", context, grad_attended, preferred_element_type=jnp.float32
    )
    output_bias_grad = jnp.sum(grad_attended.astype(jnp.float32), axis=0)
    grad_context = jnp.einsum(
        "rd,cd->rc", grad_attended, output_weight, preferred_element_type=jnp.float32
    )
    grad_context = grad_context.astype(jnp.bfloat16).reshape(doc_count, slot_count, H, head_dim)
    grad_probs = jnp.einsum(
        "bqhd,bkhd->bhqk", grad_context, value_heads, preferred_element_type=jnp.float32
    )
    grad_scores = soft_pull(grad_probs)[0].astype(jnp.bfloat16)
    grad_queries = (
        jnp.einsum("bhqk,bkhd->bqhd", grad_scores, key_heads, preferred_element_type=jnp.float32)
        * scaling
    )
    grad_queries = grad_queries.astype(jnp.bfloat16).reshape(row_count, features)
    key_term = (
        jnp.einsum("bhqk,bqhd->bkhd", grad_scores, query_heads, preferred_element_type=jnp.float32)
        * scaling
    )
    value_term = jnp.einsum(
        "bhqk,bqhd->bkhd", probs_low, grad_context, preferred_element_type=jnp.float32
    )
    key_sum, value_sum = (
        lax.psum_scatter(
            key_term.reshape(doc_count, all_slots, features).astype(jnp.bfloat16),
            "seq",
            scatter_dimension=1,
            tiled=True,
        ).astype(jnp.float32),
        lax.psum_scatter(
            value_term.reshape(doc_count, all_slots, features).astype(jnp.bfloat16),
            "seq",
            scatter_dimension=1,
            tiled=True,
        ).astype(jnp.float32),
    )
    grad_keys = key_sum.astype(jnp.bfloat16).reshape(row_count, features)
    grad_values = value_sum.astype(jnp.bfloat16).reshape(row_count, features)
    grad_project = jnp.concatenate([grad_queries, grad_keys, grad_values], axis=1)
    qkv_weight_grad = jnp.einsum(
        "rd,re->de", token_rows, grad_project, preferred_element_type=jnp.float32
    )
    query_bias_grad = jnp.sum(grad_queries.astype(jnp.float32), axis=0)
    value_bias_grad = jnp.sum(grad_values.astype(jnp.float32), axis=0)
    tokens_grad = grad_first + jnp.einsum(
        "re,de->rd", grad_project, qkv_weight, preferred_element_type=jnp.float32
    )
    tokens_grad = tokens_grad.astype(jnp.bfloat16).reshape(doc_count, slot_count, features)
    shares = (
        lax.psum_scatter(qkv_weight_grad, "dp", scatter_dimension=0, tiled=True),
        lax.psum_scatter(query_bias_grad, "dp", scatter_dimension=0, tiled=True),
        lax.psum_scatter(value_bias_grad, "dp", scatter_dimension=0, tiled=True),
        lax.psum_scatter(output_weight_grad, "dp", scatter_dimension=0, tiled=True),
        lax.psum_scatter(output_bias_grad, "dp", scatter_dimension=0, tiled=True),
        lax.psum_scatter(first_gain_grad, "dp", scatter_dimension=0, tiled=True),
        lax.psum_scatter(first_shift_grad, "dp", scatter_dimension=0, tiled=True),
        lax.psum_scatter(inner_weight_grad, "dp", scatter_dimension=0, tiled=True),
        lax.psum_scatter(inner_bias_grad, "dp", scatter_dimension=0, tiled=True),
        lax.psum_scatter(outer_weight_grad, "dp", scatter_dimension=0, tiled=True),
        lax.psum_scatter(outer_bias_grad, "dp", scatter_dimension=0, tiled=True),
        lax.psum_scatter(second_gain_grad, "dp", scatter_dimension=0, tiled=True),
        lax.psum_scatter(second_shift_grad, "dp", scatter_dimension=0, tiled=True),
    )
    summed = (
        lax.psum(shares[0].astype(jnp.bfloat16), "seq").astype(jnp.float32),
        lax.psum(shares[1].astype(jnp.bfloat16), "seq").astype(jnp.float32),
        lax.psum(shares[2].astype(jnp.bfloat16), "seq").astype(jnp.float32),
        lax.psum(shares[3].astype(jnp.bfloat16), "seq").astype(jnp.float32),
        lax.psum(shares[4].astype(jnp.bfloat16), "seq").astype(jnp.float32),
        lax.psum(shares[5].astype(jnp.bfloat16), "seq").astype(jnp.float32),
        lax.psum(shares[6].astype(jnp.bfloat16), "seq").astype(jnp.float32),
        lax.psum(shares[7].astype(jnp.bfloat16), "seq").astype(jnp.float32),
        lax.psum(shares[8].astype(jnp.bfloat16), "seq").astype(jnp.float32),
        lax.psum(shares[9].astype(jnp.bfloat16), "seq").astype(jnp.float32),
        lax.psum(shares[10].astype(jnp.bfloat16), "seq").astype(jnp.float32),
        lax.psum(shares[11].astype(jnp.bfloat16), "seq").astype(jnp.float32),
        lax.psum(shares[12].astype(jnp.bfloat16), "seq").astype(jnp.float32),
    )
    block_output = layer_out.astype(jnp.bfloat16).reshape(doc_count, slot_count, features)
    return (
        block_output,
        tokens_grad,
        summed[0],
        summed[1],
        summed[2],
        summed[3],
        summed[4],
        summed[5],
        summed[6],
        summed[7],
        summed[8],
        summed[9],
        summed[10],
        summed[11],
        summed[12],
    )


def local(
    tokens,
    seg_count,
    seg_align,
    cotangent,
    qkv_weight,
    query_bias,
    value_bias,
    output_weight,
    output_bias,
    first_gain,
    first_shift,
    inner_weight,
    inner_bias,
    outer_weight,
    outer_bias,
    second_gain,
    second_shift,
):
    dp, seq = lax.axis_size("dp"), lax.axis_size("seq")
    documents, _, features = tokens.shape
    if dp != PARTS or seq != 2 or documents != 2 or features != PARTS * UNIT_ROWS:
        return plain(
            tokens, seg_count, seg_align, cotangent, qkv_weight, query_bias, value_bias, output_weight, output_bias, first_gain, first_shift, inner_weight, inner_bias, outer_weight, outer_bias, second_gain, second_shift
        )
    vectors = (
        query_bias, value_bias, output_bias, first_gain, first_shift, outer_bias, second_gain, second_shift, inner_bias
    )
    block, grad, shards, sums, _ = layer(
        tokens, cotangent, seg_align, seg_count, vectors, qkv_weight, output_weight, inner_weight, outer_weight
    )
    return tuple(finish(block, grad, shards, sums, inner_weight.shape[1]))


def solution(mesh):
    return jax.shard_map(
        local,
        mesh=mesh,
        in_specs=(
            P("dp", "seq", None),
            P("dp"),
            P("dp", None),
            P("dp", "seq", None),
            P(),
            P(),
            P(),
            P(),
            P(),
            P(),
            P(),
            P(),
            P(),
            P(),
            P(),
            P(),
            P(),
        ),
        out_specs=(
            P("dp", "seq", None),
            P("dp", "seq", None),
            P("dp", None),
            P("dp"),
            P("dp"),
            P("dp", None),
            P("dp"),
            P("dp"),
            P("dp"),
            P("dp", None),
            P("dp"),
            P("dp", None),
            P("dp"),
            P("dp"),
            P("dp"),
        ),
        check_vma=False,
    )
```

```python
import functools

import jax
import jax.numpy as jnp
from jax import lax
from jax.experimental import pallas as pl
from jax.experimental.pallas import tpu as pltpu
from jax.sharding import PartitionSpec as P

H = 12


LAYOUT_REWARD = 2.0
BLOCKED_SCORE = -1000000000.0
NORM_EPS = 1e-05
LOG2E = 1.4426950408889634
HEAD = 64
PAIR = 128
WIDE = 256
BF, F32 = jnp.bfloat16, jnp.float32


def dot(left, right):
    return jnp.dot(left, right, preferred_element_type=F32)


def dot_nt(left, right):
    return lax.dot_general(left, right, (((1,), (1,)), ((), ())), preferred_element_type=F32)


def dot_tn(left, right):
    return lax.dot_general(left, right, (((0,), (0,)), ((), ())), preferred_element_type=F32)


def at(start, size):
    return pl.ds(pl.multiple_of(start, size), size)


def loop(count, body):
    def step(index, carry):
        body(index)
        return carry

    lax.fori_loop(0, count, step, 0)


def fold_rows(block):
    rows, columns = block.shape
    return jnp.sum(block.reshape(rows // 8, 8, columns), axis=0)


def project_tokens(x, w_qkv, bias_row, qkv, rows):
    columns = w_qkv.shape[1]

    def body(index):
        here = at(index * WIDE, WIDE)
        qkv[rows, here] = (dot(x[rows, :], w_qkv[:, here]) + bias_row[0:1, here]).astype(BF)

    loop(columns // WIDE, body)


def fill_reward(reward, seg_row, count):
    text = seg_row.shape[1]
    segs = reward.shape[0] - text
    key = lax.broadcasted_iota(jnp.int32, (segs, text), 0)
    match = jnp.where(key == seg_row, LAYOUT_REWARD * LOG2E, 0.0).astype(F32)
    dead = jnp.where(key >= count, BLOCKED_SCORE * LOG2E, 0.0).astype(F32)
    turned = jnp.transpose(match)
    reward[...] = jnp.zeros_like(reward)
    slots = text + segs
    for head in range(2):
        reward[text:slots, head * slots : head * slots + text] = match + dead
        reward[text:slots, head * slots + text : (head + 1) * slots] = dead[:, :segs]
        reward[0:text, head * slots + text : (head + 1) * slots] = turned


def split_heads(block, both):
    slots = block.shape[0]
    first = lax.broadcasted_iota(jnp.int32, block.shape, 1) < HEAD
    zero = jnp.zeros_like(block)
    both[0:slots, :] = jnp.where(first, block, zero)
    both[slots:, :] = jnp.where(first, zero, block)


def attend(qkv, reward, probs_of, context_t, both, turned, side):
    slots, features = qkv.shape[0], qkv.shape[1] // 3
    pairs = features // PAIR
    scaling = HEAD ** (-0.5) * LOG2E

    def pair_step(pair):
        here = at(pair * PAIR, PAIR)
        keys = qkv[:, at(features + pair * PAIR, PAIR)]
        split_heads(qkv[:, here], both)
        turned[...] = jnp.transpose(qkv[:, at(2 * features + pair * PAIR, PAIR)])
        probs = probs_of(pair)

        for chunk in range(2 * slots // WIDE):
            block = slice(chunk * WIDE, (chunk + 1) * WIDE)
            scores = dot_nt(keys, both[block, :]) * scaling + reward[:, block]
            scores = jnp.exp2(scores - jnp.max(scores, axis=0, keepdims=True))
            probs[:, block] = (scores * (1.0 / jnp.sum(scores, axis=0, keepdims=True))).astype(BF)
        side[...] = dot(turned[...], probs[...]).astype(BF)
        context_t[at(pair * PAIR, HEAD), :] = side[:HEAD, :slots]
        context_t[at(pair * PAIR + HEAD, HEAD), :] = side[HEAD:, slots:]

    return pair_step, pairs


def first_norm(x, attended, bias, gain, shift, normal, root, low, rows):
    def body(index):
        here = at(index * rows, rows)
        hidden = x[here, :].astype(F32) + (attended[here, :] + bias[...])
        centre = hidden - jnp.mean(hidden, axis=1, keepdims=True)
        inverse = lax.rsqrt(jnp.mean(centre * centre, axis=1, keepdims=True) + NORM_EPS)
        unit = centre * inverse
        normal[here, :] = unit
        root[here, :] = jnp.broadcast_to(inverse, (rows, PAIR))
        low[here, :] = (unit * gain[...] + shift[...]).astype(BF)

    loop(x.shape[0] // rows, body)


def gate(inner):
    normal = 0.5 * (1.0 + lax.erf(inner * 0.7071067811865476))
    density = jnp.exp2(inner * inner * (-0.5 * LOG2E)) * 0.3989422804014327
    return inner * normal, normal + inner * density


def feed_forward(low, w_inner, b_inner, hidden, slope):
    def body(index):
        here = at(index * WIDE, WIDE)
        value, grade = gate(dot(low[...], w_inner[:, here]) + b_inner[0:1, here])
        hidden[:, here] = value.astype(BF)
        slope[:, here] = grade.astype(BF)

    loop(w_inner.shape[1] // WIDE, body)


def second_norm(normal, first_gain, first_shift, mlp, bias, gain, shift, cotangent, output, grad, grad_low, sums, rows):
    sums[0:3] = jnp.zeros((3,) + sums.shape[1:], F32)

    def body(index):
        here = at(index * rows, rows)
        one = normal[here, :] * first_gain[...] + first_shift[...]
        total = one + (mlp[here, :] + bias[...])
        centre = total - jnp.mean(total, axis=1, keepdims=True)
        inverse = lax.rsqrt(jnp.mean(centre * centre, axis=1, keepdims=True) + NORM_EPS)
        unit = centre * inverse
        pull = cotangent[here, :].astype(F32)
        output[here, :] = (unit * gain[...] + shift[...]).astype(BF)
        scaled = pull * gain[...]
        back = inverse * (
            scaled
            - jnp.mean(scaled, axis=1, keepdims=True)
            - unit * jnp.mean(scaled * unit, axis=1, keepdims=True)
        )
        rounded = back.astype(BF)
        grad[here, :] = back
        grad_low[here, :] = rounded
        sums[0] += fold_rows(pull * unit)
        sums[1] += fold_rows(pull)
        sums[2] += fold_rows(rounded.astype(F32))

    loop(normal.shape[0] // rows, body)


def first_norm_back(grad_second, back, normal, root, gain, grad_first, grad_low, sums, rows):
    sums[3:6] = jnp.zeros((3,) + sums.shape[1:], F32)

    def body(index):
        here = at(index * rows, rows)
        pull = grad_second[here, :] + back[here, :]
        unit = normal[here, :]
        scaled = pull * gain[...]
        inverse = root[here, 0:1]
        first = inverse * (
            scaled
            - jnp.mean(scaled, axis=1, keepdims=True)
            - unit * jnp.mean(scaled * unit, axis=1, keepdims=True)
        )
        rounded = first.astype(BF)
        grad_first[here, :] = first
        grad_low[here, :] = rounded
        sums[3] += fold_rows(pull * unit)
        sums[4] += fold_rows(pull)
        sums[5] += fold_rows(rounded.astype(F32))

    loop(normal.shape[0] // rows, body)


def attend_back(qkv, grad_context, probs_of, grad_qkv, both, both_grad, turned, scores, side, points):
    slots, features = qkv.shape[0], qkv.shape[1] // 3
    scaling = HEAD ** (-0.5)

    def pair_step(pair):
        here = at(pair * PAIR, PAIR)
        there = at(features + pair * PAIR, PAIR)
        last = at(2 * features + pair * PAIR, PAIR)
        split_heads(qkv[:, here], both)
        split_heads(grad_context[:, here], both_grad)
        turned[...] = jnp.transpose(qkv[:, there])
        values = qkv[:, last]
        probs = probs_of(pair)
        for chunk in range(2 * slots // WIDE):
            block = slice(chunk * WIDE, (chunk + 1) * WIDE)
            pull = dot_nt(values, both_grad[block, :])
            weight = probs[:, block].astype(F32)
            mean = jnp.sum(weight * pull, axis=0, keepdims=True)
            low = (weight * (pull - mean)).astype(BF)
            scores[:, block] = low
            if chunk == 2:
                points("u", pair)
        points("v", pair)
        side[...] = dot(turned[...], scores[...])
        grad_qkv[:, there] = (dot(scores[...], both[...]) * scaling).astype(BF)
        grad_qkv[:, last] = dot(probs[...], both_grad[...]).astype(BF)
        mine = jnp.concatenate([side[:HEAD, :slots], side[HEAD:, slots:]], axis=0)
        grad_qkv[:, here] = jnp.transpose(mine * scaling).astype(BF)

    return pair_step, features // PAIR


PARTS = 16
MESH = pl.DeviceIdType.MESH
UNIT_ROWS = 48
UNITS = 12
WEIGHT = {"c": 1, "y": 2, "l": 4, "h": 8}
ORDERS = (
    "cylhxg",
    "cylxhg",
    "cxylhg",
    "cxylhg",
    "clxhyg",
    "cyxlhg",
    "cyxlhg",
    "clyhxg",
    "cylxhg",
    "cxlhyg",
    "cylxhg",
    "cylxhg",
)
SMALL_ORDER = "cylhx"
SWAP = 0


def partner_of(bit, me, seq):
    if bit in "xg":
        return (me, 1 - seq)
    weight = WEIGHT[bit]
    return (me + weight * (1 - 2 * ((me // weight) % 2)), seq)


def stage_shapes(order, rows, columns):
    bits, shapes = 4, []
    for bit in order:
        if bit == "x":
            columns //= 2
        elif bit != "g":
            bits -= 1
        shapes.append((2,) * bits + (rows, columns))
    return shapes


def add_into(target, other):
    lead = target.shape[:-2]
    total = 1
    for size in lead:
        total *= size

    def step(index, carry):
        place, rest = [], index
        for size in reversed(lead):
            place.append(rest % size)
            rest = rest // size
        place = tuple(reversed(place)) + (slice(None), slice(None))
        target[place] = target[place] + other[place]
        return carry

    if total == 1:
        step(0, 0)
    else:
        lax.fori_loop(0, total, step, 0)


class Unit:
    def __init__(self, number, source, order, buffers, sends, recvs, me, seq):
        self.number, self.source, self.order, self.buffers = number, source, order, buffers
        self.sends, self.recvs, self.me, self.seq = sends, recvs, me, seq

    def at_stage(self, stage):
        bits = ["h", "l", "y", "c"]
        for bit in self.order[:stage]:
            if bit in bits:
                bits.remove(bit)
        current = self.buffers[stage - 1] if stage else self.source
        bit = self.order[stage]
        if bit == "g":
            return current, None
        if bit == "x":
            size = current.shape[-1] // 2
            lead = (slice(None),) * (len(bits) + 1)
            own = current.at[lead + (pl.ds(pl.multiple_of(self.seq * size, PAIR), size),)]
            return current.at[lead + (pl.ds(pl.multiple_of((1 - self.seq) * size, PAIR), size),)], own
        mine = (self.me // WEIGHT[bit]) % 2
        lead = (slice(None),) * bits.index(bit)
        return current.at[lead + (1 - mine,)], current.at[lead + (mine,)]

    def copy(self, stage):
        return pltpu.make_async_remote_copy(
            src_ref=self.at_stage(stage)[0],
            dst_ref=self.buffers[stage],
            send_sem=self.sends.at[self.number, stage],
            recv_sem=self.recvs.at[self.number, stage],
            device_id=partner_of(self.order[stage], self.me, self.seq),
            device_id_type=MESH,
        )

    def advance(self, stage):
        self.copy(stage).wait()
        self.add(stage)

    def add(self, stage):
        kept = self.at_stage(stage)[1]
        if kept is not None:
            add_into(self.buffers[stage], kept)
        if stage + 1 < len(self.order):
            self.copy(stage + 1).start()


def with_stages(schedule):
    reached = [1] * 4 + [0] * (UNITS - 3)
    plan = {}
    for point, numbers in schedule:
        steps = plan.setdefault(point, [])
        for number in numbers:
            steps.append((number, reached[number]))
            reached[number] += 1
    return plan


def layer_kernel(
    tokens, cotangent, seg_align, seg_count,
    query_bias, value_bias, output_bias, first_gain, first_shift, outer_bias, second_gain, second_shift, inner_bias,
    w_qkv, w_out, w_inner, w_outer,
    block_output, tokens_grad, shards, sums_out, probs_hbm,
    vectors, x, qkv, context_t, w_out_v, normal, root, cot, acc, grad_att, sums, own, small, small_got, *rest,
):
    rest = list(rest)
    buffers = [[rest.pop(0) for _ in ORDERS[0][:-1]] for _ in range(UNITS)]
    unit_send, unit_recv, outer_send, outer_recv, local_sem, pair_sem, swap_send, swap_recv, small_send, small_recv, vector_sem, shard_sem, chunk_send, chunk_recv = rest
    slots, features = x.shape
    half = slots // 2
    wide = w_inner.shape[1]
    me, seq = lax.axis_index("dp"), lax.axis_index("seq")
    core = me % 2
    mine, other = at(seq * half, half), at((1 - seq) * half, half)
    b_out, gain1, shift1, b_outer, gain2, shift2 = (vectors.at[i : i + 1] for i in range(3, 9))
    columns = [slice(c * WIDE, (c + 1) * WIDE) for c in range(features // WIDE)]

    barrier = pltpu.get_barrier_semaphore()
    for bit in "xcylh":
        pl.semaphore_signal(barrier, inc=1, device_id=partner_of(bit, me, seq), device_id_type=MESH)

    def local(source, target, index):
        return pltpu.make_async_copy(source, target, local_sem.at[index])

    def swap(source, target, index):
        return pltpu.make_async_remote_copy(
            src_ref=source, dst_ref=target, send_sem=swap_send.at[index], recv_sem=swap_recv.at[index],
            device_id=(me, 1 - seq), device_id_type=MESH)

    keep_tokens = local(tokens.at[seq], x.at[mine], 0)
    keep_cot = local(cotangent.at[seq], cot.at[mine], 1)
    load_out = local(w_out, w_out_v, 2)
    swap_tokens = swap(tokens.at[1 - seq], x.at[mine], 0)
    swap_cot = swap(cotangent.at[1 - seq], cot.at[mine], 1)
    keep_output = local(cot.at[mine], block_output.at[seq], 3)
    swap_output = swap(cot.at[other], block_output.at[seq], 2)
    keep_grad = local(x.at[mine], tokens_grad.at[seq], 4)
    swap_grad = swap(x.at[other], tokens_grad.at[seq], 3)
    keep_tokens.start()
    rows_of = {0: query_bias, 2: value_bias, 3: output_bias, 4: first_gain, 5: first_shift, 6: outer_bias, 7: second_gain, 8: second_shift}
    load_vectors = [pltpu.make_async_copy(ref, vectors.at[i], vector_sem.at[i]) for i, ref in rows_of.items()]
    load_vectors += [
        pltpu.make_async_copy(inner_bias.at[pl.ds(i * features, features)], vectors.at[9 + i], vector_sem.at[9 + i])
        for i in range(wide // features)
    ]
    for copy in load_vectors:
        copy.start()
    vectors[1:2] = jnp.zeros((1, features), F32)

    units = [
        Unit(n, own.at[n if n < 8 else n - 8], ORDERS[n], buffers[n] + [shards.at[n, seq]], unit_send, unit_recv, me, seq)
        for n in range(UNITS)
    ]

    def keep_shard(number):
        return pltpu.make_async_copy(buffers[number][-1], shards.at[number, seq], shard_sem.at[number])

    def outer_copy(j, sub):
        hi, lo = j // 2, j % 2
        return pltpu.make_async_remote_copy(
            src_ref=own.at[sub, hi, lo, :, 1 - core],
            dst_ref=buffers[sub][0].at[hi, lo],
            send_sem=outer_send.at[j, sub], recv_sem=outer_recv.at[j, sub],
            device_id=partner_of("c", me, seq), device_id_type=MESH)

    def chunk_copy(j, sub):
        bit, held = ORDERS[sub][1], buffers[sub][0].at[j // 2, j % 2]
        if bit == "x":
            size = features // 2
            given = held.at[:, :, pl.ds(pl.multiple_of((1 - seq) * size, PAIR), size)]
        else:
            given = held.at[1 - (me // WEIGHT[bit]) % 2]
        return pltpu.make_async_remote_copy(
            src_ref=given,
            dst_ref=buffers[sub][1].at[j // 2, j % 2],
            send_sem=chunk_send.at[j, sub], recv_sem=chunk_recv.at[j, sub],
            device_id=partner_of(bit, me, seq), device_id_type=MESH)

    def take_chunk(j):
        for sub in range(4):
            outer_copy(j, sub).wait()
            add_into(buffers[sub][0].at[j // 2, j % 2], own.at[sub, j // 2, j % 2, :, core])
            chunk_copy(j, sub).start()

    def small_copy(stage):
        return pltpu.make_async_remote_copy(
            src_ref=small, dst_ref=small_got.at[stage], send_sem=small_send.at[stage], recv_sem=small_recv.at[stage],
            device_id=partner_of(SMALL_ORDER[stage], me, seq), device_id_type=MESH)

    def advance(number, stage):
        if number == UNITS:
            small_copy(stage).wait()
            small[...] += small_got[stage]
            if stage + 1 < len(SMALL_ORDER):
                small_copy(stage + 1).start()
        elif number < 4 and stage == 1:
            for j in range(4):
                chunk_copy(j, number).wait()
            units[number].add(1)
        else:
            units[number].advance(stage)
        if number < UNITS and stage == 4:
            keep_shard(number).start()

    plan = with_stages(SCHEDULE)

    def point(name):
        for number, stage in plan.get(name, ()):
            advance(number, stage)

    def points(name, index, count):
        for i in range(count):
            if (name, i) in plan:
                pl.when(index == i)(functools.partial(point, (name, i)))

    def forward(w_inner_v, w_outer_v):
        load_inner, load_outer = local(w_inner, w_inner_v, 5), local(w_outer, w_outer_v, 6)

        def attention(w_qkv_v, reward, both, turned, side, probs_buf):
            load_qkv = local(w_qkv, w_qkv_v, 7)
            load_qkv.start()
            pl.semaphore_wait(barrier, 5)
            swap_tokens.start()
            load_out.start()
            fill_reward(reward, seg_align[pl.ds(seq, 1), :], seg_count[seq])
            keep_tokens.wait()
            for copy in load_vectors:
                copy.wait()
            load_qkv.wait()

            def project(rows):
                def body(index):
                    here = at(index * features, features)
                    bias = vectors[pl.ds(index, 1), :]
                    qkv[rows, here] = (dot(x[rows, :], w_qkv_v[:, here]) + bias).astype(BF)

                loop(3, body)

            project(mine)
            load_inner.start()
            load_outer.start()
            keep_cot.start()
            swap_tokens.wait()
            swap_cot.start()
            project(other)
            step, pairs = attend(qkv, reward, lambda pair: probs_buf.at[pair % 2], context_t, both, turned, side)

            def out_copy(pair):
                return pltpu.make_async_copy(probs_buf.at[pair % 2], probs_hbm.at[pair], pair_sem.at[pair % 2])

            def body(pair):
                @pl.when(pair >= 2)
                def _():
                    out_copy(pair - 2).wait()

                step(pair)
                out_copy(pair).start()

            loop(pairs, body)
            out_copy(pairs - 2).wait()
            out_copy(pairs - 1).wait()

        pl.run_scoped(
            attention,
            pltpu.VMEM((features, 3 * features), BF),
            pltpu.VMEM((slots, 2 * slots), F32),
            pltpu.VMEM((2 * slots, PAIR), BF),
            pltpu.VMEM((PAIR, slots), BF),
            pltpu.VMEM((PAIR, 2 * slots), BF),
            pltpu.VMEM((2, slots, 2 * slots), BF),
        )

        def mlp(low, turned_low, hidden, slope, grad_second):
            low[...] = jnp.transpose(context_t[...])
            load_out.wait()
            for here in columns:
                acc[:, here] = dot(low[...], w_out_v[:, here])
            first_norm(x, acc, b_out, gain1, shift1, normal, root, low, 160)
            load_inner.wait()

            def inner_body(index):
                here = at(index * features, features)
                bias = vectors[pl.ds(9 + index, 1), :]
                value, grade = gate(dot(low[...], w_inner_v[:, here]) + bias)
                hidden[:, here] = value.astype(BF)
                slope[:, here] = grade.astype(BF)

            loop(wide // features, inner_body)
            load_outer.wait()
            for here in columns:
                acc[:, here] = dot(hidden[...], w_outer_v[:, here])
            keep_cot.wait()
            swap_cot.wait()
            second_norm(normal, gain1, shift1, acc, b_outer, gain2, shift2, cot, cot, grad_second, grad_att, sums, 160)
            keep_output.start()


            def outer_step(j):
                block = dot_tn(hidden[:, at(j * features, features)], grad_att[...]).astype(BF)
                block = block.reshape(2, 2, 4, UNIT_ROWS, features)
                for sub in range(4):
                    own[sub, j // 2, j % 2] = block[:, :, sub]
                for sub in range(4):
                    outer_copy(j, sub).start()
                pl.when(j >= 2)(lambda: take_chunk(j - 2))

            loop(4, outer_step)
            take_chunk(2)
            turned_low[...] = jnp.transpose(low[...])
            take_chunk(3)

            def inner_step(j):
                here = at(j * features, features)
                low_grad = (
                    dot_nt(grad_att[...], w_outer_v[here, :]) * slope[:, here].astype(F32)
                ).astype(BF)
                hidden[:, here] = low_grad
                sums[8 + j] = fold_rows(low_grad.astype(F32))
                points("g", j, 4)
                block = dot(turned_low[...], hidden[:, here]).astype(BF)
                own[4 + j] = block.reshape(2, 2, 2, 2, UNIT_ROWS, features)
                for i in range(4):
                    pl.when(j == i)(lambda i=i: units[4 + i].copy(0).start())
                points("i", j, 4)

            loop(4, inner_step)
            swap_output.start()
            for c, here in enumerate(columns):
                acc[:, here] = dot_nt(hidden[...], w_inner_v[here, :])
                point(("a", c))
            first_norm_back(grad_second, acc, normal, root, gain1, acc, grad_att, sums, 160)

        pl.run_scoped(
            mlp,
            pltpu.VMEM((slots, features), BF),
            pltpu.VMEM((features, slots), BF),
            pltpu.VMEM((slots, wide), BF),
            pltpu.VMEM((slots, wide), BF),
            pltpu.VMEM((slots, features), F32),
        )

    pl.run_scoped(forward, pltpu.VMEM(w_inner.shape, BF), pltpu.VMEM(w_outer.shape, BF))

    def back(w_qkv_v, both, both_grad, turned, scores, side, probs_buf, grad_ctx, grad_qkv, turned_x):
        load_qkv = local(w_qkv, w_qkv_v, 8)
        load_qkv.start()

        def in_copy(pair):
            return pltpu.make_async_copy(probs_hbm.at[pair], probs_buf.at[pair % 2], pair_sem.at[pair % 2])

        in_copy(0).start()
        point(("n", 0))
        for c, here in enumerate(columns):
            block = dot(context_t[...], grad_att[:, here]).astype(BF)
            own[0, :, :, :, :, :, here] = block.reshape(2, 2, 2, 2, UNIT_ROWS, WIDE)
        units[8].copy(0).start()
        point(("o", 0))
        for c, here in enumerate(columns):
            grad_ctx[:, here] = dot_nt(grad_att[...], w_out_v[here, :]).astype(BF)
        turned_x[...] = jnp.transpose(x[...])
        point(("o", 1))
        step, pairs = attend_back(
            qkv, grad_ctx, lambda pair: probs_buf.at[pair % 2], grad_qkv, both, both_grad, turned, scores, side,
            lambda name, pair: points(name, pair, pairs))

        def body(pair):
            @pl.when(pair + 1 < pairs)
            def _():
                in_copy(pair + 1).start()

            in_copy(pair).wait()
            step(pair)
            points("r", pair, pairs)

            @pl.when(pair % 2 == 1)
            def _():
                group = pair // 2
                for part in range(3):
                    there = at(part * features + group * WIDE, WIDE)
                    block = dot(turned_x[...], grad_qkv[:, there]).astype(BF)
                    own[1 + group, :, :, :, :, :, part * WIDE : (part + 1) * WIDE] = block.reshape(
                        2, 2, 2, 2, UNIT_ROWS, WIDE)
                for i in range(3):
                    pl.when(group == i)(lambda i=i: units[9 + i].copy(0).start())

            points("s", pair, pairs)

        loop(pairs, body)
        sums[6] = fold_rows(grad_qkv[:, :features].astype(F32))
        sums[7] = fold_rows(grad_qkv[:, 2 * features :].astype(F32))
        small[...] = jnp.sum(sums[...], axis=1)
        small_copy(0).start()
        load_qkv.wait()
        for side_index, rows in enumerate((other, mine)):
            for c, here in enumerate(columns):
                x[rows, here] = (acc[rows, here] + dot_nt(grad_qkv[rows, :], w_qkv_v[here, :])).astype(BF)
                point(("t", side_index * 3 + c))
            (swap_grad if side_index == 0 else keep_grad).start()

    pl.run_scoped(
        back,
        pltpu.VMEM((features, 3 * features), BF),
        pltpu.VMEM((2 * slots, PAIR), BF),
        pltpu.VMEM((2 * slots, PAIR), BF),
        pltpu.VMEM((PAIR, slots), BF),
        pltpu.VMEM((slots, 2 * slots), BF),
        pltpu.VMEM((PAIR, 2 * slots), F32),
        pltpu.VMEM((2, slots, 2 * slots), BF),
        pltpu.VMEM((slots, features), BF),
        pltpu.VMEM((slots, 3 * features), BF),
        pltpu.VMEM((features, slots), BF),
    )
    point(("end", 0))
    keep_output.wait()
    swap_output.wait()
    keep_grad.wait()
    swap_grad.wait()
    for number in range(UNITS):
        keep_shard(number).wait()
    sums_out[...] = small[...]


def finish_kernel(
    block_in, grad_in, shards, sums,
    block_output, tokens_grad, g_qkv, g_query, g_value, g_out, g_out_bias, g_gain1, g_shift1, g_inner, g_inner_bias,
    g_outer, g_outer_bias, g_gain2, g_shift2, passed, sem,
):
    ins, outs = [], []
    for index, (source, target) in enumerate(((block_in, block_output), (grad_in, tokens_grad))):
        for part in range(2):
            buffer, number = passed.at[index, part], 2 * index + part
            ins.append(pltpu.make_async_copy(source.at[part], buffer, sem.at[0, number]))
            outs.append(pltpu.make_async_copy(buffer, target.at[part], sem.at[1, number]))
    for copy in ins:
        copy.start()
    for copy, onward in zip(ins, outs):
        copy.wait()
        onward.start()
    me = lax.axis_index("dp")
    features = sums.shape[1]
    size = features // 2
    for number in range(UNITS):
        for place in range(2):
            value = shards[number, place].astype(F32)
            start = place * size
            if number < 4:
                g_outer[number * UNIT_ROWS : (number + 1) * UNIT_ROWS, start : start + size] = value
            elif number < 8:
                start += (number - 4) * features
                g_inner[:, start : start + size] = value
            elif number == 8:
                g_out[:, start : start + size] = value
            else:
                for piece in range(size // PAIR):
                    column = start + piece * PAIR
                    target = column // WIDE * features + (number - 9) * WIDE + column % WIDE
                    g_qkv[:, target : target + PAIR] = value[:, piece * PAIR : (piece + 1) * PAIR]
    rows = pltpu.roll(sums[0:8], (features - me * UNIT_ROWS) % features, 1)
    for index, out in enumerate((g_gain2, g_shift2, g_outer_bias, g_gain1, g_shift1, g_out_bias, g_query, g_value)):
        out[...] = rows[index, :UNIT_ROWS]
    share = 4 * UNIT_ROWS
    place = me * share
    line = pltpu.roll(sums[pl.ds(8 + place // features, 1)], (features - place % features) % features, 1)
    g_inner_bias[...] = line[0, :share]
    for copy in outs:
        copy.wait()


def finish(block, grad, shards, sums, wide):
    features = block.shape[-1]
    S = jax.ShapeDtypeStruct
    vector = S((UNIT_ROWS,), F32)
    hbm, vmem = pl.BlockSpec(memory_space=pltpu.HBM), pl.BlockSpec(memory_space=pltpu.VMEM)
    return pl.pallas_call(
        finish_kernel,
        name="finish",
        out_shape=[
            S(block.shape, BF), S(grad.shape, BF), S((UNIT_ROWS, 3 * features), F32), vector, vector,
            S((UNIT_ROWS, features), F32), vector, vector, vector, S((UNIT_ROWS, wide), F32), S((4 * UNIT_ROWS,), F32),
            S((4 * UNIT_ROWS, features), F32), vector, vector, vector,
        ],
        in_specs=[hbm, hbm, vmem, vmem],
        out_specs=[hbm, hbm] + [vmem] * 13,
        scratch_shapes=[pltpu.VMEM((2,) + block.shape, BF), pltpu.SemaphoreType.DMA((2, 4))],
        compiler_params=pltpu.CompilerParams(vmem_limit_bytes=60 * 2**20),
    )(block, grad, shards, sums)


def layer(tokens, cotangent, seg_align, seg_count, vectors, w_qkv, w_out, w_inner, w_outer):
    documents, half, features = tokens.shape
    slots, wide = 2 * half, w_inner.shape[1]
    pairs = features // PAIR
    S, V, D = jax.ShapeDtypeStruct, pltpu.VMEM, pltpu.SemaphoreType.DMA
    scratch = [
        V((16, features), F32), V((slots, features), BF), V((slots, 3 * features), BF), V((features, slots), BF), V(w_out.shape, BF),
        V((slots, features), F32), V((slots, PAIR), F32), V((slots, features), BF), V((slots, features), F32),
        V((slots, features), BF), V((16, 8, features), F32), V((8, 2, 2, 2, 2, UNIT_ROWS, features), BF),
        V((16, features), F32), V((len(SMALL_ORDER), 16, features), F32),
    ]
    for number in range(UNITS):
        scratch += [V(shape, BF) for shape in stage_shapes(ORDERS[number], UNIT_ROWS, features)[:-1]]
    scratch += [D((UNITS, 6)), D((UNITS, 6)), D((4, 4)), D((4, 4)), D((9,)), D((2,)), D((4,)), D((4,)), D((5,)), D((5,)), D((16,)), D((UNITS,)), D((4, 4)), D((4, 4))]
    hbm, vmem = pl.BlockSpec(memory_space=pltpu.HBM), pl.BlockSpec(memory_space=pltpu.VMEM)
    return pl.pallas_call(
        layer_kernel,
        name="layer",
        out_shape=[
            S(tokens.shape, BF), S(tokens.shape, BF), S((UNITS, 2, UNIT_ROWS, features // 2), BF), S((16, features), F32),
            S((pairs, slots, 2 * slots), BF),
        ],
        in_specs=[hbm, hbm, vmem, pl.BlockSpec(memory_space=pltpu.SMEM)] + [hbm] * 13,
        out_specs=[hbm, hbm, hbm, vmem, hbm],
        scratch_shapes=scratch,
        compiler_params=pltpu.CompilerParams(collective_id=0, has_side_effects=True, vmem_limit_bytes=60 * 2**20),
    )(tokens, cotangent, seg_align, seg_count, *vectors, w_qkv, w_out, w_inner, w_outer)


SCHEDULE = (
    (("i", 2), (4,)),
    (("i", 3), (5,)),
    (("a", 0), (0, 2, 6, 1, 3)),
    (("a", 1), (7,)),
    (("n", 0), (4,)),
    (("o", 1), (5, 0)),
    (("u", 0), (8,)),
    (("v", 0), (2,)),
    (("r", 0), (1,)),
    (("s", 1), (4,)),
    (("u", 2), (6,)),
    (("v", 2), (7, 5)),
    (("u", 3), (9, 1, 3)),
    (("v", 3), (0, 2)),
    (("s", 3), (6,)),
    (("u", 4), (4, 5)),
    (("r", 4), (1,)),
    (("u", 5), (10, 8, 3)),
    (("v", 5), (2,)),
    (("r", 5), (6, 9)),
    (("s", 5), (7, 0, 4, 5, 1)),
    (("t", 0), (2,)),
    (("t", 3), (8,)),
    (("t", 4), (11, 0, 12)),
    (("t", 5), (4, 3)),
    (("end", 0), (5, 6, 10, 9, 7, 11, 10, 12, 9, 8, 3, 11, 6, 9, 12, 7, 8, 10, 11, 12, 9, 7, 10, 8, 11, 12, 10, 11)),
)


def slot_groups(seg_count, seg_align, all_slots):
    doc_count, text_slots = seg_align.shape
    slot_index = jnp.arange(all_slots, dtype=jnp.int32)
    filler = jnp.zeros((doc_count, all_slots - text_slots), jnp.int32)
    padded = jnp.concatenate([seg_align, filler], axis=1)
    is_text = slot_index < text_slots
    groups = jnp.where(is_text[None, :], padded, (slot_index - text_slots)[None, :])
    present_keys = slot_index[None, :] < text_slots + seg_count[:, None]
    return (groups, is_text, present_keys)


def layer_norm(hidden, gain, shift):
    centre = hidden - jnp.mean(hidden, axis=-1, keepdims=True)
    spread = jnp.mean(centre * centre, axis=-1, keepdims=True)
    return centre * lax.rsqrt(spread + NORM_EPS) * gain + shift


def smooth_gate(inner):
    return jax.nn.gelu(inner, approximate=False)


def softmax_rows(logit_scores):
    return jax.nn.softmax(logit_scores, axis=-1)


def project(tokens, qkv_weight, query_bias, value_bias):
    doc_count, slot_count, features = tokens.shape
    token_rows = tokens.reshape(doc_count * slot_count, features)
    pre = jnp.dot(token_rows, qkv_weight, preferred_element_type=jnp.float32)
    queries = (pre[:, :features] + query_bias).astype(jnp.bfloat16)
    own_keys = (
        pre[:, features : 2 * features]
        .astype(jnp.bfloat16)
        .reshape(doc_count, slot_count, features)
    )
    own_values = (
        (pre[:, 2 * features :] + value_bias)
        .astype(jnp.bfloat16)
        .reshape(doc_count, slot_count, features)
    )
    all_keys, values = (
        lax.all_gather(own_keys, "seq", axis=1, tiled=True),
        lax.all_gather(own_values, "seq", axis=1, tiled=True),
    )
    return (queries, all_keys, values)


def plain(
    tokens,
    seg_count,
    seg_align,
    cotangent,
    qkv_weight,
    query_bias,
    value_bias,
    output_weight,
    output_bias,
    first_gain,
    first_shift,
    inner_weight,
    inner_bias,
    outer_weight,
    outer_bias,
    second_gain,
    second_shift,
):
    doc_count, slot_count, features = tokens.shape
    row_count = doc_count * slot_count
    head_dim = features // H
    scaling = head_dim ** (-0.5)
    all_slots = slot_count * lax.axis_size("seq")
    row_start = lax.axis_index("seq") * slot_count
    groups, is_text, present_keys = slot_groups(seg_count, seg_align, all_slots)
    group_rows = lax.dynamic_slice_in_dim(groups, row_start, slot_count, 1)
    text_rows = lax.dynamic_slice_in_dim(is_text, row_start, slot_count, 0)
    matched_pairs = (group_rows[:, :, None] == groups[:, None, :]) & (
        text_rows[None, :, None] != is_text[None, None, :]
    )
    layout_reward = LAYOUT_REWARD * matched_pairs.astype(jnp.float32)
    queries, all_keys, values = project(tokens, qkv_weight, query_bias, value_bias)
    query_heads = queries.reshape(doc_count, slot_count, H, head_dim)
    key_heads = all_keys.reshape(doc_count, all_slots, H, head_dim)
    value_heads = values.reshape(doc_count, all_slots, H, head_dim)
    unadjusted_scores = (
        jnp.einsum("bqhd,bkhd->bhqk", query_heads, key_heads, preferred_element_type=jnp.float32)
        * scaling
    )
    logit_scores = jnp.where(
        present_keys[:, None, None, :], unadjusted_scores + layout_reward[:, None], BLOCKED_SCORE
    )
    attn_probs, soft_pull = jax.vjp(softmax_rows, logit_scores)
    probs_low = attn_probs.astype(jnp.bfloat16)
    context = jnp.einsum(
        "bhqk,bkhd->bqhd", probs_low, value_heads, preferred_element_type=jnp.float32
    )
    context = context.reshape(row_count, features).astype(jnp.bfloat16)
    token_rows = tokens.reshape(row_count, features)
    attended = jnp.dot(context, output_weight, preferred_element_type=jnp.float32) + output_bias
    normed_one, first_pull = jax.vjp(
        layer_norm, token_rows.astype(jnp.float32) + attended, first_gain, first_shift
    )
    normed_low = normed_one.astype(jnp.bfloat16)
    inner = jnp.dot(normed_low, inner_weight, preferred_element_type=jnp.float32) + inner_bias
    activated, gate_pull = jax.vjp(smooth_gate, inner)
    hidden = activated.astype(jnp.bfloat16)
    mlp_out = jnp.dot(hidden, outer_weight, preferred_element_type=jnp.float32) + outer_bias
    layer_out, second_pull = jax.vjp(layer_norm, normed_one + mlp_out, second_gain, second_shift)
    grad_out = cotangent.reshape(row_count, features).astype(jnp.float32)
    grad_second, second_gain_grad, second_shift_grad = second_pull(grad_out)
    grad_mlp = grad_second.astype(jnp.bfloat16)
    outer_weight_grad = jnp.einsum(
        "rf,rd->fd", hidden, grad_mlp, preferred_element_type=jnp.float32
    )
    outer_bias_grad = jnp.sum(grad_mlp.astype(jnp.float32), axis=0)
    grad_hidden = jnp.einsum(
        "rd,fd->rf", grad_mlp, outer_weight, preferred_element_type=jnp.float32
    )
    grad_inner = gate_pull(grad_hidden)[0].astype(jnp.bfloat16)
    inner_weight_grad = jnp.einsum(
        "rd,rf->df", normed_low, grad_inner, preferred_element_type=jnp.float32
    )
    inner_bias_grad = jnp.sum(grad_inner.astype(jnp.float32), axis=0)
    grad_normed = grad_second + jnp.einsum(
        "rf,df->rd", grad_inner, inner_weight, preferred_element_type=jnp.float32
    )
    grad_first, first_gain_grad, first_shift_grad = first_pull(grad_normed)
    grad_attended = grad_first.astype(jnp.bfloat16)
    output_weight_grad = jnp.einsum(
        "rc,rd->cd", context, grad_attended, preferred_element_type=jnp.float32
    )
    output_bias_grad = jnp.sum(grad_attended.astype(jnp.float32), axis=0)
    grad_context = jnp.einsum(
        "rd,cd->rc", grad_attended, output_weight, preferred_element_type=jnp.float32
    )
    grad_context = grad_context.astype(jnp.bfloat16).reshape(doc_count, slot_count, H, head_dim)
    grad_probs = jnp.einsum(
        "bqhd,bkhd->bhqk", grad_context, value_heads, preferred_element_type=jnp.float32
    )
    grad_scores = soft_pull(grad_probs)[0].astype(jnp.bfloat16)
    grad_queries = (
        jnp.einsum("bhqk,bkhd->bqhd", grad_scores, key_heads, preferred_element_type=jnp.float32)
        * scaling
    )
    grad_queries = grad_queries.astype(jnp.bfloat16).reshape(row_count, features)
    key_term = (
        jnp.einsum("bhqk,bqhd->bkhd", grad_scores, query_heads, preferred_element_type=jnp.float32)
        * scaling
    )
    value_term = jnp.einsum(
        "bhqk,bqhd->bkhd", probs_low, grad_context, preferred_element_type=jnp.float32
    )
    key_sum, value_sum = (
        lax.psum_scatter(
            key_term.reshape(doc_count, all_slots, features).astype(jnp.bfloat16),
            "seq",
            scatter_dimension=1,
            tiled=True,
        ).astype(jnp.float32),
        lax.psum_scatter(
            value_term.reshape(doc_count, all_slots, features).astype(jnp.bfloat16),
            "seq",
            scatter_dimension=1,
            tiled=True,
        ).astype(jnp.float32),
    )
    grad_keys = key_sum.astype(jnp.bfloat16).reshape(row_count, features)
    grad_values = value_sum.astype(jnp.bfloat16).reshape(row_count, features)
    grad_project = jnp.concatenate([grad_queries, grad_keys, grad_values], axis=1)
    qkv_weight_grad = jnp.einsum(
        "rd,re->de", token_rows, grad_project, preferred_element_type=jnp.float32
    )
    query_bias_grad = jnp.sum(grad_queries.astype(jnp.float32), axis=0)
    value_bias_grad = jnp.sum(grad_values.astype(jnp.float32), axis=0)
    tokens_grad = grad_first + jnp.einsum(
        "re,de->rd", grad_project, qkv_weight, preferred_element_type=jnp.float32
    )
    tokens_grad = tokens_grad.astype(jnp.bfloat16).reshape(doc_count, slot_count, features)
    shares = (
        lax.psum_scatter(qkv_weight_grad, "dp", scatter_dimension=0, tiled=True),
        lax.psum_scatter(query_bias_grad, "dp", scatter_dimension=0, tiled=True),
        lax.psum_scatter(value_bias_grad, "dp", scatter_dimension=0, tiled=True),
        lax.psum_scatter(output_weight_grad, "dp", scatter_dimension=0, tiled=True),
        lax.psum_scatter(output_bias_grad, "dp", scatter_dimension=0, tiled=True),
        lax.psum_scatter(first_gain_grad, "dp", scatter_dimension=0, tiled=True),
        lax.psum_scatter(first_shift_grad, "dp", scatter_dimension=0, tiled=True),
        lax.psum_scatter(inner_weight_grad, "dp", scatter_dimension=0, tiled=True),
        lax.psum_scatter(inner_bias_grad, "dp", scatter_dimension=0, tiled=True),
        lax.psum_scatter(outer_weight_grad, "dp", scatter_dimension=0, tiled=True),
        lax.psum_scatter(outer_bias_grad, "dp", scatter_dimension=0, tiled=True),
        lax.psum_scatter(second_gain_grad, "dp", scatter_dimension=0, tiled=True),
        lax.psum_scatter(second_shift_grad, "dp", scatter_dimension=0, tiled=True),
    )
    summed = (
        lax.psum(shares[0].astype(jnp.bfloat16), "seq").astype(jnp.float32),
        lax.psum(shares[1].astype(jnp.bfloat16), "seq").astype(jnp.float32),
        lax.psum(shares[2].astype(jnp.bfloat16), "seq").astype(jnp.float32),
        lax.psum(shares[3].astype(jnp.bfloat16), "seq").astype(jnp.float32),
        lax.psum(shares[4].astype(jnp.bfloat16), "seq").astype(jnp.float32),
        lax.psum(shares[5].astype(jnp.bfloat16), "seq").astype(jnp.float32),
        lax.psum(shares[6].astype(jnp.bfloat16), "seq").astype(jnp.float32),
        lax.psum(shares[7].astype(jnp.bfloat16), "seq").astype(jnp.float32),
        lax.psum(shares[8].astype(jnp.bfloat16), "seq").astype(jnp.float32),
        lax.psum(shares[9].astype(jnp.bfloat16), "seq").astype(jnp.float32),
        lax.psum(shares[10].astype(jnp.bfloat16), "seq").astype(jnp.float32),
        lax.psum(shares[11].astype(jnp.bfloat16), "seq").astype(jnp.float32),
        lax.psum(shares[12].astype(jnp.bfloat16), "seq").astype(jnp.float32),
    )
    block_output = layer_out.astype(jnp.bfloat16).reshape(doc_count, slot_count, features)
    return (
        block_output,
        tokens_grad,
        summed[0],
        summed[1],
        summed[2],
        summed[3],
        summed[4],
        summed[5],
        summed[6],
        summed[7],
        summed[8],
        summed[9],
        summed[10],
        summed[11],
        summed[12],
    )


def local(
    tokens,
    seg_count,
    seg_align,
    cotangent,
    qkv_weight,
    query_bias,
    value_bias,
    output_weight,
    output_bias,
    first_gain,
    first_shift,
    inner_weight,
    inner_bias,
    outer_weight,
    outer_bias,
    second_gain,
    second_shift,
):
    dp, seq = lax.axis_size("dp"), lax.axis_size("seq")
    documents, _, features = tokens.shape
    if dp != PARTS or seq != 2 or documents != 2 or features != PARTS * UNIT_ROWS:
        return plain(
            tokens, seg_count, seg_align, cotangent, qkv_weight, query_bias, value_bias, output_weight, output_bias, first_gain, first_shift, inner_weight, inner_bias, outer_weight, outer_bias, second_gain, second_shift
        )
    vectors = (
        query_bias, value_bias, output_bias, first_gain, first_shift, outer_bias, second_gain, second_shift, inner_bias
    )
    block, grad, shards, sums, _ = layer(
        tokens, cotangent, seg_align, seg_count, vectors, qkv_weight, output_weight, inner_weight, outer_weight
    )
    return tuple(finish(block, grad, shards, sums, inner_weight.shape[1]))


def solution(mesh):
    return jax.shard_map(
        local,
        mesh=mesh,
        in_specs=(
            P("dp", "seq", None),
            P("dp"),
            P("dp", None),
            P("dp", "seq", None),
            P(),
            P(),
            P(),
            P(),
            P(),
            P(),
            P(),
            P(),
            P(),
            P(),
            P(),
            P(),
            P(),
        ),
        out_specs=(
            P("dp", "seq", None),
            P("dp", "seq", None),
            P("dp", None),
            P("dp"),
            P("dp"),
            P("dp", None),
            P("dp"),
            P("dp"),
            P("dp"),
            P("dp", None),
            P("dp"),
            P("dp", None),
            P("dp"),
            P("dp"),
            P("dp"),
        ),
        check_vma=False,
    )
```

```python
import functools

import jax
import jax.numpy as jnp
from jax import lax
from jax.experimental import pallas as pl
from jax.experimental.pallas import tpu as pltpu
from jax.sharding import PartitionSpec as P

H = 12


LAYOUT_REWARD = 2.0
BLOCKED_SCORE = -1000000000.0
NORM_EPS = 1e-05
LOG2E = 1.4426950408889634
HEAD = 64
PAIR = 128
WIDE = 256
BF, F32 = jnp.bfloat16, jnp.float32


def dot(left, right):
    return jnp.dot(left, right, preferred_element_type=F32)


def dot_nt(left, right):
    return lax.dot_general(left, right, (((1,), (1,)), ((), ())), preferred_element_type=F32)


def dot_tn(left, right):
    return lax.dot_general(left, right, (((0,), (0,)), ((), ())), preferred_element_type=F32)


def at(start, size):
    return pl.ds(pl.multiple_of(start, size), size)


def loop(count, body):
    def step(index, carry):
        body(index)
        return carry

    lax.fori_loop(0, count, step, 0)


def fold_rows(block):
    rows, columns = block.shape
    return jnp.sum(block.reshape(rows // 8, 8, columns), axis=0)


def project_tokens(x, w_qkv, bias_row, qkv, rows):
    columns = w_qkv.shape[1]

    def body(index):
        here = at(index * WIDE, WIDE)
        qkv[rows, here] = (dot(x[rows, :], w_qkv[:, here]) + bias_row[0:1, here]).astype(BF)

    loop(columns // WIDE, body)


def fill_reward(reward, seg_row, count):
    text = seg_row.shape[1]
    segs = reward.shape[0] - text
    key = lax.broadcasted_iota(jnp.int32, (segs, text), 0)
    match = jnp.where(key == seg_row, LAYOUT_REWARD * LOG2E, 0.0).astype(F32)
    dead = jnp.where(key >= count, BLOCKED_SCORE * LOG2E, 0.0).astype(F32)
    turned = jnp.transpose(match)
    reward[...] = jnp.zeros_like(reward)
    slots = text + segs
    for head in range(2):
        reward[text:slots, head * slots : head * slots + text] = match + dead
        reward[text:slots, head * slots + text : (head + 1) * slots] = dead[:, :segs]
        reward[0:text, head * slots + text : (head + 1) * slots] = turned


def split_heads(block, both):
    slots = block.shape[0]
    first = lax.broadcasted_iota(jnp.int32, block.shape, 1) < HEAD
    zero = jnp.zeros_like(block)
    both[0:slots, :] = jnp.where(first, block, zero)
    both[slots:, :] = jnp.where(first, zero, block)


def attend(qkv, reward, probs_of, context_t, both, turned, side):
    slots, features = qkv.shape[0], qkv.shape[1] // 3
    pairs = features // PAIR
    scaling = HEAD ** (-0.5) * LOG2E

    def pair_step(pair):
        here = at(pair * PAIR, PAIR)
        keys = qkv[:, at(features + pair * PAIR, PAIR)]
        split_heads(qkv[:, here], both)
        turned[...] = jnp.transpose(qkv[:, at(2 * features + pair * PAIR, PAIR)])
        probs = probs_of(pair)

        for chunk in range(2 * slots // WIDE):
            block = slice(chunk * WIDE, (chunk + 1) * WIDE)
            scores = dot_nt(keys, both[block, :]) * scaling + reward[:, block]
            scores = jnp.exp2(scores - jnp.max(scores, axis=0, keepdims=True))
            probs[:, block] = (scores * (1.0 / jnp.sum(scores, axis=0, keepdims=True))).astype(BF)
        side[...] = dot(turned[...], probs[...]).astype(BF)
        context_t[at(pair * PAIR, HEAD), :] = side[:HEAD, :slots]
        context_t[at(pair * PAIR + HEAD, HEAD), :] = side[HEAD:, slots:]

    return pair_step, pairs


def first_norm(x, attended, bias, gain, shift, normal, root, low, rows):
    def body(index):
        here = at(index * rows, rows)
        hidden = x[here, :].astype(F32) + (attended[here, :] + bias[...])
        centre = hidden - jnp.mean(hidden, axis=1, keepdims=True)
        inverse = lax.rsqrt(jnp.mean(centre * centre, axis=1, keepdims=True) + NORM_EPS)
        unit = centre * inverse
        normal[here, :] = unit
        root[here, :] = jnp.broadcast_to(inverse, (rows, PAIR))
        low[here, :] = (unit * gain[...] + shift[...]).astype(BF)

    loop(x.shape[0] // rows, body)


def gate(inner):
    normal = 0.5 * (1.0 + lax.erf(inner * 0.7071067811865476))
    density = jnp.exp2(inner * inner * (-0.5 * LOG2E)) * 0.3989422804014327
    return inner * normal, normal + inner * density


def feed_forward(low, w_inner, b_inner, hidden, slope):
    def body(index):
        here = at(index * WIDE, WIDE)
        value, grade = gate(dot(low[...], w_inner[:, here]) + b_inner[0:1, here])
        hidden[:, here] = value.astype(BF)
        slope[:, here] = grade.astype(BF)

    loop(w_inner.shape[1] // WIDE, body)


def second_norm(normal, first_gain, first_shift, mlp, bias, gain, shift, cotangent, output, grad, grad_low, sums, rows):
    sums[0:3] = jnp.zeros((3,) + sums.shape[1:], F32)

    def body(index):
        here = at(index * rows, rows)
        one = normal[here, :] * first_gain[...] + first_shift[...]
        total = one + (mlp[here, :] + bias[...])
        centre = total - jnp.mean(total, axis=1, keepdims=True)
        inverse = lax.rsqrt(jnp.mean(centre * centre, axis=1, keepdims=True) + NORM_EPS)
        unit = centre * inverse
        pull = cotangent[here, :].astype(F32)
        output[here, :] = (unit * gain[...] + shift[...]).astype(BF)
        scaled = pull * gain[...]
        back = inverse * (
            scaled
            - jnp.mean(scaled, axis=1, keepdims=True)
            - unit * jnp.mean(scaled * unit, axis=1, keepdims=True)
        )
        rounded = back.astype(BF)
        grad[here, :] = back
        grad_low[here, :] = rounded
        sums[0] += fold_rows(pull * unit)
        sums[1] += fold_rows(pull)
        sums[2] += fold_rows(rounded.astype(F32))

    loop(normal.shape[0] // rows, body)


def first_norm_back(grad_second, back, normal, root, gain, grad_first, grad_low, sums, rows):
    sums[3:6] = jnp.zeros((3,) + sums.shape[1:], F32)

    def body(index):
        here = at(index * rows, rows)
        pull = grad_second[here, :] + back[here, :]
        unit = normal[here, :]
        scaled = pull * gain[...]
        inverse = root[here, 0:1]
        first = inverse * (
            scaled
            - jnp.mean(scaled, axis=1, keepdims=True)
            - unit * jnp.mean(scaled * unit, axis=1, keepdims=True)
        )
        rounded = first.astype(BF)
        grad_first[here, :] = first
        grad_low[here, :] = rounded
        sums[3] += fold_rows(pull * unit)
        sums[4] += fold_rows(pull)
        sums[5] += fold_rows(rounded.astype(F32))

    loop(normal.shape[0] // rows, body)


def attend_back(qkv, grad_context, probs_of, grad_qkv, both, both_grad, turned, scores, side, points):
    slots, features = qkv.shape[0], qkv.shape[1] // 3
    scaling = HEAD ** (-0.5)

    def pair_step(pair):
        here = at(pair * PAIR, PAIR)
        there = at(features + pair * PAIR, PAIR)
        last = at(2 * features + pair * PAIR, PAIR)
        split_heads(qkv[:, here], both)
        split_heads(grad_context[:, here], both_grad)
        turned[...] = jnp.transpose(qkv[:, there])
        values = qkv[:, last]
        probs = probs_of(pair)
        for chunk in range(2 * slots // WIDE):
            block = slice(chunk * WIDE, (chunk + 1) * WIDE)
            pull = dot_nt(values, both_grad[block, :])
            weight = probs[:, block].astype(F32)
            mean = jnp.sum(weight * pull, axis=0, keepdims=True)
            low = (weight * (pull - mean)).astype(BF)
            scores[:, block] = low
            if chunk == 2:
                points("u", pair)
        points("v", pair)
        side[...] = dot(turned[...], scores[...])
        grad_qkv[:, there] = (dot(scores[...], both[...]) * scaling).astype(BF)
        grad_qkv[:, last] = dot(probs[...], both_grad[...]).astype(BF)
        mine = jnp.concatenate([side[:HEAD, :slots], side[HEAD:, slots:]], axis=0)
        grad_qkv[:, here] = jnp.transpose(mine * scaling).astype(BF)

    return pair_step, features // PAIR


PARTS = 16
MESH = pl.DeviceIdType.MESH
UNIT_ROWS = 48
UNITS = 12
WEIGHT = {"c": 1, "y": 2, "l": 4, "h": 8}
ORDERS = (
    "cylhxg",
    "cylxhg",
    "cxylhg",
    "cxylhg",
    "clxhyg",
    "cyxlhg",
    "cyxlhg",
    "clyhxg",
    "cylxhg",
    "cxlhyg",
    "cylxhg",
    "cylxhg",
)
SMALL_ORDER = "cylhx"
SWAP = 0


def partner_of(bit, me, seq):
    if bit in "xg":
        return (me, 1 - seq)
    weight = WEIGHT[bit]
    return (me + weight * (1 - 2 * ((me // weight) % 2)), seq)


def stage_shapes(order, rows, columns):
    bits, shapes = 4, []
    for bit in order:
        if bit == "x":
            columns //= 2
        elif bit != "g":
            bits -= 1
        shapes.append((2,) * bits + (rows, columns))
    return shapes


def add_into(target, other):
    lead = target.shape[:-2]
    total = 1
    for size in lead:
        total *= size

    def step(index, carry):
        place, rest = [], index
        for size in reversed(lead):
            place.append(rest % size)
            rest = rest // size
        place = tuple(reversed(place)) + (slice(None), slice(None))
        target[place] = target[place] + other[place]
        return carry

    if total == 1:
        step(0, 0)
    else:
        lax.fori_loop(0, total, step, 0)


class Unit:
    def __init__(self, number, source, order, buffers, sends, recvs, me, seq):
        self.number, self.source, self.order, self.buffers = number, source, order, buffers
        self.sends, self.recvs, self.me, self.seq = sends, recvs, me, seq

    def at_stage(self, stage):
        bits = ["h", "l", "y", "c"]
        for bit in self.order[:stage]:
            if bit in bits:
                bits.remove(bit)
        current = self.buffers[stage - 1] if stage else self.source
        bit = self.order[stage]
        if bit == "g":
            return current, None
        if bit == "x":
            size = current.shape[-1] // 2
            lead = (slice(None),) * (len(bits) + 1)
            own = current.at[lead + (pl.ds(pl.multiple_of(self.seq * size, PAIR), size),)]
            return current.at[lead + (pl.ds(pl.multiple_of((1 - self.seq) * size, PAIR), size),)], own
        mine = (self.me // WEIGHT[bit]) % 2
        lead = (slice(None),) * bits.index(bit)
        return current.at[lead + (1 - mine,)], current.at[lead + (mine,)]

    def copy(self, stage):
        return pltpu.make_async_remote_copy(
            src_ref=self.at_stage(stage)[0],
            dst_ref=self.buffers[stage],
            send_sem=self.sends.at[self.number, stage],
            recv_sem=self.recvs.at[self.number, stage],
            device_id=partner_of(self.order[stage], self.me, self.seq),
            device_id_type=MESH,
        )

    def advance(self, stage):
        self.copy(stage).wait()
        self.add(stage)

    def add(self, stage):
        kept = self.at_stage(stage)[1]
        if kept is not None:
            add_into(self.buffers[stage], kept)
        if stage + 1 < len(self.order):
            self.copy(stage + 1).start()


def with_stages(schedule):
    reached = [1] * 4 + [0] * (UNITS - 3)
    plan = {}
    for point, numbers in schedule:
        steps = plan.setdefault(point, [])
        for number in numbers:
            steps.append((number, reached[number]))
            reached[number] += 1
    return plan


def layer_kernel(
    tokens, cotangent, seg_align, seg_count,
    query_bias, value_bias, output_bias, first_gain, first_shift, outer_bias, second_gain, second_shift, inner_bias,
    w_qkv, w_out, w_inner, w_outer,
    block_output, tokens_grad, shards, sums_out, probs_hbm,
    vectors, x, qkv, context_t, w_out_v, normal, root, cot, acc, grad_att, sums, own, small, small_got, *rest,
):
    rest = list(rest)
    buffers = [[rest.pop(0) for _ in ORDERS[0][:-1]] for _ in range(UNITS)]
    unit_send, unit_recv, outer_send, outer_recv, local_sem, pair_sem, swap_send, swap_recv, small_send, small_recv, vector_sem, shard_sem, chunk_send, chunk_recv = rest
    slots, features = x.shape
    half = slots // 2
    wide = w_inner.shape[1]
    me, seq = lax.axis_index("dp"), lax.axis_index("seq")
    core = me % 2
    mine, other = at(seq * half, half), at((1 - seq) * half, half)
    b_out, gain1, shift1, b_outer, gain2, shift2 = (vectors.at[i : i + 1] for i in range(3, 9))
    columns = [slice(c * WIDE, (c + 1) * WIDE) for c in range(features // WIDE)]

    barrier = pltpu.get_barrier_semaphore()
    for bit in "xcylh":
        pl.semaphore_signal(barrier, inc=1, device_id=partner_of(bit, me, seq), device_id_type=MESH)

    def local(source, target, index):
        return pltpu.make_async_copy(source, target, local_sem.at[index])

    def swap(source, target, index):
        return pltpu.make_async_remote_copy(
            src_ref=source, dst_ref=target, send_sem=swap_send.at[index], recv_sem=swap_recv.at[index],
            device_id=(me, 1 - seq), device_id_type=MESH)

    keep_tokens = local(tokens.at[seq], x.at[mine], 0)
    keep_cot = local(cotangent.at[seq], cot.at[mine], 1)
    load_out = local(w_out, w_out_v, 2)
    swap_tokens = swap(tokens.at[1 - seq], x.at[mine], 0)
    swap_cot = swap(cotangent.at[1 - seq], cot.at[mine], 1)
    keep_output = local(cot.at[mine], block_output.at[seq], 3)
    swap_output = swap(cot.at[other], block_output.at[seq], 2)
    keep_grad = local(x.at[mine], tokens_grad.at[seq], 4)
    swap_grad = swap(x.at[other], tokens_grad.at[seq], 3)
    keep_tokens.start()
    rows_of = {0: query_bias, 2: value_bias, 3: output_bias, 4: first_gain, 5: first_shift, 6: outer_bias, 7: second_gain, 8: second_shift}
    load_vectors = [pltpu.make_async_copy(ref, vectors.at[i], vector_sem.at[i]) for i, ref in rows_of.items()]
    load_vectors += [
        pltpu.make_async_copy(inner_bias.at[pl.ds(i * features, features)], vectors.at[9 + i], vector_sem.at[9 + i])
        for i in range(wide // features)
    ]
    for copy in load_vectors:
        copy.start()
    vectors[1:2] = jnp.zeros((1, features), F32)

    units = [
        Unit(n, own.at[n if n < 8 else n - 8], ORDERS[n], buffers[n] + [shards.at[n, seq]], unit_send, unit_recv, me, seq)
        for n in range(UNITS)
    ]

    def keep_shard(number):
        return pltpu.make_async_copy(buffers[number][-1], shards.at[number, seq], shard_sem.at[number])

    def outer_copy(j, sub):
        hi, lo = j // 2, j % 2
        return pltpu.make_async_remote_copy(
            src_ref=own.at[sub, hi, lo, :, 1 - core],
            dst_ref=buffers[sub][0].at[hi, lo],
            send_sem=outer_send.at[j, sub], recv_sem=outer_recv.at[j, sub],
            device_id=partner_of("c", me, seq), device_id_type=MESH)

    def chunk_copy(j, sub):
        bit, held = ORDERS[sub][1], buffers[sub][0].at[j // 2, j % 2]
        if bit == "x":
            size = features // 2
            given = held.at[:, :, pl.ds(pl.multiple_of((1 - seq) * size, PAIR), size)]
        else:
            given = held.at[1 - (me // WEIGHT[bit]) % 2]
        return pltpu.make_async_remote_copy(
            src_ref=given,
            dst_ref=buffers[sub][1].at[j // 2, j % 2],
            send_sem=chunk_send.at[j, sub], recv_sem=chunk_recv.at[j, sub],
            device_id=partner_of(bit, me, seq), device_id_type=MESH)

    def take_chunk(j):
        for sub in range(4):
            outer_copy(j, sub).wait()
            add_into(buffers[sub][0].at[j // 2, j % 2], own.at[sub, j // 2, j % 2, :, core])
            chunk_copy(j, sub).start()

    def small_copy(stage):
        return pltpu.make_async_remote_copy(
            src_ref=small, dst_ref=small_got.at[stage], send_sem=small_send.at[stage], recv_sem=small_recv.at[stage],
            device_id=partner_of(SMALL_ORDER[stage], me, seq), device_id_type=MESH)

    def advance(number, stage):
        if number == UNITS:
            small_copy(stage).wait()
            small[...] += small_got[stage]
            if stage + 1 < len(SMALL_ORDER):
                small_copy(stage + 1).start()
        elif number < 4 and stage == 1:
            for j in range(4):
                chunk_copy(j, number).wait()
            units[number].add(1)
        else:
            units[number].advance(stage)
        if number < UNITS and stage == 4:
            keep_shard(number).start()

    plan = with_stages(SCHEDULE)

    def point(name):
        for number, stage in plan.get(name, ()):
            advance(number, stage)

    def points(name, index, count):
        for i in range(count):
            if (name, i) in plan:
                pl.when(index == i)(functools.partial(point, (name, i)))

    def forward(w_inner_v, w_outer_v):
        load_inner, load_outer = local(w_inner, w_inner_v, 5), local(w_outer, w_outer_v, 6)

        def attention(w_qkv_v, reward, both, turned, side, probs_buf):
            load_qkv = local(w_qkv, w_qkv_v, 7)
            load_qkv.start()
            pl.semaphore_wait(barrier, 5)
            swap_tokens.start()
            load_out.start()
            fill_reward(reward, seg_align[pl.ds(seq, 1), :], seg_count[seq])
            keep_tokens.wait()
            for copy in load_vectors:
                copy.wait()
            load_qkv.wait()

            def project(rows):
                def body(index):
                    here = at(index * features, features)
                    bias = vectors[pl.ds(index, 1), :]
                    qkv[rows, here] = (dot(x[rows, :], w_qkv_v[:, here]) + bias).astype(BF)

                loop(3, body)

            project(mine)
            load_inner.start()
            load_outer.start()
            keep_cot.start()
            swap_tokens.wait()
            swap_cot.start()
            project(other)
            step, pairs = attend(qkv, reward, lambda pair: probs_buf.at[pair % 2], context_t, both, turned, side)

            def out_copy(pair):
                return pltpu.make_async_copy(probs_buf.at[pair % 2], probs_hbm.at[pair], pair_sem.at[pair % 2])

            def body(pair):
                @pl.when(pair >= 2)
                def _():
                    out_copy(pair - 2).wait()

                step(pair)
                out_copy(pair).start()

            loop(pairs, body)
            out_copy(pairs - 2).wait()
            out_copy(pairs - 1).wait()

        pl.run_scoped(
            attention,
            pltpu.VMEM((features, 3 * features), BF),
            pltpu.VMEM((slots, 2 * slots), F32),
            pltpu.VMEM((2 * slots, PAIR), BF),
            pltpu.VMEM((PAIR, slots), BF),
            pltpu.VMEM((PAIR, 2 * slots), BF),
            pltpu.VMEM((2, slots, 2 * slots), BF),
        )

        def mlp(low, turned_low, hidden, slope, grad_second):
            low[...] = jnp.transpose(context_t[...])
            load_out.wait()
            for here in columns:
                acc[:, here] = dot(low[...], w_out_v[:, here])
            first_norm(x, acc, b_out, gain1, shift1, normal, root, low, 320)
            load_inner.wait()

            def inner_body(index):
                here = at(index * features, features)
                bias = vectors[pl.ds(9 + index, 1), :]
                value, grade = gate(dot(low[...], w_inner_v[:, here]) + bias)
                hidden[:, here] = value.astype(BF)
                slope[:, here] = grade.astype(BF)

            loop(wide // features, inner_body)
            load_outer.wait()
            for here in columns:
                acc[:, here] = dot(hidden[...], w_outer_v[:, here])
            keep_cot.wait()
            swap_cot.wait()
            second_norm(normal, gain1, shift1, acc, b_outer, gain2, shift2, cot, cot, grad_second, grad_att, sums, 320)
            keep_output.start()


            def outer_step(j):
                block = dot_tn(hidden[:, at(j * features, features)], grad_att[...]).astype(BF)
                block = block.reshape(2, 2, 4, UNIT_ROWS, features)
                for sub in range(4):
                    own[sub, j // 2, j % 2] = block[:, :, sub]
                for sub in range(4):
                    outer_copy(j, sub).start()
                pl.when(j >= 2)(lambda: take_chunk(j - 2))

            loop(4, outer_step)
            take_chunk(2)
            turned_low[...] = jnp.transpose(low[...])
            take_chunk(3)

            def inner_step(j):
                here = at(j * features, features)
                low_grad = (
                    dot_nt(grad_att[...], w_outer_v[here, :]) * slope[:, here].astype(F32)
                ).astype(BF)
                hidden[:, here] = low_grad
                sums[8 + j] = fold_rows(low_grad.astype(F32))
                points("g", j, 4)
                block = dot(turned_low[...], hidden[:, here]).astype(BF)
                own[4 + j] = block.reshape(2, 2, 2, 2, UNIT_ROWS, features)
                for i in range(4):
                    pl.when(j == i)(lambda i=i: units[4 + i].copy(0).start())
                points("i", j, 4)

            loop(4, inner_step)
            swap_output.start()
            for c, here in enumerate(columns):
                acc[:, here] = dot_nt(hidden[...], w_inner_v[here, :])
                point(("a", c))
            first_norm_back(grad_second, acc, normal, root, gain1, acc, grad_att, sums, 320)

        pl.run_scoped(
            mlp,
            pltpu.VMEM((slots, features), BF),
            pltpu.VMEM((features, slots), BF),
            pltpu.VMEM((slots, wide), BF),
            pltpu.VMEM((slots, wide), BF),
            pltpu.VMEM((slots, features), F32),
        )

    pl.run_scoped(forward, pltpu.VMEM(w_inner.shape, BF), pltpu.VMEM(w_outer.shape, BF))

    def back(w_qkv_v, both, both_grad, turned, scores, side, probs_buf, grad_ctx, grad_qkv, turned_x):
        load_qkv = local(w_qkv, w_qkv_v, 8)
        load_qkv.start()

        def in_copy(pair):
            return pltpu.make_async_copy(probs_hbm.at[pair], probs_buf.at[pair % 2], pair_sem.at[pair % 2])

        in_copy(0).start()
        point(("n", 0))
        for c, here in enumerate(columns):
            block = dot(context_t[...], grad_att[:, here]).astype(BF)
            own[0, :, :, :, :, :, here] = block.reshape(2, 2, 2, 2, UNIT_ROWS, WIDE)
        units[8].copy(0).start()
        point(("o", 0))
        for c, here in enumerate(columns):
            grad_ctx[:, here] = dot_nt(grad_att[...], w_out_v[here, :]).astype(BF)
        turned_x[...] = jnp.transpose(x[...])
        point(("o", 1))
        step, pairs = attend_back(
            qkv, grad_ctx, lambda pair: probs_buf.at[pair % 2], grad_qkv, both, both_grad, turned, scores, side,
            lambda name, pair: points(name, pair, pairs))

        def body(pair):
            @pl.when(pair + 1 < pairs)
            def _():
                in_copy(pair + 1).start()

            in_copy(pair).wait()
            step(pair)
            points("r", pair, pairs)

            @pl.when(pair % 2 == 1)
            def _():
                group = pair // 2
                for part in range(3):
                    there = at(part * features + group * WIDE, WIDE)
                    block = dot(turned_x[...], grad_qkv[:, there]).astype(BF)
                    own[1 + group, :, :, :, :, :, part * WIDE : (part + 1) * WIDE] = block.reshape(
                        2, 2, 2, 2, UNIT_ROWS, WIDE)
                for i in range(3):
                    pl.when(group == i)(lambda i=i: units[9 + i].copy(0).start())

            points("s", pair, pairs)

        loop(pairs, body)
        sums[6] = fold_rows(grad_qkv[:, :features].astype(F32))
        sums[7] = fold_rows(grad_qkv[:, 2 * features :].astype(F32))
        small[...] = jnp.sum(sums[...], axis=1)
        small_copy(0).start()
        load_qkv.wait()
        for side_index, rows in enumerate((other, mine)):
            for c, here in enumerate(columns):
                x[rows, here] = (acc[rows, here] + dot_nt(grad_qkv[rows, :], w_qkv_v[here, :])).astype(BF)
                point(("t", side_index * 3 + c))
            (swap_grad if side_index == 0 else keep_grad).start()

    pl.run_scoped(
        back,
        pltpu.VMEM((features, 3 * features), BF),
        pltpu.VMEM((2 * slots, PAIR), BF),
        pltpu.VMEM((2 * slots, PAIR), BF),
        pltpu.VMEM((PAIR, slots), BF),
        pltpu.VMEM((slots, 2 * slots), BF),
        pltpu.VMEM((PAIR, 2 * slots), F32),
        pltpu.VMEM((2, slots, 2 * slots), BF),
        pltpu.VMEM((slots, features), BF),
        pltpu.VMEM((slots, 3 * features), BF),
        pltpu.VMEM((features, slots), BF),
    )
    point(("end", 0))
    keep_output.wait()
    swap_output.wait()
    keep_grad.wait()
    swap_grad.wait()
    for number in range(UNITS):
        keep_shard(number).wait()
    sums_out[...] = small[...]


def finish_kernel(
    block_in, grad_in, shards, sums,
    block_output, tokens_grad, g_qkv, g_query, g_value, g_out, g_out_bias, g_gain1, g_shift1, g_inner, g_inner_bias,
    g_outer, g_outer_bias, g_gain2, g_shift2, passed, sem,
):
    ins, outs = [], []
    for index, (source, target) in enumerate(((block_in, block_output), (grad_in, tokens_grad))):
        for part in range(2):
            buffer, number = passed.at[index, part], 2 * index + part
            ins.append(pltpu.make_async_copy(source.at[part], buffer, sem.at[0, number]))
            outs.append(pltpu.make_async_copy(buffer, target.at[part], sem.at[1, number]))
    for copy in ins:
        copy.start()
    for copy, onward in zip(ins, outs):
        copy.wait()
        onward.start()
    me = lax.axis_index("dp")
    features = sums.shape[1]
    size = features // 2
    for number in range(UNITS):
        for place in range(2):
            value = shards[number, place].astype(F32)
            start = place * size
            if number < 4:
                g_outer[number * UNIT_ROWS : (number + 1) * UNIT_ROWS, start : start + size] = value
            elif number < 8:
                start += (number - 4) * features
                g_inner[:, start : start + size] = value
            elif number == 8:
                g_out[:, start : start + size] = value
            else:
                for piece in range(size // PAIR):
                    column = start + piece * PAIR
                    target = column // WIDE * features + (number - 9) * WIDE + column % WIDE
                    g_qkv[:, target : target + PAIR] = value[:, piece * PAIR : (piece + 1) * PAIR]
    rows = pltpu.roll(sums[0:8], (features - me * UNIT_ROWS) % features, 1)
    for index, out in enumerate((g_gain2, g_shift2, g_outer_bias, g_gain1, g_shift1, g_out_bias, g_query, g_value)):
        out[...] = rows[index, :UNIT_ROWS]
    share = 4 * UNIT_ROWS
    place = me * share
    line = pltpu.roll(sums[pl.ds(8 + place // features, 1)], (features - place % features) % features, 1)
    g_inner_bias[...] = line[0, :share]
    for copy in outs:
        copy.wait()


def finish(block, grad, shards, sums, wide):
    features = block.shape[-1]
    S = jax.ShapeDtypeStruct
    vector = S((UNIT_ROWS,), F32)
    hbm, vmem = pl.BlockSpec(memory_space=pltpu.HBM), pl.BlockSpec(memory_space=pltpu.VMEM)
    return pl.pallas_call(
        finish_kernel,
        name="finish",
        out_shape=[
            S(block.shape, BF), S(grad.shape, BF), S((UNIT_ROWS, 3 * features), F32), vector, vector,
            S((UNIT_ROWS, features), F32), vector, vector, vector, S((UNIT_ROWS, wide), F32), S((4 * UNIT_ROWS,), F32),
            S((4 * UNIT_ROWS, features), F32), vector, vector, vector,
        ],
        in_specs=[hbm, hbm, vmem, vmem],
        out_specs=[hbm, hbm] + [vmem] * 13,
        scratch_shapes=[pltpu.VMEM((2,) + block.shape, BF), pltpu.SemaphoreType.DMA((2, 4))],
        compiler_params=pltpu.CompilerParams(vmem_limit_bytes=60 * 2**20),
    )(block, grad, shards, sums)


def layer(tokens, cotangent, seg_align, seg_count, vectors, w_qkv, w_out, w_inner, w_outer):
    documents, half, features = tokens.shape
    slots, wide = 2 * half, w_inner.shape[1]
    pairs = features // PAIR
    S, V, D = jax.ShapeDtypeStruct, pltpu.VMEM, pltpu.SemaphoreType.DMA
    scratch = [
        V((16, features), F32), V((slots, features), BF), V((slots, 3 * features), BF), V((features, slots), BF), V(w_out.shape, BF),
        V((slots, features), F32), V((slots, PAIR), F32), V((slots, features), BF), V((slots, features), F32),
        V((slots, features), BF), V((16, 8, features), F32), V((8, 2, 2, 2, 2, UNIT_ROWS, features), BF),
        V((16, features), F32), V((len(SMALL_ORDER), 16, features), F32),
    ]
    for number in range(UNITS):
        scratch += [V(shape, BF) for shape in stage_shapes(ORDERS[number], UNIT_ROWS, features)[:-1]]
    scratch += [D((UNITS, 6)), D((UNITS, 6)), D((4, 4)), D((4, 4)), D((9,)), D((2,)), D((4,)), D((4,)), D((5,)), D((5,)), D((16,)), D((UNITS,)), D((4, 4)), D((4, 4))]
    hbm, vmem = pl.BlockSpec(memory_space=pltpu.HBM), pl.BlockSpec(memory_space=pltpu.VMEM)
    return pl.pallas_call(
        layer_kernel,
        name="layer",
        out_shape=[
            S(tokens.shape, BF), S(tokens.shape, BF), S((UNITS, 2, UNIT_ROWS, features // 2), BF), S((16, features), F32),
            S((pairs, slots, 2 * slots), BF),
        ],
        in_specs=[hbm, hbm, vmem, pl.BlockSpec(memory_space=pltpu.SMEM)] + [hbm] * 13,
        out_specs=[hbm, hbm, hbm, vmem, hbm],
        scratch_shapes=scratch,
        compiler_params=pltpu.CompilerParams(collective_id=0, has_side_effects=True, vmem_limit_bytes=60 * 2**20),
    )(tokens, cotangent, seg_align, seg_count, *vectors, w_qkv, w_out, w_inner, w_outer)


SCHEDULE = (
    (("i", 2), (4,)),
    (("i", 3), (5,)),
    (("a", 0), (0, 2, 6, 1, 3)),
    (("a", 1), (7,)),
    (("n", 0), (4,)),
    (("o", 1), (5, 0)),
    (("u", 0), (8,)),
    (("v", 0), (2,)),
    (("r", 0), (1,)),
    (("s", 1), (4,)),
    (("u", 2), (6,)),
    (("v", 2), (7, 5)),
    (("u", 3), (9, 1, 3)),
    (("v", 3), (0, 2)),
    (("s", 3), (6,)),
    (("u", 4), (4, 5)),
    (("r", 4), (1,)),
    (("u", 5), (10, 8, 3)),
    (("v", 5), (2,)),
    (("r", 5), (6, 9)),
    (("s", 5), (7, 0, 4, 5, 1)),
    (("t", 0), (2,)),
    (("t", 3), (8,)),
    (("t", 4), (11, 0, 12)),
    (("t", 5), (4, 3)),
    (("end", 0), (5, 6, 10, 9, 7, 11, 10, 12, 9, 8, 3, 11, 6, 9, 12, 7, 8, 10, 11, 12, 9, 7, 10, 8, 11, 12, 10, 11)),
)


def slot_groups(seg_count, seg_align, all_slots):
    doc_count, text_slots = seg_align.shape
    slot_index = jnp.arange(all_slots, dtype=jnp.int32)
    filler = jnp.zeros((doc_count, all_slots - text_slots), jnp.int32)
    padded = jnp.concatenate([seg_align, filler], axis=1)
    is_text = slot_index < text_slots
    groups = jnp.where(is_text[None, :], padded, (slot_index - text_slots)[None, :])
    present_keys = slot_index[None, :] < text_slots + seg_count[:, None]
    return (groups, is_text, present_keys)


def layer_norm(hidden, gain, shift):
    centre = hidden - jnp.mean(hidden, axis=-1, keepdims=True)
    spread = jnp.mean(centre * centre, axis=-1, keepdims=True)
    return centre * lax.rsqrt(spread + NORM_EPS) * gain + shift


def smooth_gate(inner):
    return jax.nn.gelu(inner, approximate=False)


def softmax_rows(logit_scores):
    return jax.nn.softmax(logit_scores, axis=-1)


def project(tokens, qkv_weight, query_bias, value_bias):
    doc_count, slot_count, features = tokens.shape
    token_rows = tokens.reshape(doc_count * slot_count, features)
    pre = jnp.dot(token_rows, qkv_weight, preferred_element_type=jnp.float32)
    queries = (pre[:, :features] + query_bias).astype(jnp.bfloat16)
    own_keys = (
        pre[:, features : 2 * features]
        .astype(jnp.bfloat16)
        .reshape(doc_count, slot_count, features)
    )
    own_values = (
        (pre[:, 2 * features :] + value_bias)
        .astype(jnp.bfloat16)
        .reshape(doc_count, slot_count, features)
    )
    all_keys, values = (
        lax.all_gather(own_keys, "seq", axis=1, tiled=True),
        lax.all_gather(own_values, "seq", axis=1, tiled=True),
    )
    return (queries, all_keys, values)


def plain(
    tokens,
    seg_count,
    seg_align,
    cotangent,
    qkv_weight,
    query_bias,
    value_bias,
    output_weight,
    output_bias,
    first_gain,
    first_shift,
    inner_weight,
    inner_bias,
    outer_weight,
    outer_bias,
    second_gain,
    second_shift,
):
    doc_count, slot_count, features = tokens.shape
    row_count = doc_count * slot_count
    head_dim = features // H
    scaling = head_dim ** (-0.5)
    all_slots = slot_count * lax.axis_size("seq")
    row_start = lax.axis_index("seq") * slot_count
    groups, is_text, present_keys = slot_groups(seg_count, seg_align, all_slots)
    group_rows = lax.dynamic_slice_in_dim(groups, row_start, slot_count, 1)
    text_rows = lax.dynamic_slice_in_dim(is_text, row_start, slot_count, 0)
    matched_pairs = (group_rows[:, :, None] == groups[:, None, :]) & (
        text_rows[None, :, None] != is_text[None, None, :]
    )
    layout_reward = LAYOUT_REWARD * matched_pairs.astype(jnp.float32)
    queries, all_keys, values = project(tokens, qkv_weight, query_bias, value_bias)
    query_heads = queries.reshape(doc_count, slot_count, H, head_dim)
    key_heads = all_keys.reshape(doc_count, all_slots, H, head_dim)
    value_heads = values.reshape(doc_count, all_slots, H, head_dim)
    unadjusted_scores = (
        jnp.einsum("bqhd,bkhd->bhqk", query_heads, key_heads, preferred_element_type=jnp.float32)
        * scaling
    )
    logit_scores = jnp.where(
        present_keys[:, None, None, :], unadjusted_scores + layout_reward[:, None], BLOCKED_SCORE
    )
    attn_probs, soft_pull = jax.vjp(softmax_rows, logit_scores)
    probs_low = attn_probs.astype(jnp.bfloat16)
    context = jnp.einsum(
        "bhqk,bkhd->bqhd", probs_low, value_heads, preferred_element_type=jnp.float32
    )
    context = context.reshape(row_count, features).astype(jnp.bfloat16)
    token_rows = tokens.reshape(row_count, features)
    attended = jnp.dot(context, output_weight, preferred_element_type=jnp.float32) + output_bias
    normed_one, first_pull = jax.vjp(
        layer_norm, token_rows.astype(jnp.float32) + attended, first_gain, first_shift
    )
    normed_low = normed_one.astype(jnp.bfloat16)
    inner = jnp.dot(normed_low, inner_weight, preferred_element_type=jnp.float32) + inner_bias
    activated, gate_pull = jax.vjp(smooth_gate, inner)
    hidden = activated.astype(jnp.bfloat16)
    mlp_out = jnp.dot(hidden, outer_weight, preferred_element_type=jnp.float32) + outer_bias
    layer_out, second_pull = jax.vjp(layer_norm, normed_one + mlp_out, second_gain, second_shift)
    grad_out = cotangent.reshape(row_count, features).astype(jnp.float32)
    grad_second, second_gain_grad, second_shift_grad = second_pull(grad_out)
    grad_mlp = grad_second.astype(jnp.bfloat16)
    outer_weight_grad = jnp.einsum(
        "rf,rd->fd", hidden, grad_mlp, preferred_element_type=jnp.float32
    )
    outer_bias_grad = jnp.sum(grad_mlp.astype(jnp.float32), axis=0)
    grad_hidden = jnp.einsum(
        "rd,fd->rf", grad_mlp, outer_weight, preferred_element_type=jnp.float32
    )
    grad_inner = gate_pull(grad_hidden)[0].astype(jnp.bfloat16)
    inner_weight_grad = jnp.einsum(
        "rd,rf->df", normed_low, grad_inner, preferred_element_type=jnp.float32
    )
    inner_bias_grad = jnp.sum(grad_inner.astype(jnp.float32), axis=0)
    grad_normed = grad_second + jnp.einsum(
        "rf,df->rd", grad_inner, inner_weight, preferred_element_type=jnp.float32
    )
    grad_first, first_gain_grad, first_shift_grad = first_pull(grad_normed)
    grad_attended = grad_first.astype(jnp.bfloat16)
    output_weight_grad = jnp.einsum(
        "rc,rd->cd", context, grad_attended, preferred_element_type=jnp.float32
    )
    output_bias_grad = jnp.sum(grad_attended.astype(jnp.float32), axis=0)
    grad_context = jnp.einsum(
        "rd,cd->rc", grad_attended, output_weight, preferred_element_type=jnp.float32
    )
    grad_context = grad_context.astype(jnp.bfloat16).reshape(doc_count, slot_count, H, head_dim)
    grad_probs = jnp.einsum(
        "bqhd,bkhd->bhqk", grad_context, value_heads, preferred_element_type=jnp.float32
    )
    grad_scores = soft_pull(grad_probs)[0].astype(jnp.bfloat16)
    grad_queries = (
        jnp.einsum("bhqk,bkhd->bqhd", grad_scores, key_heads, preferred_element_type=jnp.float32)
        * scaling
    )
    grad_queries = grad_queries.astype(jnp.bfloat16).reshape(row_count, features)
    key_term = (
        jnp.einsum("bhqk,bqhd->bkhd", grad_scores, query_heads, preferred_element_type=jnp.float32)
        * scaling
    )
    value_term = jnp.einsum(
        "bhqk,bqhd->bkhd", probs_low, grad_context, preferred_element_type=jnp.float32
    )
    key_sum, value_sum = (
        lax.psum_scatter(
            key_term.reshape(doc_count, all_slots, features).astype(jnp.bfloat16),
            "seq",
            scatter_dimension=1,
            tiled=True,
        ).astype(jnp.float32),
        lax.psum_scatter(
            value_term.reshape(doc_count, all_slots, features).astype(jnp.bfloat16),
            "seq",
            scatter_dimension=1,
            tiled=True,
        ).astype(jnp.float32),
    )
    grad_keys = key_sum.astype(jnp.bfloat16).reshape(row_count, features)
    grad_values = value_sum.astype(jnp.bfloat16).reshape(row_count, features)
    grad_project = jnp.concatenate([grad_queries, grad_keys, grad_values], axis=1)
    qkv_weight_grad = jnp.einsum(
        "rd,re->de", token_rows, grad_project, preferred_element_type=jnp.float32
    )
    query_bias_grad = jnp.sum(grad_queries.astype(jnp.float32), axis=0)
    value_bias_grad = jnp.sum(grad_values.astype(jnp.float32), axis=0)
    tokens_grad = grad_first + jnp.einsum(
        "re,de->rd", grad_project, qkv_weight, preferred_element_type=jnp.float32
    )
    tokens_grad = tokens_grad.astype(jnp.bfloat16).reshape(doc_count, slot_count, features)
    shares = (
        lax.psum_scatter(qkv_weight_grad, "dp", scatter_dimension=0, tiled=True),
        lax.psum_scatter(query_bias_grad, "dp", scatter_dimension=0, tiled=True),
        lax.psum_scatter(value_bias_grad, "dp", scatter_dimension=0, tiled=True),
        lax.psum_scatter(output_weight_grad, "dp", scatter_dimension=0, tiled=True),
        lax.psum_scatter(output_bias_grad, "dp", scatter_dimension=0, tiled=True),
        lax.psum_scatter(first_gain_grad, "dp", scatter_dimension=0, tiled=True),
        lax.psum_scatter(first_shift_grad, "dp", scatter_dimension=0, tiled=True),
        lax.psum_scatter(inner_weight_grad, "dp", scatter_dimension=0, tiled=True),
        lax.psum_scatter(inner_bias_grad, "dp", scatter_dimension=0, tiled=True),
        lax.psum_scatter(outer_weight_grad, "dp", scatter_dimension=0, tiled=True),
        lax.psum_scatter(outer_bias_grad, "dp", scatter_dimension=0, tiled=True),
        lax.psum_scatter(second_gain_grad, "dp", scatter_dimension=0, tiled=True),
        lax.psum_scatter(second_shift_grad, "dp", scatter_dimension=0, tiled=True),
    )
    summed = (
        lax.psum(shares[0].astype(jnp.bfloat16), "seq").astype(jnp.float32),
        lax.psum(shares[1].astype(jnp.bfloat16), "seq").astype(jnp.float32),
        lax.psum(shares[2].astype(jnp.bfloat16), "seq").astype(jnp.float32),
        lax.psum(shares[3].astype(jnp.bfloat16), "seq").astype(jnp.float32),
        lax.psum(shares[4].astype(jnp.bfloat16), "seq").astype(jnp.float32),
        lax.psum(shares[5].astype(jnp.bfloat16), "seq").astype(jnp.float32),
        lax.psum(shares[6].astype(jnp.bfloat16), "seq").astype(jnp.float32),
        lax.psum(shares[7].astype(jnp.bfloat16), "seq").astype(jnp.float32),
        lax.psum(shares[8].astype(jnp.bfloat16), "seq").astype(jnp.float32),
        lax.psum(shares[9].astype(jnp.bfloat16), "seq").astype(jnp.float32),
        lax.psum(shares[10].astype(jnp.bfloat16), "seq").astype(jnp.float32),
        lax.psum(shares[11].astype(jnp.bfloat16), "seq").astype(jnp.float32),
        lax.psum(shares[12].astype(jnp.bfloat16), "seq").astype(jnp.float32),
    )
    block_output = layer_out.astype(jnp.bfloat16).reshape(doc_count, slot_count, features)
    return (
        block_output,
        tokens_grad,
        summed[0],
        summed[1],
        summed[2],
        summed[3],
        summed[4],
        summed[5],
        summed[6],
        summed[7],
        summed[8],
        summed[9],
        summed[10],
        summed[11],
        summed[12],
    )


def local(
    tokens,
    seg_count,
    seg_align,
    cotangent,
    qkv_weight,
    query_bias,
    value_bias,
    output_weight,
    output_bias,
    first_gain,
    first_shift,
    inner_weight,
    inner_bias,
    outer_weight,
    outer_bias,
    second_gain,
    second_shift,
):
    dp, seq = lax.axis_size("dp"), lax.axis_size("seq")
    documents, _, features = tokens.shape
    if dp != PARTS or seq != 2 or documents != 2 or features != PARTS * UNIT_ROWS:
        return plain(
            tokens, seg_count, seg_align, cotangent, qkv_weight, query_bias, value_bias, output_weight, output_bias, first_gain, first_shift, inner_weight, inner_bias, outer_weight, outer_bias, second_gain, second_shift
        )
    vectors = (
        query_bias, value_bias, output_bias, first_gain, first_shift, outer_bias, second_gain, second_shift, inner_bias
    )
    block, grad, shards, sums, _ = layer(
        tokens, cotangent, seg_align, seg_count, vectors, qkv_weight, output_weight, inner_weight, outer_weight
    )
    return tuple(finish(block, grad, shards, sums, inner_weight.shape[1]))


def solution(mesh):
    return jax.shard_map(
        local,
        mesh=mesh,
        in_specs=(
            P("dp", "seq", None),
            P("dp"),
            P("dp", None),
            P("dp", "seq", None),
            P(),
            P(),
            P(),
            P(),
            P(),
            P(),
            P(),
            P(),
            P(),
            P(),
            P(),
            P(),
            P(),
        ),
        out_specs=(
            P("dp", "seq", None),
            P("dp", "seq", None),
            P("dp", None),
            P("dp"),
            P("dp"),
            P("dp", None),
            P("dp"),
            P("dp"),
            P("dp"),
            P("dp", None),
            P("dp"),
            P("dp", None),
            P("dp"),
            P("dp"),
            P("dp"),
        ),
        check_vma=False,
    )
```
